32 devices in a mesh: blk: 2 (over x), seq: 16 (over z, y, core).
Axes of the slice: x: 2, y: 2, z: 4, core: 2. Of those that a mesh axis runs over, the one named last changes fastest.
Arguments:
- byte_ids: int32 [64, 1032], P('seq'), may hold values from 0 to 258
- lengths: int32 [64], P('seq'), may hold values from 1 to 1032, 49536 in all
- lang_ids: int32 [64], P('seq'), may hold values from 0 to 7
- owners: int32 [3], replicated, may hold values from 0 to 15
- table: float32 [259, 768], replicated, may hold values from -6 to 6
- conv_w: float32 [5, 768], replicated, may hold values from -3 to 3
- score_w: float32 [8, 768], replicated, may hold values from -0.4375 to 0.4375
- cotangent: bfloat16 [64, 516, 768], P('seq', None, 'blk'), may hold values from -6 to 6
- table_m: float32 [259, 768], P(None, 'blk'), may hold values from -6 to 6
- table_v: float32 [259, 768], P(None, 'blk'), may hold values from 0.01719 to 0.06876
- convolution_first_moment: float32 [5, 768], P(None, 'blk'), may hold values from -40 to 40
- convolution_second_moment: float32 [5, 768], P(None, 'blk'), may hold values from 4.45824 to 17.83296
- score_m: float32 [8, 768], P(None, 'blk'), may hold values from -6 to 6
- score_v: float32 [8, 768], P(None, 'blk'), may hold values from 0.06192 to 0.24768
Outputs:
- pooled_rows: bfloat16 [64, 516, 768], P('seq', None, 'blk')
- table_m_new: float32 [16, 259, 768], P('seq', None, 'blk')
- table_v_new: float32 [16, 259, 768], P('seq', None, 'blk')
- table_new: float32 [16, 259, 768], P('seq', None, 'blk')
- conv_m_new: float32 [16, 5, 768], P('seq', None, 'blk')
- conv_v_new: float32 [16, 5, 768], P('seq', None, 'blk')
- conv_new: float32 [16, 5, 768], P('seq', None, 'blk')
- score_m_new: float32 [16, 8, 768], P('seq', None, 'blk')
- score_v_new: float32 [16, 8, 768], P('seq', None, 'blk')
- score_new: float32 [16, 8, 768], P('seq', None, 'blk')
The draws below stay inside these ranges and needn't reach their ends.
Inputs may be any that keep to these rules, and one draw needn't show every extreme that they name: `lengths`: the longest sequence has exactly 1032 live positions.
All inputs are finite; a program needn't handle non-finite values. No bound on the sum of `lengths` on one device may be relied on, other than what follows from the above.
Results may differ from the reference program's by a relative error of at most 0.0049.
The reference program's roundings to bfloat16 on the way count: a program that leaves them out, or rounds other values in their place, can miss the bound.
Values may be sent and summed in bfloat16 or wider, within the bound.
No kernel may reach another device: no remote copies, remote signals or barrier semaphores. Data moves between devices by JAX's collectives and lax.ppermute only.
A program may use at most 384 MiB of HBM per device.

```python
import functools
import math
import jax
import jax.numpy as jnp
import numpy as np
from jax import lax

D = 768
V = 259
G = 8
SLOT = 1032
STEP_NUMBER = 5
SEQS = 64
N_SEQ = 16


def with_ends(array, rng, least, largest):
    longest = array.shape.index(max(array.shape))
    spots = []
    for shift in (0, 1):
        where = [jax.random.randint(jax.random.fold_in(rng, axis), (), 0, length) for axis, length in enumerate(array.shape)]
        where[longest] = (where[longest] + shift) % array.shape[longest]
        spots.append(tuple(where))
    return array.at[spots[0]].set(least).at[spots[1]].set(largest)


def steps_of(rng, shape, split, least, top_value):
    level = 1.0
    for position, blocks in split:
        steps = jax.random.uniform(jax.random.fold_in(jax.random.fold_in(rng, 6), position), (blocks,), jnp.float32, least / len(split), top_value / len(split))
        level = level * jnp.repeat(jnp.exp(steps), shape[position] // blocks).reshape((-1,) + (1,) * (len(shape) - 1 - position))
    return level


def rank_table(number_of, skew):
    weights = [(1 << 20) // math.isqrt(standing ** skew) + 1 for standing in range(1, number_of + 1)]
    spread = 1 + sum(weights) // (1 << 30)
    return np.cumsum(np.array([max(1, weight // spread) for weight in weights]))


def ranked(own_key, extent, count, lean):
    grid = rank_table(count, lean)
    pick = jax.random.randint(jax.random.fold_in(own_key, 1), extent, 0, int(grid[count - 1]))
    grade = jnp.searchsorted(jnp.asarray(grid, jnp.int32), pick, side="right")
    return jax.random.permutation(jax.random.fold_in(own_key, 2), count)[grade].astype(jnp.int32)


def profile(amount, total, reach, skew):
    weights = [(1 << 20) // math.isqrt(standing ** skew) + 1 for standing in range(2, amount + 1)]
    spare, given = total - reach - (amount - 1), [1] * (amount - 1)
    while spare > 0:
        candidates = [i for i in range(amount - 1) if given[i] < reach]
        whole, budget = sum([weights[i] for i in candidates]), spare
        for i in candidates:
            addition = min(reach - given[i], max(1, budget * weights[i] // whole), spare)
            given[i] = given[i] + addition
            spare = spare - addition
    return np.array([reach] + given)


def uneven(stream_key, number_of, total, limit, skew):
    if number_of == 2:
        one = jax.random.randint(stream_key, (), max(1, total - limit), min(limit, total - 1) + 1)
        return jnp.stack([one, total - one])
    sizes = jnp.asarray(profile(number_of, total, limit, skew), jnp.int32)
    twos = (number_of - 1) // 2
    giver, sink = sizes[1:1 + 2 * twos:2], sizes[2:2 + 2 * twos:2]
    room = jnp.minimum(giver - 1, limit - sink)
    moved = jax.random.randint(jax.random.fold_in(stream_key, 1), (twos,), 0, 1 << 20) % (room + 1)
    sizes = sizes.at[1:1 + 2 * twos:2].set(giver - moved).at[2:2 + 2 * twos:2].set(sink + moved)
    return sizes[jax.random.permutation(jax.random.fold_in(stream_key, 2), number_of)]


def normal_values(rng, shape, spread, limit, cuts=(), kind=jnp.bfloat16):
    factor_of = steps_of(rng, shape, cuts, -0.22, 0.18) if cuts else 1.0
    values = jax.random.normal(rng, shape, jnp.float32) * spread * factor_of
    return jnp.minimum(jnp.maximum(values, -limit), limit).astype(kind)


def setup_inputs(seed: int = 0) -> dict:
    splits = jax.random.split(jax.random.key(seed), 15)
    return {
        "byte_ids": with_ends(ranked(splits[0], (SEQS, SLOT), V, 2), jax.random.fold_in(splits[0], 3), 0, V - 1).astype(jnp.int32),
        "lengths": uneven(splits[1], SEQS, SEQS * SLOT * 3 // 4, SLOT, 2).astype(jnp.int32),
        "lang_ids": with_ends(jax.random.randint(splits[2], (SEQS,), 0, G), jax.random.fold_in(splits[2], 1), 0, G - 1).astype(jnp.int32),
        "owners": jax.random.randint(splits[3], (3,), 0, N_SEQ).astype(jnp.int32),
        "table": normal_values(splits[4], (V, D), 1.0, 6.0, (), jnp.float32),
        "conv_w": normal_values(splits[5], (5, D), 4 ** -0.5, 3.0, (), jnp.float32),
        "score_w": normal_values(splits[6], (G, D), (D // 4) ** -0.5, 0.4375, (), jnp.float32),
        "cotangent": normal_values(splits[7], (SEQS, SLOT // 2, D), 1.0, 6.0, ((0, 16), (2, 2))),
        "table_m": normal_values(splits[8], (V, D), (0.033 * (SEQS * SLOT * 3 // (4 * V)) ** 0.5), 6.0, ((1, 2),), jnp.float32),
        "table_v": jnp.clip(jnp.exp(math.log(0.06876) - 1.3862944 * jax.random.uniform(splits[9], (V, D), jnp.float32) ** steps_of(splits[9], (V, D), ((1, 2),), -0.2, 0.2)), 0.01719, 0.06876),
        "convolution_first_moment": normal_values(splits[10], (5, D), (0.033 * (SEQS * SLOT * 3 // 4) ** 0.5), 40.0, ((1, 2),), jnp.float32),
        "convolution_second_moment": jnp.clip(jnp.exp(math.log(17.83296) - 1.3862944 * jax.random.uniform(splits[11], (5, D), jnp.float32) ** steps_of(splits[11], (5, D), ((1, 2),), -0.2, 0.2)), 4.45824, 17.83296),
        "score_m": normal_values(splits[12], (G, D), (0.011 * (SEQS * SLOT * 3 // (4 * G)) ** 0.5), 6.0, ((1, 2),), jnp.float32),
        "score_v": jnp.clip(jnp.exp(math.log(0.24768) - 1.3862944 * jax.random.uniform(splits[13], (G, D), jnp.float32) ** steps_of(splits[13], (G, D), ((1, 2),), -0.2, 0.2)), 0.06192, 0.24768),
    }


@jax.custom_vjp
def lower_precision(v):
    return lax.optimization_barrier(v.astype(jnp.bfloat16)).astype(jnp.float32)

@jax.custom_vjp
def low_back(v):
    return v

def low_keep(v):
    return (lower_precision(v), None)

def low_pass(kept, grad):
    return (grad,)

def back_keep(v):
    return (v, None)

def back_low(kept, grad):
    return (lower_precision(grad),)
lower_precision.defvjp(low_keep, low_pass)
low_back.defvjp(back_keep, back_low)

def pool_size(field, live_mask, size_val):
    groups = field.shape[1] // size_val
    totals = lax.optimization_barrier(jnp.sum((field * live_mask[..., None]).reshape(field.shape[0], groups, size_val, field.shape[2]), axis=2))
    tallied_count = lax.optimization_barrier(jnp.sum(live_mask.reshape(live_mask.shape[0], groups, size_val), axis=2))
    means = totals / jnp.maximum(tallied_count, 1.0)[..., None]
    return jnp.repeat(means, size_val, axis=1)

def forward_group(table, conv_w, score_w, inputs):
    ids_group, lens_group, langs_group = inputs
    places = jnp.arange(SLOT, dtype=jnp.int32)
    live_mask = (places[None, :] < lens_group[:, None]).astype(jnp.float32)
    indicator_matrix = (ids_group[..., None] == jnp.arange(V, dtype=jnp.int32)).astype(jnp.float32)
    fetched_rows = jnp.einsum('row,wg->rog', indicator_matrix, lower_precision(table), precision=lax.Precision.HIGHEST)
    embedded = low_back(fetched_rows) * live_mask[..., None]
    convolved = conv_w[4] + jnp.zeros_like(embedded)
    for tap_index in range(4):
        shifted = jnp.pad(embedded, ((0, 0), (tap_index, 0), (0, 0)))[:, :SLOT]
        convolved = convolved + conv_w[tap_index] * shifted
    lang_hot = (langs_group[:, None] == jnp.arange(G, dtype=jnp.int32)).astype(jnp.float32)
    score_vec = jnp.dot(lang_hot, score_w, precision=lax.Precision.HIGHEST)
    pooled = [pool_size(convolved, live_mask, size_val) for size_val in (1, 2, 3, 4)]
    scores = jnp.stack([lax.optimization_barrier(jnp.sum(entry * score_vec[:, None, :], axis=-1)) for entry in pooled])
    soft = jax.nn.softmax(scores, axis=0)
    mixed = soft[0][..., None] * pooled[0]
    for size_index in range(1, 4):
        mixed = mixed + soft[size_index][..., None] * pooled[size_index]
    mixed = mixed * live_mask[..., None]
    return 0.5 * lax.optimization_barrier(jnp.sum(mixed.reshape(mixed.shape[0], SLOT // 2, 2, mixed.shape[2]), axis=2))

def adamw(weight, grad, moment, second, rate):
    new_m = 0.9 * moment + 0.1 * grad
    new_v = 0.999 * second + 0.001 * grad * grad
    m_hat = new_m / (1.0 - 0.9 ** STEP_NUMBER)
    v_hat = new_v / (1.0 - 0.999 ** STEP_NUMBER)
    new_w = weight - rate * (m_hat / (jnp.sqrt(v_hat) + 1e-08) + 0.01 * weight)
    return (new_m, new_v, new_w)

def owned(value, owner):
    hit = (jnp.arange(N_SEQ, dtype=jnp.int32) == owner).astype(jnp.float32)
    return hit[:, None, None] * value[None]

def reference(byte_ids, lengths, lang_ids, owners, table, conv_w, score_w, cotangent, table_m, table_v, convolution_first_moment, convolution_second_moment, score_m, score_v):
    groups = SEQS // 4
    inputs = (byte_ids.reshape(groups, 4, SLOT), lengths.reshape(groups, 4), lang_ids.reshape(groups, 4))

    def forward(table_in, conv_in, score_in):
        step_fn = jax.checkpoint(functools.partial(forward_group, table_in, conv_in, score_in))
        result = lax.map(step_fn, inputs)
        return result.reshape(SEQS, SLOT // 2, table_in.shape[1])
    result, pullback = jax.vjp(forward, table, conv_w, score_w)
    grad_table, grad_conv, grad_score = pullback(cotangent.astype(jnp.float32))
    output_values = [result.astype(jnp.bfloat16)]
    for weight, grad, moment, second, rate, owner in ((table, grad_table, table_m, table_v, 0.5, owners[0]), (conv_w, grad_conv, convolution_first_moment, convolution_second_moment, 0.3, owners[1]), (score_w, grad_score, score_m, score_v, 0.05, owners[2])):
        new_m, new_v, new_w = adamw(weight, grad, moment, second, rate)
        output_values = output_values + [owned(new_m, owner), owned(new_v, owner), owned(new_w, owner)]
    return (output_values[0], output_values[1], output_values[2], output_values[3], output_values[4], output_values[5], output_values[6], output_values[7], output_values[8], output_values[9])
```

```python
import functools

import jax
import jax.numpy as jnp
from jax import lax
from jax.experimental import pallas as pl
from jax.experimental.pallas import tpu as pltpu
from jax.sharding import PartitionSpec as P

STEP_NUMBER = 5
F32, BF16 = jnp.float32, jnp.bfloat16
TJ = 96
NO_ID = 511.0
VP = 272
NN = (((1,), (0,)), ((), ()))
NT = (((1,), (1,)), ((), ()))
TN = (((0,), (0,)), ((), ()))


def dot(a, b, dims=NN):
    return lax.dot_general(a, b, dims, preferred_element_type=F32)


def iota(shape, dim):
    return lax.broadcasted_iota(jnp.int32, shape, dim)


def split2(x):
    high = x.astype(BF16)
    return high, (x - high.astype(F32)).astype(BF16)


def split3(x):
    high = x.astype(BF16)
    rest = x - high.astype(F32)
    mid = rest.astype(BF16)
    return high, mid, (rest - mid.astype(F32)).astype(BF16)


def block_masks():
    ju, jt = iota((TJ, TJ), 0), iota((TJ, TJ), 1)
    one = lambda cond: jnp.where(cond, 1.0, 0.0).astype(F32)
    third = lambda j, par: (2 * j + par) // 3
    return [
        one(ju == jt),
        one(ju // 2 == jt // 2),
        one(third(ju, 0) == third(jt, 0)),
        one(third(ju, 0) == third(jt, 1)),
        one(third(ju, 1) == third(jt, 0)),
        one(third(ju, 1) == third(jt, 1)),
    ]


def pick_row(x, index):
    return jnp.sum(jnp.where(iota(x.shape, 0) == index, x, 0.0), axis=0, keepdims=True)


def store_masks(mask_ref, wide):
    for k, mask in enumerate(block_masks()):
        if wide:
            mask_ref[k] = jnp.zeros(mask_ref.shape[1:], F32)
        mask_ref[k, :, :TJ] = mask


def load_table(table_ref, tail_ref, tab_ref):
    vocab = table_ref.shape[0]
    whole = vocab // 128 * 128
    tab_ref[:whole, :] = table_ref[:whole, :].astype(BF16)
    tail_ref[...] = jnp.zeros(tail_ref.shape, F32)
    tail_ref[: vocab - whole, :] = table_ref[whole:, :]
    tab_ref[whole:, :] = tail_ref[...].astype(BF16)


def load_cot_rows(cot_ref, first, rows):
    have = cot_ref.shape[1]
    if first + rows <= have:
        return cot_ref[0, first : first + rows, :]
    whole = (have - first) // 16 * 16
    parts = [cot_ref[0, first : first + whole, :]]
    left = have - first - whole
    if left:
        last = cot_ref[0, first + whole :, :].astype(F32)
        pad = jnp.zeros((16 - left, last.shape[1]), F32)
        parts.append(jnp.concatenate([last, pad], axis=0).astype(BF16))
        whole += 16
    if rows > whole:
        parts.append(jnp.zeros((rows - whole, cot_ref.shape[2]), BF16))
    return jnp.concatenate(parts, axis=0)


def forward_kernel(
    half_ref, len_ref, ids_ref, cot_ref, table_ref, conv_ref,
    emb_out, conv_out, inner_out, rows_out,
    xs, cs, idc, tail, tab, emb, masks,
):
    s = pl.program_id(0)
    seqs, slot = ids_ref.shape
    chans = cot_ref.shape[2]
    tiles = emb_out.shape[2] // TJ
    pairs = tiles * TJ

    @pl.when(s == 0)
    def _():
        xs[...] = jnp.full(xs.shape, NO_ID, F32)
        xs[:seqs, :slot] = ids_ref[...].astype(F32)
        for i in range(xs.shape[1] // 128):
            cs[128 * i : 128 * (i + 1), :] = xs[:, 128 * i : 128 * (i + 1)].T
        rows_out[...] = jnp.full(rows_out.shape, NO_ID, F32)
        for par in range(2):
            cols = cs[pl.ds(par, pairs, stride=2), :]
            for k in range(seqs):
                idc[k, par] = jnp.broadcast_to(cols[:, k : k + 1], (pairs, 128))
            for i in range(tiles):
                flipped = cols[TJ * i : TJ * (i + 1), :].T
                for k in range(seqs):
                    rows_out[k, par : par + 1, 128 * i : 128 * i + TJ] = flipped[k : k + 1, :]
        load_table(table_ref, tail, tab)
        emb[:, :8, :] = jnp.zeros((2, 8, chans), F32)
        store_masks(masks, False)

    inner_out[...] = jnp.zeros(inner_out.shape, F32)
    lane = iota((2 * TJ, 128), 1).astype(F32)
    length = len_ref[s]
    taps = [conv_ref[k : k + 1, :] for k in range(5)]
    for i in range(tiles):
        r = TJ * i
        ids = jnp.concatenate([idc[s, 0, r : r + TJ, :], idc[s, 1, r : r + TJ, :]], axis=0)
        hot = jnp.concatenate(
            [jnp.where(ids == lane + 128.0 * k, 1.0, 0.0).astype(BF16) for k in range(3)], axis=1
        )
        rows = dot(hot, tab[...])
        for par in range(2):
            emb[par, 8 + r : 8 + r + TJ, :] = rows[par * TJ : (par + 1) * TJ]
            emb_out[0, par, r : r + TJ, :] = rows[par * TJ : (par + 1) * TJ].astype(BF16)
        even, odd = rows[:TJ], rows[TJ:]
        even1 = emb[0, 7 + r : 7 + r + TJ, :]
        odd1 = emb[1, 7 + r : 7 + r + TJ, :]
        odd2 = emb[1, 6 + r : 6 + r + TJ, :]
        conv_even = taps[4] + taps[0] * even + taps[1] * odd1 + taps[2] * even1 + taps[3] * odd2
        conv_odd = taps[4] + taps[0] * odd + taps[1] * even + taps[2] * odd1 + taps[3] * even1
        high, low = split2(jnp.concatenate([conv_even, conv_odd], axis=0))
        conv_out[0, i] = high
        cot = load_cot_rows(cot_ref, r, TJ)
        prod = dot(high, cot, NT) + dot(low, cot, NT)
        place = 2 * (r + iota((TJ, TJ), 0))
        pe = jnp.where(place < length, prod[:TJ], 0.0)
        po = jnp.where(place + 1 < length, prod[TJ:], 0.0)
        total = lambda x: jnp.sum(x, axis=0, keepdims=True)
        sums = [
            total(masks[0] * pe),
            total(masks[0] * po),
            total(masks[1] * (pe + po)),
            total(masks[2] * pe + masks[4] * po),
            total(masks[3] * pe + masks[5] * po),
        ]
        for k, row in enumerate(sums):
            inner_out[0, k : k + 1, 128 * i : 128 * i + TJ] = row


def lane_facts(width):
    lane = iota((8, width), 1)
    within = lane % 128
    pair = TJ * (lane // 128) + within
    return within, pair


def shift_right(x, n):
    width = x.shape[1]
    within, pair = lane_facts(width)
    inside = pltpu.roll(x, n, 1)
    across = pltpu.roll(x, n + 128 - TJ, 1)
    return jnp.where(pair < n, 0.0, jnp.where(within < n, across, inside))


def shift_left(x, n):
    width = x.shape[1]
    within, pair = lane_facts(width)
    inside = pltpu.roll(x, width - n, 1)
    across = pltpu.roll(x, width - n - (128 - TJ), 1)
    last = TJ * (width // 128)
    return jnp.where(pair >= last - n, 0.0, jnp.where(within >= TJ - n, across, inside))


def block_sums(even, odd):
    width = even.shape[1]
    _, pair = lane_facts(width)
    after = lambda x: pltpu.roll(x, width - 1, 1)
    before = lambda x: pltpu.roll(x, 1, 1)
    two = even + odd
    four = two + jnp.where(pair % 2 == 0, after(two), before(two))
    third = pair % 3
    en, on, ep, op = after(even), after(odd), before(even), before(odd)
    first, last = two + en, op + two
    three_even = jnp.where(third == 0, first, jnp.where(third == 1, ep + op + even, last))
    three_odd = jnp.where(third == 0, first, jnp.where(third == 1, odd + en + on, last))
    return [even, two, three_even, four], [odd, two, three_odd, four]


def live_rows(len_ref, seqs, width):
    within, pair = lane_facts(width)
    sub = iota((8, width), 0)
    length = jnp.zeros((8, width), jnp.int32)
    for s in range(seqs):
        length = jnp.where(sub == s, len_ref[s], length)
    length = jnp.where(within < TJ, length, 0)
    return [jnp.where(2 * pair + par < length, 1.0, 0.0).astype(F32) for par in range(2)]


def inverse_counts(live):
    return [[1.0 / jnp.maximum(c, 1.0) for c in side] for side in block_sums(*live)]


def band(mask_ref, rows, seq, tile_start, length):
    r = [rows[k : k + 1, :] for k in range(5)]
    four = mask_ref[1] * r[4]
    even = mask_ref[0] * r[0] + mask_ref[2] * r[2] + mask_ref[3] * r[3] + four
    odd = mask_ref[0] * r[1] + mask_ref[4] * r[2] + mask_ref[5] * r[3] + four
    place = 2 * (tile_start + iota((TJ, 128), 0))
    even = jnp.where(place < length, even, 0.0)
    odd = jnp.where(place + 1 < length, odd, 0.0)
    return jnp.concatenate([even, odd], axis=0)


def pooled_kernel(
    len_ref, lang_ref, rows_ref, table_ref, convw_ref, score_ref, conv_ref,
    out_ref, prob_out, band_out,
    tail, tab, lookups, bias, masks,
):
    s = pl.program_id(0)
    seqs = len_ref.shape[0]
    width = rows_ref.shape[2]
    tiles = width // 128

    @pl.when(s == 0)
    def _():
        load_table(table_ref, tail, tab)
        store_masks(masks, True)
        scores = score_ref[...]
        mixed = jnp.concatenate([convw_ref[k : k + 1, :] * scores for k in range(4)], axis=0)
        small = dot(jnp.concatenate(split3(mixed), axis=0), tab[...], NT)
        small = small[:32] + small[32:64] + small[64:96]
        small = jnp.concatenate(split3(small), axis=0)
        constant = jnp.sum(convw_ref[4:5, :] * scores, axis=1, keepdims=True)
        constant = jnp.broadcast_to(constant, (8, width))
        for k in range(seqs):
            bias[k : k + 1, :] = pick_row(constant, lang_ref[k])
        bias[seqs:, :] = jnp.zeros((8 - seqs, width), F32)
        lookups[...] = jnp.zeros(lookups.shape, F32)
        for par in range(2):
            for k in range(seqs):
                sub = iota((VP, width), 0).astype(F32)
                hot = jnp.where(rows_ref[k, par : par + 1, :] == sub, 1.0, 0.0).astype(BF16)
                hot = jnp.concatenate([hot, jnp.zeros((384 - VP, width), BF16)], axis=0)
                got = dot(small, hot)
                got = got[:32] + got[32:64] + got[64:96]
                for tap in range(4):
                    lookups[par, tap, k : k + 1, :] = pick_row(got[8 * tap : 8 * tap + 8], lang_ref[k])
        look = lambda par, tap: lookups[par, tap]
        shift = shift_right
        even = bias[...] + look(0, 0) + shift(look(1, 1), 1) + shift(look(0, 2), 1) + shift(look(1, 3), 2)
        odd = bias[...] + look(1, 0) + look(0, 1) + shift(look(1, 2), 1) + shift(look(0, 3), 1)
        live = live_rows(len_ref, seqs, width)
        inverse = inverse_counts(live)
        totals = block_sums(jnp.where(live[0] > 0, even, 0.0), jnp.where(live[1] > 0, odd, 0.0))
        weights = []
        for par in range(2):
            score = [t * c for t, c in zip(totals[par], inverse[par])]
            top = functools.reduce(jnp.maximum, score)
            grown = [jnp.exp(x - top) for x in score]
            scale = 1.0 / functools.reduce(jnp.add, grown)
            prob = [x * scale for x in grown]
            for size in range(4):
                prob_out[par, size] = prob[size]
            weights.append([0.5 * live[par] * p * c for p, c in zip(prob, inverse[par])])
        (e1, e2, e3, e4), (o1, o2, o3, o4) = weights
        for k, row in enumerate([e1 + e2 + o2, o1 + e2 + o2, e3, o3, e4 + o4]):
            for q in range(seqs):
                band_out[q, k : k + 1, :] = row[q : q + 1, :]

    length = len_ref[s]
    have = out_ref.shape[1]
    for i in range(tiles):
        weights = band(masks, band_out[s, :, 128 * i : 128 * (i + 1)], s, TJ * i, length)
        got = dot(weights.astype(BF16), conv_ref[0, i], TN)
        rows = min(TJ, have - TJ * i)
        out_ref[0, TJ * i : TJ * i + rows, :] = got[:rows].astype(BF16)


def backward_kernel(
    half_ref, len_ref, lang_ref, core_ref, rows_ref, cot_ref, table_ref, convw_ref, score_ref,
    emb_ref, prob_ref, band_ref, inner_ref, other_ref,
    keep_out, send_out,
    tail, tab, masks, pulls, shifted, sums, emb, grad, gemb, hots, hist, acc, taps_acc, flat,
):
    s = pl.program_id(0)
    seqs = len_ref.shape[0]
    width = rows_ref.shape[2]
    tiles = width // 128
    pairs = tiles * TJ
    chans = cot_ref.shape[2]

    @pl.when(s == 0)
    def _():
        load_table(table_ref, tail, tab)
        store_masks(masks, True)
        pulls[...] = jnp.zeros(pulls.shape, F32)
        for q in range(seqs):
            both = inner_ref[q] + other_ref[q]
            for k in range(5):
                pulls[k, q : q + 1, :] = both[k : k + 1, :]
        live = live_rows(len_ref, seqs, width)
        inverse = inverse_counts(live)
        one_e, one_o, four, three_e, three_o = [pulls[k] for k in range(5)]
        two = one_e + one_o
        dots = [[one_e, two, three_e, four], [one_o, two, three_o, four]]
        parts = [[], []]
        for par in range(2):
            inner = [
                0.5 * jnp.where(live[par] > 0, d, 0.0) * c for d, c in zip(dots[par], inverse[par])
            ]
            prob = [prob_ref[par, size] for size in range(4)]
            mean = functools.reduce(jnp.add, [p * x for p, x in zip(prob, inner)])
            parts[par] = [p * (x - mean) * c for p, x, c in zip(prob, inner, inverse[par])]
        pull = [0.0, 0.0]
        for size in range(4):
            totals = block_sums(parts[0][size], parts[1][size])
            pull = [pull[par] + totals[par][size] for par in range(2)]
        pe, po = [live[par] * pull[par] for par in range(2)]
        sums[...] = jnp.broadcast_to(jnp.sum(pe + po, axis=1, keepdims=True), sums.shape)
        ahead = [
            [pe, po, shift_left(pe, 1), shift_left(po, 1)],
            [po, shift_left(pe, 1), shift_left(po, 1), shift_left(pe, 2)],
        ]
        for par in range(2):
            for k in range(4):
                high = ahead[par][k].astype(BF16).astype(F32)
                low = ahead[par][k] - high
                for q in range(seqs):
                    shifted[q, par, k : k + 1, :] = high[q : q + 1, :]
                    shifted[q, par, 4 + k : 5 + k, :] = low[q : q + 1, :]
        emb[:, :8, :] = jnp.zeros((2, 8, chans), F32)
        grad[:, pairs:, :] = jnp.zeros((2, 8, chans), F32)
        acc[...] = jnp.zeros(acc.shape, F32)
        taps_acc[...] = jnp.zeros(taps_acc.shape, F32)

    length = len_ref[s]
    lang = lang_ref[s]
    score = pick_row(score_ref[...], lang)
    high = score.astype(BF16).astype(F32)
    sub = iota((128 - TJ, chans), 0)
    gap = jnp.where(sub == 0, high, jnp.where(sub == 1, score - high, 0.0)).astype(BF16)
    lane = iota((TJ, 128), 1)
    extra = (lane == TJ) | (lane == TJ + 1)
    blank = jnp.zeros((120, 128), F32)
    for i in range(tiles):
        r = TJ * i
        cot = jnp.concatenate([load_cot_rows(cot_ref, r, TJ), gap], axis=0)
        lanes = slice(128 * i, 128 * (i + 1))
        weights = band(masks, band_ref[s, :, lanes], s, r, length)
        columns = []
        for par in range(2):
            both = jnp.concatenate([shifted[s, par, :, lanes], blank], axis=0).T
            gemb[256 * i + 128 * par : 256 * i + 128 * (par + 1), chans:] = both.astype(BF16)
            columns.append(jnp.where(extra, both[:TJ, 0:1] + both[:TJ, 4:5], weights[par * TJ : (par + 1) * TJ]))
        wide = jnp.concatenate(split2(jnp.concatenate(columns, axis=0)), axis=1)
        got = dot(wide, jnp.concatenate([cot, cot], axis=0))
        for par in range(2):
            grad[par, r : r + TJ, :] = got[par * TJ : (par + 1) * TJ]
            emb[par, 8 + r : 8 + r + TJ, :] = emb_ref[0, par, r : r + TJ, :].astype(F32)
            sub = iota((VP, 128), 0).astype(F32)
            hots[:, 256 * i + 128 * par : 256 * i + 128 * (par + 1)] = jnp.where(
                rows_ref[s, par : par + 1, lanes] == sub, 1.0, 0.0
            ).astype(BF16)
    taps = [convw_ref[k : k + 1, :] for k in range(4)]
    fold = lambda x: jnp.sum(x.reshape(TJ // 8, 8, chans), axis=0)
    for i in range(tiles):
        r = TJ * i
        ge, go = grad[0, r : r + TJ, :], grad[1, r : r + TJ, :]
        ge1, go1 = grad[0, r + 1 : r + 1 + TJ, :], grad[1, r + 1 : r + 1 + TJ, :]
        ge2 = grad[0, r + 2 : r + 2 + TJ, :]
        ee, eo = emb[0, 8 + r : 8 + r + TJ, :], emb[1, 8 + r : 8 + r + TJ, :]
        ee1, eo1 = emb[0, 7 + r : 7 + r + TJ, :], emb[1, 7 + r : 7 + r + TJ, :]
        eo2 = emb[1, 6 + r : 6 + r + TJ, :]
        back_e = taps[0] * ge + taps[1] * go + taps[2] * ge1 + taps[3] * go1
        back_o = taps[0] * go + taps[1] * ge1 + taps[2] * go1 + taps[3] * ge2
        zeros = jnp.zeros((128 - TJ, chans), BF16)
        gemb[256 * i : 256 * (i + 1), :chans] = jnp.concatenate(
            [back_e.astype(BF16), zeros, back_o.astype(BF16), zeros], axis=0
        )
        for k, part in enumerate(
            [ge * ee + go * eo, ge * eo1 + go * ee, ge * ee1 + go * eo1, ge * eo2 + go * ee1, ge + go]
        ):
            taps_acc[k] += fold(part)
    got = dot(hots[...], gemb[...])
    acc[...] += got[:, :chans]
    hist[...] = jnp.zeros(hist.shape, F32)
    hist[:VP, :] = got[:, chans:]
    counts = hist[...].T[:8]
    counts = jnp.concatenate(split3(jnp.concatenate([counts[:4] + counts[4:], jnp.zeros((12, 384), F32)], axis=0)), axis=0)
    from_table = dot(counts, tab[...])
    from_table = from_table[:16] + from_table[16:32] + from_table[32:]
    part = convw_ref[4:5, :] * pick_row(sums[:, :chans], s)
    for k in range(4):
        part = part + taps[k] * from_table[k : k + 1, :]
    groups = score_ref.shape[0]
    acc[VP - groups : VP, :] += jnp.where(iota((groups, chans), 0) == lang, part, 0.0)

    @pl.when(s == seqs - 1)
    def _():
        for k in range(5):
            row = VP - groups - 5 + k
            acc[row : row + 1, :] = jnp.sum(taps_acc[k], axis=0, keepdims=True)
        flat[...] = jnp.zeros(flat.shape, F32)
        for k in range(chans // 128):
            flat[VP * k : VP * (k + 1), :] = acc[:, 128 * k : 128 * (k + 1)]
        rows = keep_out.shape[0]
        mine = pl.multiple_of(core_ref[0] * rows, 8)
        theirs = pl.multiple_of((1 - core_ref[0]) * rows, 8)
        keep_out[...] = flat[pl.ds(mine, rows), :]
        send_out[...] = flat[pl.ds(theirs, rows), :]


def adamw(weight, grad, moment, second, rate):
    new_m = 0.9 * moment + 0.1 * grad
    new_v = 0.999 * second + 0.001 * grad * grad
    m_hat = new_m / (1.0 - 0.9**STEP_NUMBER)
    v_hat = new_v / (1.0 - 0.999**STEP_NUMBER)
    new_w = weight - rate * (m_hat / (jnp.sqrt(v_hat) + 1e-08) + 0.01 * weight)
    return new_m, new_v, new_w


def update_kernel(half_ref, place_ref, owner_ref, mine_ref, other_ref, *refs):
    ins, outs, flat = refs[:9], refs[9:18], refs[18]
    core, near, seq = place_ref[0], place_ref[1], place_ref[2]
    rows = mine_ref.shape[0] // 2
    for side, ref in ((core, mine_ref), (1 - core, other_ref)):
        for k in range(2):
            piece = near if k == 0 else 1 - near
            flat[pl.ds(pl.multiple_of((2 * side + piece) * rows, 8), rows), :] = ref[k * rows : (k + 1) * rows, :]
    vocab = ins[0].shape[0]
    chans = ins[0].shape[1]
    groups = ins[6].shape[0]
    spans = ((0, vocab), (VP - groups - 5, 5), (VP - groups, groups))
    for t, rate in enumerate((0.5, 0.3, 0.05)):
        first, count = spans[t]
        owned = owner_ref[t] == seq
        for k in range(chans // 128):
            lanes = slice(128 * k, 128 * (k + 1))
            grad = flat[VP * k + first : VP * k + first + count, :]
            new = adamw(ins[3 * t][:, lanes], grad, ins[3 * t + 1][:, lanes], ins[3 * t + 2][:, lanes], rate)
            for q in range(3):
                outs[3 * t + q][0, :, lanes] = jnp.where(owned, new[q], 0.0)


def local(
    seq_size, byte_ids, lengths, lang_ids, owners, table, conv_w, score_w, cotangent,
    table_m, table_v, conv_m, conv_v, score_m, score_v,
):
    seqs, slot = byte_ids.shape
    vocab, full = table.shape
    half_rows, chans = cotangent.shape[1:]
    groups = score_w.shape[0]
    tiles = -(-half_rows // TJ)
    pairs, width = tiles * TJ, tiles * 128
    half = lax.axis_index("blk").astype(jnp.int32).reshape(1)
    seq = lax.axis_index("seq").astype(jnp.int32)
    core, near = seq % 2, (seq // 4) % 2
    vmem = pltpu.VMEM
    params = lambda mib: pltpu.CompilerParams(vmem_limit_bytes=mib * 1024 * 1024, dimension_semantics=("arbitrary",))
    shape = jax.ShapeDtypeStruct
    whole = lambda *dims: pl.BlockSpec(dims, lambda s, *_: (0,) * len(dims))
    by_seq = lambda *dims: pl.BlockSpec((1,) + dims, lambda s, *_: (s,) + (0,) * len(dims))
    by_half = lambda rows: pl.BlockSpec((rows, chans), lambda s, half, *_: (0, half[0]))

    emb, conv, inner, rows = pl.pallas_call(
        forward_kernel,
        grid_spec=pltpu.PrefetchScalarGridSpec(
            num_scalar_prefetch=2,
            grid=(seqs,),
            in_specs=[whole(seqs, slot), by_seq(half_rows, chans), by_half(vocab), by_half(5)],
            out_specs=[
                by_seq(2, pairs, chans), by_seq(tiles, 2 * TJ, chans), by_seq(8, width), whole(seqs, 8, width)
            ],
            scratch_shapes=[
                vmem((8, 2 * pairs), F32), vmem((2 * pairs, 8), F32), vmem((seqs, 2, pairs, 128), F32),
                vmem((128, chans), F32), vmem((384, chans), BF16), vmem((2, 8 + pairs, chans), F32),
                vmem((6, TJ, TJ), F32),
            ],
        ),
        out_shape=[
            shape((seqs, 2, pairs, chans), BF16), shape((seqs, tiles, 2 * TJ, chans), BF16),
            shape((seqs, 8, width), F32), shape((seqs, 8, width), F32),
        ],
        compiler_params=params(32),
        name="forward",
    )(half, lengths, byte_ids, cotangent, table, conv_w)

    other = lax.ppermute(inner, "blk", [(0, 1), (1, 0)])

    pooled, prob, weights = pl.pallas_call(
        pooled_kernel,
        grid_spec=pltpu.PrefetchScalarGridSpec(
            num_scalar_prefetch=2,
            grid=(seqs,),
            in_specs=[
                whole(seqs, 8, width), whole(vocab, full), whole(5, full), whole(groups, full),
                by_seq(tiles, 2 * TJ, chans),
            ],
            out_specs=[by_seq(half_rows, chans), whole(2, 4, 8, width), whole(seqs, 8, width)],
            scratch_shapes=[
                vmem((128, full), F32), vmem((384, full), BF16),
                vmem((2, 4, 8, width), F32), vmem((8, width), F32), vmem((6, TJ, 128), F32),
            ],
        ),
        out_shape=[
            shape((seqs, half_rows, chans), BF16), shape((2, 4, 8, width), F32), shape((seqs, 8, width), F32)
        ],
        compiler_params=params(32),
        name="pooled",
    )(lengths, lang_ids, rows, table, conv_w, score_w, conv)

    total = -(-VP * (chans // 128) // 32) * 32
    keep, send = pl.pallas_call(
        backward_kernel,
        grid_spec=pltpu.PrefetchScalarGridSpec(
            num_scalar_prefetch=4,
            grid=(seqs,),
            in_specs=[
                whole(seqs, 8, width), by_seq(half_rows, chans), by_half(vocab), by_half(5), by_half(groups),
                by_seq(2, pairs, chans), whole(2, 4, 8, width), whole(seqs, 8, width),
                whole(seqs, 8, width), whole(seqs, 8, width),
            ],
            out_specs=[whole(total // 2, 128), whole(total // 2, 128)],
            scratch_shapes=[
                vmem((128, chans), F32), vmem((384, chans), BF16), vmem((6, TJ, 128), F32),
                vmem((5, 8, width), F32), vmem((seqs, 2, 8, width), F32), vmem((8, width), F32),
                vmem((2, 8 + pairs, chans), F32), vmem((2, pairs + 8, chans), F32),
                vmem((2 * width, chans + 128), BF16), vmem((VP, 2 * width), BF16), vmem((384, 128), F32),
                vmem((VP, chans), F32), vmem((5, 8, chans), F32), vmem((total, 128), F32),
            ],
        ),
        out_shape=[shape((total // 2, 128), F32)] * 2,
        compiler_params=params(40),
        name="backward",
    )(half, lengths, lang_ids, core.reshape(1), rows, cotangent, table, conv_w, score_w, emb, prob, weights, inner, other)

    def swap(x, step):
        return lax.ppermute(x, "seq", [(i, i ^ step) for i in range(seq_size)])

    mine = keep + swap(send, 1)
    quarter = total // 4
    held = lax.dynamic_slice_in_dim(mine, near * quarter, quarter, 0)
    sent = lax.dynamic_slice_in_dim(mine, (1 - near) * quarter, quarter, 0)
    held = held + swap(sent, 4)
    step = 2
    while step < seq_size:
        if step != 4:
            held = held + swap(held, step)
        step *= 2
    mine = jnp.concatenate([held, swap(held, 4)], axis=0)
    other = swap(mine, 1)

    place = jnp.stack([core, near, seq])
    triples = ((table, table_m, table_v), (conv_w, conv_m, conv_v), (score_w, score_m, score_v))
    counts = (vocab, 5, groups)
    in_specs = [whole(total // 2, 128), whole(total // 2, 128)]
    out_specs, out_shape = [], []
    for count in counts:
        in_specs += [by_half(count), whole(count, chans), whole(count, chans)]
        out_specs += [by_seq(count, chans)] * 3
        out_shape += [shape((1, count, chans), F32)] * 3
    updated = pl.pallas_call(
        update_kernel,
        grid_spec=pltpu.PrefetchScalarGridSpec(
            num_scalar_prefetch=3,
            grid=(1,),
            in_specs=in_specs,
            out_specs=out_specs,
            scratch_shapes=[vmem((total, 128), F32)],
        ),
        out_shape=out_shape,
        compiler_params=params(24),
        name="update",
    )(half, place, owners, mine, other, *[x for triple in triples for x in triple])
    return (pooled, *updated)


def solution(mesh):
    row, split, copied = P("seq"), P(None, "blk"), P()
    return jax.shard_map(
        functools.partial(local, mesh.shape["seq"]),
        mesh=mesh,
        in_specs=(P("seq", None), row, row, copied, copied, copied, copied, P("seq", None, "blk"))
        + (split,) * 6,
        out_specs=(P("seq", None, "blk"),) * 10,
        check_vma=False,
    )
```

```python
import functools

import jax
import jax.numpy as jnp
from jax import lax
from jax.experimental import pallas as pl
from jax.experimental.pallas import tpu as pltpu
from jax.sharding import PartitionSpec as P

STEP_NUMBER = 5
F32, BF16 = jnp.float32, jnp.bfloat16
PLANES = 12
RP = 96
NO_ID = 511.0
VP = 272
FORWARD_MIB, BACKWARD_MIB, UPDATE_MIB = 32, 32, 16
NN = (((1,), (0,)), ((), ()))
NT = (((1,), (1,)), ((), ()))


def dot(a, b, dims=NN):
    return lax.dot_general(a, b, dims, preferred_element_type=F32)


def iota(shape, dim):
    return lax.broadcasted_iota(jnp.int32, shape, dim)


def split3(x):
    high = x.astype(BF16)
    rest = x - high.astype(F32)
    mid = rest.astype(BF16)
    return high, mid, (rest - mid.astype(F32)).astype(BF16)


def pick_row(x, index):
    return jnp.sum(jnp.where(iota(x.shape, 0) == index, x, 0.0), axis=0, keepdims=True)


def half_lanes(half_ref, chans):
    return pl.ds(pl.multiple_of(half_ref[0] * chans, 128), chans)


def load_table(table_ref, lanes, tail_ref, tab_ref, count):
    vocab = table_ref.shape[0]
    whole = vocab // 128 * 128
    tab_ref[:whole, :count] = table_ref[:whole, lanes].astype(BF16)
    tail_ref[...] = jnp.zeros(tail_ref.shape, F32)
    tail_ref[: vocab - whole, :] = table_ref[whole:, lanes]
    tab_ref[whole:, :count] = tail_ref[...].astype(BF16)


def blocks(x):
    two = [x[2 * p] + x[2 * p + 1] for p in range(6)]
    three = [two[0] + x[2], x[3] + two[2], two[3] + x[8], x[9] + two[5]]
    four = [two[0] + two[1], two[2] + two[3], two[4] + two[5]]
    return [x, two, three, four]


def live_planes(length):
    place = PLANES * iota((1, 128), 1)
    return [jnp.where(place + m < length, 1.0, 0.0).astype(F32) for m in range(PLANES)]


def inverse_counts(live):
    return [[1.0 / jnp.maximum(c, 1.0) for c in side] for side in blocks(live)]


def after_lane(x):
    return jnp.where(iota(x.shape, 1) == 127, 0.0, pltpu.roll(x, 127, 1))


def before_lane(x):
    return jnp.where(iota(x.shape, 1) == 0, 0.0, pltpu.roll(x, 1, 1))


def coefficients(weights):
    one, two, three, four = weights
    rows = [one[m] + two[m // 2 * 2] + two[m // 2 * 2 + 1] for m in range(PLANES)]
    rows += [four[2 * p] + four[2 * p + 1] for p in range(6)]
    for h in (0, 6):
        rows += [three[h] + three[h + 1], three[h + 2], three[h + 3], three[h + 4] + three[h + 5]]
    return rows


def pair_terms(pairs, sums):
    terms = [(m, m // 2, sums[0][m]) for m in range(PLANES)]
    terms += [(12 + p, p, sums[3][p // 2]) for p in range(6)]
    for h in range(2):
        for k, (p, j) in enumerate(((0, 0), (1, 0), (1, 1), (2, 1))):
            terms.append((18 + 4 * h + k, 3 * h + p, sums[2][2 * h + j]))
    return terms


THIRD = [18, 18, 19, 20, 21, 21, 22, 22, 23, 24, 25, 25]


def forward_kernel(
    half_ref, len_ref, lang_ref, ids_ref, cot_ref, table_ref, convw_ref, score_ref,
    emb_out, pooled_out, prob_out, coef_out, inner_out, rows_out,
    xs, cs, idcol, idc, tail, tab_all, looks, tail_half, tab, emb, conv_half, bias,
):
    s = pl.program_id(0)
    seqs, slot = ids_ref.shape
    rows, chans = cot_ref.shape[2:]
    mine = half_lanes(half_ref, chans)

    @pl.when(s == 0)
    def _():
        xs[...] = jnp.full(xs.shape, NO_ID, F32)
        xs[:seqs, :slot] = ids_ref[...].astype(F32)
        for i in range(xs.shape[1] // 128):
            cs[128 * i : 128 * (i + 1), :] = xs[:, 128 * i : 128 * (i + 1)].T
        idcol[...] = jnp.full(idcol.shape, NO_ID, F32)
        for m in range(PLANES):
            idcol[RP * m : RP * m + rows, :] = cs[pl.ds(m, rows, stride=PLANES), :]
        cols = idcol[...]
        high = jnp.floor(cols * (1.0 / 128.0))
        idc[:, 0:8] = (cols - 128.0 * high).astype(BF16)
        idc[:, 8:16] = high.astype(BF16)
        rows_out[...] = jnp.zeros(rows_out.shape, F32)
        for i in range(PLANES * RP // 128):
            flipped = idcol[128 * i : 128 * (i + 1), :].T
            for k in range(seqs):
                rows_out[k, 0:1, 128 * i : 128 * (i + 1)] = flipped[k : k + 1, :]
        load_table(table_ref, mine, tail_half, tab, chans)
        load_table(table_ref, slice(None), tail, tab_all, table_ref.shape[1])
        scores = score_ref[...]
        mixed = jnp.concatenate([convw_ref[k : k + 1, :] * scores for k in range(4)], axis=0)
        whole = tab_all[...]
        got = dot(jnp.concatenate([whole] * 3, axis=1), jnp.concatenate(split3(mixed), axis=1), NT)
        for k, part in enumerate(split3(got)):
            looks[k] = part
        constant = jnp.sum(convw_ref[4:5, :] * scores, axis=1, keepdims=True)
        bias[...] = jnp.broadcast_to(constant, bias.shape)
        conv_half[...] = convw_ref[:, mine]
        emb[PLANES * RP :, :] = jnp.zeros((emb.shape[0] - PLANES * RP, emb.shape[1]), F32)

    length, lang = len_ref[s], lang_ref[s]
    sub, lane = iota((32, 128), 0), iota((32, 128), 1)
    here = (sub % 8 == lang) & (lane % 8 == sub // 8)
    extra = 0.0
    for k in range(3):
        extra = extra + dot(looks[k], jnp.where(here & (lane // 8 == k), 1.0, 0.0).astype(BF16))
    tab[:, chans:] = extra.astype(BF16)
    sub = iota((16, 128), 0)
    spread = jnp.where(sub == s, 1.0, jnp.where(sub == s + 8, 128.0, 0.0)).astype(BF16)
    ids = dot(idc[...], spread)
    lane = iota((PLANES * RP, 128), 1).astype(F32)
    hot = jnp.concatenate([jnp.where(ids == lane + 128.0 * k, 1.0, 0.0).astype(BF16) for k in range(3)], axis=1)
    found = dot(hot, tab[...])
    emb[: PLANES * RP, :] = found
    emb_out[0] = found[:, :chans].astype(BF16)

    look = []
    for m in range(PLANES):
        x = emb[RP * m : RP * m + 128, chans : chans + 24].T
        look.append(x[0:8] + x[8:16] + x[16:24])
    ahead = {m: before_lane(look[m]) for m in (9, 10, 11)}
    live = live_planes(length)
    inverse = inverse_counts(live)
    base = pick_row(bias[...], lang)
    score = []
    for m in range(PLANES):
        value = base
        for k in range(4):
            x = look[m - k] if m >= k else ahead[m - k + PLANES]
            value = value + x[k : k + 1, :]
        score.append(jnp.where(live[m] > 0, value, 0.0))
    means = [[t * c for t, c in zip(side, inv)] for side, inv in zip(blocks(score), inverse)]
    weights = [[], [], [], []]
    for m in range(PLANES):
        own = [means[b][m // (b + 1)] for b in range(4)]
        top = functools.reduce(jnp.maximum, own)
        grown = [jnp.exp(x - top) for x in own]
        scale = 1.0 / functools.reduce(jnp.add, grown)
        for b in range(4):
            prob = grown[b] * scale
            prob_out[0, PLANES * b + m : PLANES * b + m + 1, :] = prob
            weights[b].append(0.5 * live[m] * prob * inverse[b][m // (b + 1)])
    coef_out[0, 24:32, :] = jnp.zeros((8, 128), F32)
    for k, row in enumerate(coefficients(weights)):
        coef_out[0, k : k + 1, :] = row
    coef = coef_out[0].T

    place = PLANES * iota((rows, 128), 0)
    inner = [0.0] * 26
    for c in range(chans // 128):
        lanes = slice(128 * c, 128 * (c + 1))
        w = [conv_half[k : k + 1, lanes] for k in range(5)]
        e = [emb[RP * m : RP * m + rows, lanes] for m in range(PLANES)]
        behind = {m: emb[RP * m - 1 : RP * m - 1 + rows, lanes] for m in (9, 10, 11)}
        conv = []
        for m in range(PLANES):
            value = w[4] + w[0] * e[m]
            for k in range(1, 4):
                value = value + w[k] * (e[m - k] if m >= k else behind[m - k + PLANES])
            conv.append(jnp.where(place < length - m, value, 0.0))
        cot = [cot_ref[0, p, :, lanes].astype(F32) for p in range(6)]
        pooled = [0.0] * 6
        for k, p, x in pair_terms(cot, blocks(conv)):
            inner[k] = inner[k] + cot[p] * x
            pooled[p] = pooled[p] + coef[:rows, k : k + 1] * x
        for p in range(6):
            pooled_out[0, p, :, lanes] = pooled[p].astype(BF16)
    lane = iota((rows, 128), 1)
    cols = jnp.zeros((rows, 128), F32)
    for k in range(26):
        cols = jnp.where(lane == k, jnp.sum(inner[k], axis=1, keepdims=True), cols)
    inner_out[0] = jnp.zeros((32, 128), F32)
    inner_out[0, :, :rows] = cols.T[:32]


def backward_kernel(
    half_ref, len_ref, lang_ref, core_ref, rows_ref, cot_ref, table_ref, convw_ref, score_ref,
    emb_ref, prob_ref, coef_ref, inner_ref, other_ref,
    keep_out, send_out,
    tail, tab, pulls, mixed, grad, gemb, hist, acc, taps_acc, flat, conv_half, score_half,
):
    s = pl.program_id(0)
    seqs = len_ref.shape[0]
    rows, chans = cot_ref.shape[2:]
    groups = score_ref.shape[0]
    mine = half_lanes(half_ref, chans)
    padded = (rows + 7) // 8 * 8

    @pl.when(s == 0)
    def _():
        load_table(table_ref, mine, tail, tab, chans)
        pulls[...] = jnp.zeros(pulls.shape, F32)
        mixed[...] = jnp.zeros(mixed.shape, F32)
        grad[...] = jnp.zeros(grad.shape, F32)
        acc[...] = jnp.zeros(acc.shape, F32)
        taps_acc[...] = jnp.zeros(taps_acc.shape, F32)
        hist[...] = jnp.zeros(hist.shape, F32)
        conv_half[...] = convw_ref[:, mine]
        score_half[...] = score_ref[:, mine]

    length, lang = len_ref[s], lang_ref[s]
    both = inner_ref[0] + other_ref[0]
    live = live_planes(length)
    inverse = inverse_counts(live)
    row = lambda k: both[k : k + 1, :]
    pull = [[], [], [], []]
    for m in range(PLANES):
        p = m // 2
        dots = [row(m), row(2 * p) + row(2 * p + 1), row(THIRD[m]), row(12 + p)]
        prob = [prob_ref[0, PLANES * b + m : PLANES * b + m + 1, :] for b in range(4)]
        inv = [inverse[b][m // (b + 1)] for b in range(4)]
        inner = [0.5 * jnp.where(live[m] > 0, d, 0.0) * c for d, c in zip(dots, inv)]
        mean = functools.reduce(jnp.add, [x * y for x, y in zip(prob, inner)])
        for b in range(4):
            pull[b].append(prob[b] * (inner[b] - mean) * inv[b])
    totals = [blocks(pull[b])[b] for b in range(4)]
    pull = [live[m] * (totals[0][m] + totals[1][m // 2] + totals[2][m // 3] + totals[3][m // 4]) for m in range(PLANES)]
    whole = jnp.sum(functools.reduce(jnp.add, pull), axis=1, keepdims=True)
    mixed[0:32, :] = coef_ref[0]
    for m in range(PLANES):
        mixed[32 + m : 33 + m, :] = pull[m]
    for m, x in enumerate(pull + [after_lane(x) for x in pull[:3]]):
        high = x.astype(BF16).astype(F32)
        pulls[m : m + 1, :] = high
        pulls[64 + m : 65 + m, :] = x - high
    coef = mixed[...].T
    turned = pulls[...].T
    for m in range(PLANES):
        x = turned if m == 0 else pltpu.roll(turned, 128 - m, 1)
        gemb[RP * m : RP * (m + 1), chans:] = x[:RP].astype(BF16)

    score = pick_row(score_half[...], lang)
    place = PLANES * iota((rows, 128), 0)
    for c in range(chans // 128):
        lanes = slice(128 * c, 128 * (c + 1))
        w = [conv_half[k : k + 1, lanes] for k in range(4)]
        cot = [cot_ref[0, p, :, lanes].astype(F32) for p in range(6)]
        times = lambda k, p: coef[:rows, k : k + 1] * cot[p]
        four = [times(12 + 2 * n, 2 * n) + times(13 + 2 * n, 2 * n + 1) for n in range(3)]
        three = []
        for h in range(2):
            three.append(times(18 + 4 * h, 3 * h) + times(19 + 4 * h, 3 * h + 1))
            three.append(times(20 + 4 * h, 3 * h + 1) + times(21 + 4 * h, 3 * h + 2))
        for m in range(PLANES):
            value = times(m, m // 2) + four[m // 4] + three[m // 3] + coef[:rows, 32 + m : 33 + m] * score[:, lanes]
            grad[c, RP * m : RP * m + rows, :] = jnp.where(place < length - m, value, 0.0)
        g = [grad[c, RP * m : RP * m + padded, :] for m in range(PLANES)]
        g += [grad[c, RP * m + 1 : RP * m + 1 + padded, :] for m in range(3)]
        tap = [0.0] * 5
        fold = lambda x: jnp.sum(x.reshape(padded // 8, 8, 128), axis=0)
        for m in range(PLANES):
            back = w[0] * g[m] + w[1] * g[m + 1] + w[2] * g[m + 2] + w[3] * g[m + 3]
            back = jnp.concatenate([back, jnp.zeros((RP - padded, 128), F32)], axis=0)
            gemb[RP * m : RP * (m + 1), lanes] = back.astype(BF16)
            e = emb_ref[0, RP * m : RP * (m + 1), lanes].astype(F32)[:padded]
            for k in range(4):
                tap[k] = tap[k] + fold(e * g[m + k])
            tap[4] = tap[4] + fold(g[m])
        for k in range(5):
            taps_acc[k, :, lanes] += tap[k]
    sub = iota((VP, PLANES * RP), 0).astype(F32)
    hot = jnp.where(rows_ref[0, 0:1, :] == sub, 1.0, 0.0).astype(BF16)
    got = dot(hot, gemb[...])
    acc[...] += got[:, :chans]
    hist[:VP, :] = got[:, chans:]
    counts = hist[...].T
    counts = counts[0:8] + counts[64:72]
    counts = jnp.concatenate(split3(jnp.concatenate([counts, jnp.zeros((8, 384), F32)], axis=0)), axis=0)
    from_table = dot(counts, tab[...])
    from_table = from_table[:16] + from_table[16:32] + from_table[32:]
    part = conv_half[4:5, :] * whole
    for k in range(4):
        part = part + conv_half[k : k + 1, :] * from_table[k : k + 1, :]
    acc[VP - groups : VP, :] += jnp.where(iota((groups, chans), 0) == lang, part, 0.0)

    @pl.when(s == seqs - 1)
    def _():
        for k in range(5):
            at = VP - groups - 5 + k
            acc[at : at + 1, :] = jnp.sum(taps_acc[k], axis=0, keepdims=True)
        flat[...] = jnp.zeros(flat.shape, F32)
        for k in range(chans // 128):
            flat[VP * k : VP * (k + 1), :] = acc[:, 128 * k : 128 * (k + 1)]
        part = keep_out.shape[0]
        own = pl.multiple_of(core_ref[0] * part, 8)
        theirs = pl.multiple_of((1 - core_ref[0]) * part, 8)
        keep_out[...] = flat[pl.ds(own, part), :]
        send_out[...] = flat[pl.ds(theirs, part), :]


def adamw(weight, grad, moment, second, rate):
    new_m = 0.9 * moment + 0.1 * grad
    new_v = 0.999 * second + 0.001 * grad * grad
    m_hat = new_m / (1.0 - 0.9**STEP_NUMBER)
    v_hat = new_v / (1.0 - 0.999**STEP_NUMBER)
    new_w = weight - rate * (m_hat / (jnp.sqrt(v_hat) + 1e-08) + 0.01 * weight)
    return new_m, new_v, new_w


def update_kernel(half_ref, place_ref, owner_ref, mine_ref, other_ref, *refs):
    ins, outs, flat = refs[:9], refs[9:18], refs[18]
    core, near, seq = place_ref[0], place_ref[1], place_ref[2]
    rows = mine_ref.shape[0] // 2
    for side, ref in ((core, mine_ref), (1 - core, other_ref)):
        for k in range(2):
            piece = near if k == 0 else 1 - near
            flat[pl.ds(pl.multiple_of((2 * side + piece) * rows, 8), rows), :] = ref[k * rows : (k + 1) * rows, :]
    vocab, chans = ins[1].shape
    groups = ins[6].shape[0]
    spans = ((0, vocab), (VP - groups - 5, 5), (VP - groups, groups))
    for t, rate in enumerate((0.5, 0.3, 0.05)):
        first, count = spans[t]
        owned = owner_ref[t] == seq
        for k in range(chans // 128):
            lanes = slice(128 * k, 128 * (k + 1))
            weight = ins[3 * t][:, pl.ds(pl.multiple_of(half_ref[0] * chans + 128 * k, 128), 128)]
            grad = flat[VP * k + first : VP * k + first + count, :]
            new = adamw(weight, grad, ins[3 * t + 1][:, lanes], ins[3 * t + 2][:, lanes], rate)
            for q in range(3):
                out = outs[3 * t + q]
                value = jnp.where(owned, new[q], 0.0)
                if count == groups:
                    out[0, :, lanes] = value
                else:
                    out[:, 0, lanes] = value


def local(
    seq_size, byte_ids, lengths, lang_ids, owners, table, conv_w, score_w, cotangent,
    table_m, table_v, conv_m, conv_v, score_m, score_v,
):
    seqs, slot = byte_ids.shape
    vocab, full = table.shape
    half_rows, chans = cotangent.shape[1:]
    groups = score_w.shape[0]
    rows = slot // PLANES
    assert rows * PLANES == slot and rows <= RP - 2
    half = lax.axis_index("blk").astype(jnp.int32).reshape(1)
    seq = lax.axis_index("seq").astype(jnp.int32)
    core, near = seq % 2, (seq // 4) % 2
    vmem = pltpu.VMEM
    shape = jax.ShapeDtypeStruct
    whole = lambda *dims: pl.BlockSpec(dims, lambda s, *_: (0,) * len(dims))
    by_seq = lambda *dims: pl.BlockSpec((1,) + dims, lambda s, *_: (s,) + (0,) * len(dims))

    def call(kernel, name, scalars, arrays, in_specs, outs, out_specs, scratch, mib, steps):
        return pl.pallas_call(
            kernel,
            grid_spec=pltpu.PrefetchScalarGridSpec(
                num_scalar_prefetch=len(scalars), grid=(steps,),
                in_specs=in_specs, out_specs=out_specs, scratch_shapes=scratch,
            ),
            out_shape=outs,
            compiler_params=pltpu.CompilerParams(
                vmem_limit_bytes=mib * 1024 * 1024, dimension_semantics=("arbitrary",)
            ),
            name=name,
        )(*scalars, *arrays)

    planes = cotangent.reshape(seqs, rows, 6, chans).transpose(0, 2, 1, 3)
    long = PLANES * RP
    emb, pooled, prob, coef, inner, id_rows = call(
        forward_kernel, "forward",
        [half, lengths, lang_ids], [byte_ids, planes, table, conv_w, score_w],
        [whole(seqs, slot), by_seq(6, rows, chans), whole(vocab, full), whole(5, full), whole(groups, full)],
        [
            pltpu.HBM((seqs, long, chans), BF16), pltpu.HBM((seqs, 6, rows, chans), BF16),
            shape((seqs, 48, 128), F32), shape((seqs, 32, 128), F32), shape((seqs, 32, 128), F32),
            shape((seqs, 8, long), F32),
        ],
        [
            by_seq(long, chans), by_seq(6, rows, chans), by_seq(48, 128), by_seq(32, 128), by_seq(32, 128),
            whole(seqs, 8, long),
        ],
        [
            vmem((8, long), F32), vmem((long, 8), F32), vmem((long, 8), F32), vmem((long, 16), BF16),
            vmem((128, full), F32), vmem((384, full), BF16), vmem((3, 384, 32), BF16),
            vmem((128, chans), F32), vmem((384, chans + 128), BF16), vmem((long + 32, chans + 128), F32),
            vmem((5, chans), F32), vmem((8, 128), F32),
        ],
        FORWARD_MIB, seqs,
    )
    other = lax.ppermute(inner, "blk", [(0, 1), (1, 0)])
    emb = pltpu.with_memory_space_constraint(emb, pltpu.HBM)
    total = -(-VP * (chans // 128) // 32) * 32
    keep, send = call(
        backward_kernel, "backward",
        [half, lengths, lang_ids, core.reshape(1)],
        [id_rows, planes, table, conv_w, score_w, emb, prob, coef, inner, other],
        [
            by_seq(8, long), by_seq(6, rows, chans), whole(vocab, full), whole(5, full), whole(groups, full),
            by_seq(long, chans), by_seq(48, 128), by_seq(32, 128), by_seq(32, 128), by_seq(32, 128),
        ],
        [shape((total // 2, 128), F32)] * 2,
        [whole(total // 2, 128)] * 2,
        [
            vmem((128, chans), F32), vmem((384, chans), BF16), vmem((128, 128), F32), vmem((48, 128), F32),
            vmem((chans // 128, long + 8, 128), F32), vmem((long, chans + 128), BF16), vmem((384, 128), F32),
            vmem((VP, chans), F32), vmem((5, 8, chans), F32), vmem((total, 128), F32),
            vmem((5, chans), F32), vmem((groups, chans), F32),
        ],
        BACKWARD_MIB, seqs,
    )

    def swap(x, step):
        return lax.ppermute(x, "seq", [(i, i ^ step) for i in range(seq_size)])

    keep, pooled = lax.optimization_barrier((keep, pooled))
    pooled = pooled.transpose(0, 2, 1, 3).reshape(seqs, half_rows, chans)
    mine = keep + swap(send, 1)
    quarter = total // 4
    held = lax.dynamic_slice_in_dim(mine, near * quarter, quarter, 0)
    sent = lax.dynamic_slice_in_dim(mine, (1 - near) * quarter, quarter, 0)
    held = held + swap(sent, 4)
    step = 2
    while step < seq_size:
        if step != 4:
            sent = swap(held, step)
            if step * 2 == seq_size:
                sent, pooled = lax.optimization_barrier((sent, pooled))
            held = held + sent
        step *= 2
    mine = jnp.concatenate([held, swap(held, 4)], axis=0)
    other = swap(mine, 1)

    place = jnp.stack([core, near, seq])
    arrays = [mine, other, table, table_m, table_v, conv_w, conv_m, conv_v, score_w, score_m, score_v]
    outs = []
    for count in (vocab, 5):
        outs += [shape((count, 1, chans), F32)] * 3
    outs += [shape((1, groups, chans), F32)] * 3
    updated = call(
        update_kernel, "update",
        [half, place, owners], arrays, [whole(*x.shape) for x in arrays],
        outs, [whole(*x.shape) for x in outs], [vmem((total, 128), F32)], UPDATE_MIB, 1,
    )
    updated = [jnp.transpose(x, (1, 0, 2)) if k < 6 else x for k, x in enumerate(updated)]
    return (pooled, *updated)


def solution(mesh):
    row, split, copied = P("seq"), P(None, "blk"), P()
    return jax.shard_map(
        functools.partial(local, mesh.shape["seq"]),
        mesh=mesh,
        in_specs=(P("seq", None), row, row, copied, copied, copied, copied, P("seq", None, "blk"))
        + (split,) * 6,
        out_specs=(P("seq", None, "blk"),) * 10,
        check_vma=False,
    )
```

```python
import functools

import jax
import jax.numpy as jnp
from jax import lax
from jax.experimental import pallas as pl
from jax.experimental.pallas import tpu as pltpu
from jax.sharding import PartitionSpec as P

STEP_NUMBER = 5
F32, BF16 = jnp.float32, jnp.bfloat16
PLANES = 12
RP = 96
NO_ID = 511.0
VP = 272
FORWARD_MIB, POOLED_MIB, BACKWARD_MIB, UPDATE_MIB = 32, 16, 32, 16
NN = (((1,), (0,)), ((), ()))
NT = (((1,), (1,)), ((), ()))


def dot(a, b, dims=NN):
    return lax.dot_general(a, b, dims, preferred_element_type=F32)


def iota(shape, dim):
    return lax.broadcasted_iota(jnp.int32, shape, dim)


def split3(x):
    high = x.astype(BF16)
    rest = x - high.astype(F32)
    mid = rest.astype(BF16)
    return high, mid, (rest - mid.astype(F32)).astype(BF16)


def pick_row(x, index):
    return jnp.sum(jnp.where(iota(x.shape, 0) == index, x, 0.0), axis=0, keepdims=True)


def half_lanes(half_ref, chans):
    return pl.ds(pl.multiple_of(half_ref[0] * chans, 128), chans)


def load_table(table_ref, lanes, tail_ref, tab_ref, count):
    vocab = table_ref.shape[0]
    whole = vocab // 128 * 128
    tab_ref[:whole, :count] = table_ref[:whole, lanes].astype(BF16)
    tail_ref[...] = jnp.zeros(tail_ref.shape, F32)
    tail_ref[: vocab - whole, :] = table_ref[whole:, lanes]
    tab_ref[whole:, :count] = tail_ref[...].astype(BF16)


def blocks(x):
    two = [x[2 * p] + x[2 * p + 1] for p in range(6)]
    three = [two[0] + x[2], x[3] + two[2], two[3] + x[8], x[9] + two[5]]
    four = [two[0] + two[1], two[2] + two[3], two[4] + two[5]]
    return [x, two, three, four]


def live_planes(length):
    place = PLANES * iota((1, 128), 1)
    return [jnp.where(place + m < length, 1.0, 0.0).astype(F32) for m in range(PLANES)]


def inverse_counts(live):
    return [[1.0 / jnp.maximum(c, 1.0) for c in side] for side in blocks(live)]


def after_lane(x):
    return jnp.where(iota(x.shape, 1) == 127, 0.0, pltpu.roll(x, 127, 1))


def before_lane(x):
    return jnp.where(iota(x.shape, 1) == 0, 0.0, pltpu.roll(x, 1, 1))


def coefficients(weights):
    one, two, three, four = weights
    rows = [one[m] + two[m // 2 * 2] + two[m // 2 * 2 + 1] for m in range(PLANES)]
    rows += [four[2 * p] + four[2 * p + 1] for p in range(6)]
    for h in (0, 6):
        rows += [three[h] + three[h + 1], three[h + 2], three[h + 3], three[h + 4] + three[h + 5]]
    return rows


def convolved(w, e, behind, live):
    out = []
    for m in range(PLANES):
        value = w[4] + w[0] * e[m]
        for k in range(1, 4):
            value = value + w[k] * (e[m - k] if m >= k else behind[m - k + PLANES])
        out.append(jnp.where(live[m], value, 0.0))
    return out


def pair_terms(sums):
    terms = [(m, m // 2, sums[0][m]) for m in range(PLANES)]
    terms += [(12 + p, p, sums[3][p // 2]) for p in range(6)]
    for h in range(2):
        for k, (p, j) in enumerate(((0, 0), (1, 0), (1, 1), (2, 1))):
            terms.append((18 + 4 * h + k, 3 * h + p, sums[2][2 * h + j]))
    return terms


THIRD = [18, 18, 19, 20, 21, 21, 22, 22, 23, 24, 25, 25]


def forward_kernel(
    half_ref, len_ref, lang_ref, ids_ref, cot_ref, table_ref, convw_ref, score_ref,
    emb_out, conv_out, look_out, inner_out, rows_out,
    xs, cs, idcol, idc, tail, tab_all, looks, tail_half, tab, emb_a, emb_b, low_a, low_b,
    conv_half, cotf, turned, hots, conv_a, conv_b, sems,
):
    n = pl.program_id(0)
    seqs, slot = ids_ref.shape
    rows, chans = cot_ref.shape[2:]
    long = PLANES * RP
    mine = half_lanes(half_ref, chans)
    slots = ((emb_a, low_a), (emb_b, low_b))
    convs = (conv_a, conv_b)

    def send(q, k):
        return pltpu.make_async_copy(slots[k][1], emb_out.at[q], sems.at[k])

    def send_conv(q, k):
        return pltpu.make_async_copy(convs[k], conv_out.at[q], sems.at[2 + k])

    def look_up(q, slot_refs):
        emb, low = slot_refs
        lang = lang_ref[q]
        sub, lane = iota((32, 128), 0), iota((32, 128), 1)
        here = (sub % 8 == lang) & (lane % 8 == sub // 8)
        extra = 0.0
        for k in range(3):
            extra = extra + dot(looks[k], jnp.where(here & (lane // 8 == k), 1.0, 0.0).astype(BF16))
        tab[:, chans:] = extra.astype(BF16)
        sub = iota((16, 128), 0)
        spread = jnp.where(sub == q, 1.0, jnp.where(sub == q + 8, 128.0, 0.0)).astype(BF16)
        ids = dot(idc[...], spread)
        lane = iota((long, 128), 1).astype(F32)
        for k in range(3):
            hots[:, 128 * k : 128 * (k + 1)] = jnp.where(ids == lane + 128.0 * k, 1.0, 0.0).astype(BF16)
        found = dot(hots[...], tab[...])
        emb[:long, :] = found
        low[...] = found[:, :chans].astype(BF16)
        for m in range(PLANES):
            x = emb[RP * m : RP * m + 128, chans : chans + 24].T
            look_out[q, 8 * m : 8 * m + 8, :] = x[0:8] + x[8:16] + x[16:24]

    def convolve(q, u):
        emb, _ = slots[u]
        length = len_ref[q]
        for p in range(6):
            cotf[p, :rows, :] = cot_ref[u, p].astype(F32)
        place = PLANES * iota((8, 128), 0)
        lane = iota((8, 128), 1)
        for r in range(0, rows, 8):
            live = [place < length - (m + PLANES * r) for m in range(PLANES)]
            inner = [0.0] * 26
            for c in range(chans // 128):
                lanes = slice(128 * c, 128 * (c + 1))
                w = [conv_half[k : k + 1, lanes] for k in range(5)]
                e = [emb[RP * m + r : RP * m + r + 8, lanes] for m in range(PLANES)]
                behind = {m: emb[RP * m - 1 + r : RP * m + 7 + r, lanes] for m in (9, 10, 11)}
                conv = convolved(w, e, behind, live)
                for m in range(PLANES):
                    convs[u][m, r : r + 8, lanes] = conv[m]
                for k, p, x in pair_terms(blocks(conv)):
                    inner[k] = inner[k] + cotf[p, r : r + 8, lanes] * x
            out = jnp.zeros((8, 128), F32)
            for k in range(26):
                out = jnp.where(lane == k, jnp.sum(inner[k], axis=1, keepdims=True), out)
            turned[r : r + 8, :] = out
        inner_out[q] = turned[...].T[:32]

    @pl.when(n == 0)
    def _():
        xs[...] = jnp.full(xs.shape, NO_ID, F32)
        xs[:seqs, :slot] = ids_ref[...].astype(F32)
        for i in range(xs.shape[1] // 128):
            cs[128 * i : 128 * (i + 1), :] = xs[:, 128 * i : 128 * (i + 1)].T
        idcol[...] = jnp.full(idcol.shape, NO_ID, F32)
        for m in range(PLANES):
            idcol[RP * m : RP * m + rows, :] = cs[pl.ds(m, rows, stride=PLANES), :]
        cols = idcol[...]
        high = jnp.floor(cols * (1.0 / 128.0))
        idc[:, 0:8] = (cols - 128.0 * high).astype(BF16)
        idc[:, 8:16] = high.astype(BF16)
        rows_out[...] = jnp.zeros(rows_out.shape, F32)
        for i in range(long // 128):
            flipped = idcol[128 * i : 128 * (i + 1), :].T
            for k in range(seqs):
                rows_out[k, 0:1, 128 * i : 128 * (i + 1)] = flipped[k : k + 1, :]
        load_table(table_ref, mine, tail_half, tab, chans)
        load_table(table_ref, slice(None), tail, tab_all, table_ref.shape[1])
        scores = score_ref[...]
        mixed = jnp.concatenate([convw_ref[k : k + 1, :] * scores for k in range(4)], axis=0)
        mixed = jnp.concatenate(list(split3(mixed)) + [jnp.zeros(mixed.shape, BF16)], axis=0)
        got = dot(tab_all[...], mixed, NT)
        got = got + pltpu.roll(got, 96, 1) + pltpu.roll(got, 64, 1)
        for k, part in enumerate(split3(got[:, :32])):
            looks[k] = part
        conv_half[...] = convw_ref[:, mine]
        turned[...] = jnp.zeros(turned.shape, F32)
        cotf[...] = jnp.zeros(cotf.shape, F32)
        for emb, _ in slots:
            emb[long:, :] = jnp.zeros((emb.shape[0] - long, emb.shape[1]), F32)
        look_up(0, slots[0])
        send(0, 0).start()

    for u in range(2):
        q = 2 * n + u
        later = q + 1
        within = jnp.minimum(later, seqs - 1)

        @pl.when(later >= 2)
        def _():
            send(0, 1 - u).wait()

        @pl.when(q >= 2)
        def _():
            send_conv(0, u).wait()

        look_up(within, slots[1 - u])
        convolve(q, u)
        send_conv(q, u).start()

        @pl.when(later < seqs)
        def _():
            send(within, 1 - u).start()

    @pl.when(n == pl.num_programs(0) - 1)
    def _():
        send(0, 1).wait()
        for k in range(2):
            send_conv(0, k).wait()


def score_kernel(len_ref, lang_ref, look_ref, convw_ref, score_ref, prob_out, coef_out):
    bias = jnp.sum(convw_ref[4:5, :] * score_ref[...], axis=1, keepdims=True)
    bias = jnp.broadcast_to(bias, (score_ref.shape[0], 128))
    for q in range(look_ref.shape[0]):
        look = [look_ref[q, 8 * m : 8 * m + 8, :] for m in range(PLANES)]
        ahead = {m: before_lane(look[m]) for m in (9, 10, 11)}
        live = live_planes(len_ref[q])
        inverse = inverse_counts(live)
        base = pick_row(bias, lang_ref[q])
        score = []
        for m in range(PLANES):
            value = base
            for k in range(4):
                x = look[m - k] if m >= k else ahead[m - k + PLANES]
                value = value + x[k : k + 1, :]
            score.append(jnp.where(live[m] > 0, value, 0.0))
        means = [[t * c for t, c in zip(side, inv)] for side, inv in zip(blocks(score), inverse)]
        weights = [[], [], [], []]
        for m in range(PLANES):
            own = [means[b][m // (b + 1)] for b in range(4)]
            top = functools.reduce(jnp.maximum, own)
            grown = [jnp.exp(x - top) for x in own]
            scale = 1.0 / functools.reduce(jnp.add, grown)
            for b in range(4):
                prob = grown[b] * scale
                prob_out[q, PLANES * b + m : PLANES * b + m + 1, :] = prob
                weights[b].append(0.5 * live[m] * prob * inverse[b][m // (b + 1)])
        coef_out[q, 24:32, :] = jnp.zeros((8, 128), F32)
        for k, row in enumerate(coefficients(weights)):
            coef_out[q, k : k + 1, :] = row


def spread_masks(keep_ref):
    lane = iota((16, 128), 1)
    for j in range(keep_ref.shape[0]):
        keep_ref[j] = jnp.where(lane % 64 == j, 1.0, 0.0).astype(BF16)


def spread_columns(both, keep_ref, cols_ref, columns):
    count = both.shape[0] // 16
    both = both.reshape(count, 16, 128)
    wide = [(both * keep_ref[j][None]).reshape(16 * count, 128) for j in columns]
    got = dot(jnp.concatenate(wide, axis=0), jnp.ones((128, 128), BF16))
    for k, j in enumerate(columns):
        cols_ref[j] = got[16 * count * k : 16 * count * (k + 1)]


def pooled_kernel(first, *refs):
    if first:
        refs = refs[1:]
    coef_ref, conv_ref, pooled_out, cols, conv, poolf, low, keep, both, sems = refs
    padded, chans = conv_ref.shape[2:]
    rows = pooled_out.shape[2]
    chunks = chans // 128
    fetches = []
    for u in range(2):
        for c in range(chunks):
            source = conv_ref.at[first + u, :, :, pl.ds(128 * c, 128)]
            fetches.append(pltpu.make_async_copy(source, conv.at[u, c], sems.at[chunks * u + c]))
            fetches[-1].start()
    sends = []
    spread_masks(keep)
    both[...] = jnp.zeros(both.shape, F32)
    for u in range(2):
        high = coef_ref[first + u].astype(BF16).astype(F32)
        both[0:32, :] = high
        both[64:96, :] = coef_ref[first + u] - high
        across = both[...].T[:RP].astype(BF16)
        for k in range(0, 26, 13):
            spread_columns(across, keep, cols, range(k, k + 13))
        for c in range(chunks):
            fetches[chunks * u + c].wait()
            for r in range(0, padded, 8):
                pooled = [0.0] * 6
                for k, p, x in pair_terms(blocks([conv[u, c, m, r : r + 8, :] for m in range(PLANES)])):
                    pooled[p] = pooled[p] + cols[k, r : r + 8, :] * x
                for p in range(6):
                    poolf[p, r : r + 8, :] = pooled[p]
            for p in range(6):
                low[u, p, :, 128 * c : 128 * (c + 1)] = poolf[p, :rows, :].astype(BF16)
        sends.append(pltpu.make_async_copy(low.at[u], pooled_out.at[first + u], sems.at[2 * chunks + u]))
        sends[-1].start()
    for copy in sends:
        copy.wait()


def backward_kernel(
    half_ref, len_ref, lang_ref, core_ref, rows_ref, cot_ref, table_ref, convw_ref, score_ref,
    emb_ref, prob_ref, coef_ref, inner_ref, other_ref,
    keep_out, send_out,
    tail, tab, pulls, mixed, grad, hist, acc, taps_acc, flat, conv_half, score_half, cotf,
    gemb_a, gemb_b, low_a, low_b, cols_a, cols_b, turned_a, turned_b, total_a, total_b, wholes_a, wholes_b, hots,
    keep, sems,
):
    n = pl.program_id(0)
    seqs = len_ref.shape[0]
    rows, chans = cot_ref.shape[2:]
    groups = score_ref.shape[0]
    mine = half_lanes(half_ref, chans)
    padded = (rows + 7) // 8 * 8
    gembs, lows, wholes = (gemb_a, gemb_b), (low_a, low_b), (wholes_a, wholes_b)
    ready = ((cols_a, turned_a, total_a), (cols_b, turned_b, total_b))

    def fetch(q, k):
        return pltpu.make_async_copy(emb_ref.at[q], lows[k], sems.at[k])

    def to_table(q, k):
        sub = iota((VP, PLANES * RP), 0).astype(F32)
        hots[...] = jnp.where(rows_ref[q, 0:1, :] == sub, 1.0, 0.0).astype(BF16)
        acc[:, :256] += dot(hots[...], gembs[k][:, :256])
        yield
        got = dot(hots[...], gembs[k][:, 256:])
        acc[:, 256:] += got[:, : chans - 256]
        hist[:VP, :] = got[:, chans - 256 :]
        yield
        counts = hist[...].T
        counts = counts[0:8] + counts[64:72]
        counts = jnp.concatenate([counts, jnp.zeros((8, 384), F32)], axis=0)
        from_table = dot(jnp.concatenate(split3(counts), axis=0), tab[...])
        from_table = from_table[:16] + from_table[16:32] + from_table[32:]
        part = conv_half[4:5, :] * wholes[k][0:1, :]
        for j in range(4):
            part = part + conv_half[j : j + 1, :] * from_table[j : j + 1, :]
        acc[VP - groups : VP, :] += jnp.where(iota((groups, chans), 0) == lang_ref[q], part, 0.0)
        yield

    def prepare(q, k):
        cols, turned, total = ready[k]
        both = inner_ref[q] + other_ref[q]
        live = live_planes(len_ref[q])
        inverse = inverse_counts(live)
        row = lambda j: both[j : j + 1, :]
        pull = [[], [], [], []]
        for m in range(PLANES):
            p = m // 2
            dots = [row(m), row(2 * p) + row(2 * p + 1), row(THIRD[m]), row(12 + p)]
            prob = [prob_ref[q, PLANES * b + m : PLANES * b + m + 1, :] for b in range(4)]
            inv = [inverse[b][m // (b + 1)] for b in range(4)]
            inner = [0.5 * jnp.where(live[m] > 0, d, 0.0) * c for d, c in zip(dots, inv)]
            mean = functools.reduce(jnp.add, [x * y for x, y in zip(prob, inner)])
            for b in range(4):
                pull[b].append(prob[b] * (inner[b] - mean) * inv[b])
            if m in (2, 5, 8):
                yield
        sums = [blocks(pull[b])[b] for b in range(4)]
        pull = [live[m] * (sums[0][m] + sums[1][m // 2] + sums[2][m // 3] + sums[3][m // 4]) for m in range(PLANES)]
        whole = jnp.sum(functools.reduce(jnp.add, pull), axis=1, keepdims=True)
        total[...] = jnp.broadcast_to(whole, total.shape)
        high = coef_ref[q].astype(BF16).astype(F32)
        mixed[0:32, :] = high
        mixed[64:96, :] = coef_ref[q] - high
        for m, x in enumerate(pull + [after_lane(x) for x in pull[:3]]):
            high = x.astype(BF16).astype(F32)
            pulls[m : m + 1, :] = high
            pulls[64 + m : 65 + m, :] = x - high
            if m < PLANES:
                mixed[32 + m : 33 + m, :] = high
                mixed[96 + m : 97 + m, :] = x - high
        yield
        turned[...] = pulls[...].T
        coef = mixed[...].T[:RP].astype(BF16)
        yield
        columns = [*range(26), *range(32, 44)]
        for k in range(0, len(columns), 5):
            spread_columns(coef, keep, cols, columns[k : k + 5])
            yield
        while True:
            yield

    def gradients(q, u, table, coming):
        cols, turned, total = ready[u]
        gemb, low = gembs[u], lows[u]
        wholes[u][...] = total[...]
        length = len_ref[q]
        for m in range(PLANES):
            x = turned[...] if m == 0 else pltpu.roll(turned[...], 128 - m, 1)
            gemb[RP * m : RP * (m + 1), chans:] = x[:RP].astype(BF16)
        score = pick_row(score_half[...], lang_ref[q])
        for p in range(6):
            cotf[p, :rows, :] = cot_ref[u, p].astype(F32)
        place = PLANES * iota((8, 128), 0)
        for r in range(0, rows, 8):
            if r == 8:
                next(table)
            alive = [place < length - (m + PLANES * r) for m in range(PLANES)]
            for c in range(chans // 128):
                lanes = slice(128 * c, 128 * (c + 1))
                cot = [cotf[p, r : r + 8, lanes] for p in range(6)]
                times = lambda j, p: cols[j, r : r + 8, :] * cot[p]
                four = [times(12 + 2 * j, 2 * j) + times(13 + 2 * j, 2 * j + 1) for j in range(3)]
                three = []
                for h in range(2):
                    three.append(times(18 + 4 * h, 3 * h) + times(19 + 4 * h, 3 * h + 1))
                    three.append(times(20 + 4 * h, 3 * h + 1) + times(21 + 4 * h, 3 * h + 2))
                for m in range(PLANES):
                    value = times(m, m // 2) + four[m // 4] + three[m // 3]
                    value = value + cols[32 + m, r : r + 8, :] * score[:, lanes]
                    grad[c, RP * m + r : RP * m + r + 8, :] = jnp.where(alive[m], value, 0.0)
        @pl.when(length > 0)
        def _():
            for c in range(chans // 128):
                lanes = slice(128 * c, 128 * (c + 1))
                w = [conv_half[k : k + 1, lanes] for k in range(4)]
                tap = [0.0] * 5
                for r in range(0, padded, 16):
                    count = min(16, padded - r)
                    if r == 16 and c < 2:
                        next(table)
                    next(coming)
                    g = [grad[c, RP * m + r : RP * m + r + count, :] for m in range(PLANES)]
                    g += [grad[c, RP * m + r + 1 : RP * m + r + 1 + count, :] for m in range(3)]
                    fold = lambda x: x[:8] + x[8:] if count == 16 else x
                    for m in range(PLANES):
                        back = w[0] * g[m] + w[1] * g[m + 1] + w[2] * g[m + 2] + w[3] * g[m + 3]
                        if count < 16:
                            back = jnp.concatenate([back, jnp.zeros((16 - count, 128), F32)], axis=0)
                        gemb[RP * m + r : RP * m + r + 16, lanes] = back.astype(BF16)
                        e = low[RP * m + r : RP * m + r + 16, lanes].astype(F32)[:count]
                        for k in range(4):
                            tap[k] = tap[k] + fold(e * g[m + k])
                        tap[4] = tap[4] + fold(g[m])
                for k in range(5):
                    taps_acc[k, :, lanes] += tap[k]

    @pl.when(n == 0)
    def _():
        fetch(0, 0).start()
        load_table(table_ref, mine, tail, tab, chans)
        for k in range(2):
            gembs[k][...] = jnp.zeros(gembs[k].shape, BF16)
            wholes[k][...] = jnp.zeros(wholes[k].shape, F32)
        cotf[...] = jnp.zeros(cotf.shape, F32)
        pulls[...] = jnp.zeros(pulls.shape, F32)
        mixed[...] = jnp.zeros(mixed.shape, F32)
        for m in range(PLANES):
            grad[:, RP * m + rows : RP * (m + 1), :] = jnp.zeros((chans // 128, RP - rows, 128), F32)
        grad[:, PLANES * RP :, :] = jnp.zeros((chans // 128, 8, 128), F32)
        acc[...] = jnp.zeros(acc.shape, F32)
        taps_acc[...] = jnp.zeros(taps_acc.shape, F32)
        hist[...] = jnp.zeros(hist.shape, F32)
        conv_half[...] = convw_ref[:, mine]
        score_half[...] = score_ref[:, mine]
        spread_masks(keep)
        first = prepare(0, 0)
        for _ in range(30):
            next(first)

    for u in range(2):
        q = 2 * n + u
        later = jnp.minimum(q + 1, seqs - 1)
        fetch(q, u).wait()

        @pl.when(q + 1 < seqs)
        def _():
            fetch(later, 1 - u).start()

        gradients(q, u, to_table(jnp.maximum(q - 1, 0), 1 - u), prepare(later, 1 - u))

    @pl.when(n == pl.num_programs(0) - 1)
    def _():
        for _ in to_table(seqs - 1, 1):
            pass
        for k in range(5):
            at = VP - groups - 5 + k
            acc[at : at + 1, :] = jnp.sum(taps_acc[k], axis=0, keepdims=True)
        flat[VP * (chans // 128) :, :] = jnp.zeros((flat.shape[0] - VP * (chans // 128), 128), F32)
        for k in range(chans // 128):
            flat[VP * k : VP * (k + 1), :] = acc[:, 128 * k : 128 * (k + 1)]
        part = keep_out.shape[0]
        own = pl.multiple_of(core_ref[0] * part, 8)
        theirs = pl.multiple_of((1 - core_ref[0]) * part, 8)
        keep_out[...] = flat[pl.ds(own, part), :]
        send_out[...] = flat[pl.ds(theirs, part), :]


def adamw(weight, grad, moment, second, rate):
    new_m = 0.9 * moment + 0.1 * grad
    new_v = 0.999 * second + 0.001 * grad * grad
    m_hat = new_m / (1.0 - 0.9**STEP_NUMBER)
    v_hat = new_v / (1.0 - 0.999**STEP_NUMBER)
    new_w = weight - rate * (m_hat / (jnp.sqrt(v_hat) + 1e-08) + 0.01 * weight)
    return new_m, new_v, new_w


def update_kernel(half_ref, place_ref, owner_ref, mine_ref, other_ref, *refs):
    ins, outs, flat = refs[:9], refs[9:18], refs[18]
    core, seq = place_ref[0], place_ref[3]
    rows = mine_ref.shape[0] // 2
    for side, near, ref in ((core, place_ref[1], mine_ref), (1 - core, place_ref[2], other_ref)):
        for k in range(2):
            piece = near if k == 0 else 1 - near
            flat[pl.ds(pl.multiple_of((2 * side + piece) * rows, 8), rows), :] = ref[k * rows : (k + 1) * rows, :]
    vocab, chans = ins[1].shape
    groups = ins[6].shape[0]
    spans = ((0, vocab), (VP - groups - 5, 5), (VP - groups, groups))
    for t, rate in enumerate((0.5, 0.3, 0.05)):
        first, count = spans[t]
        owned = owner_ref[t] == seq
        for k in range(chans // 128):
            lanes = slice(128 * k, 128 * (k + 1))
            weight = ins[3 * t][:, pl.ds(pl.multiple_of(half_ref[0] * chans + 128 * k, 128), 128)]
            grad = flat[VP * k + first : VP * k + first + count, :]
            new = adamw(weight, grad, ins[3 * t + 1][:, lanes], ins[3 * t + 2][:, lanes], rate)
            for q in range(3):
                out = outs[3 * t + q]
                value = jnp.where(owned, new[q], 0.0)
                if count == groups:
                    out[0, :, lanes] = value
                else:
                    out[:, 0, lanes] = value


def local(
    seq_size, byte_ids, lengths, lang_ids, owners, table, conv_w, score_w, cotangent,
    table_m, table_v, conv_m, conv_v, score_m, score_v,
):
    seqs, slot = byte_ids.shape
    vocab, full = table.shape
    half_rows, chans = cotangent.shape[1:]
    groups = score_w.shape[0]
    rows = slot // PLANES
    assert rows * PLANES == slot and rows <= RP - 2 and seqs % 2 == 0
    half = lax.axis_index("blk").astype(jnp.int32).reshape(1)
    seq = lax.axis_index("seq").astype(jnp.int32)
    core, far_bit, near_bit = seq % 2, (seq // 4) % 2, (seq // 2) % 2
    near = jnp.where(core == 0, far_bit, near_bit)
    near_other = jnp.where(core == 0, near_bit, far_bit)
    vmem = pltpu.VMEM
    shape = jax.ShapeDtypeStruct
    whole = lambda *dims: pl.BlockSpec(dims, lambda s, *_: (0,) * len(dims))
    by_two = lambda *dims: pl.BlockSpec((2,) + dims, lambda s, *_: (s,) + (0,) * len(dims))
    by_seq = lambda *dims: pl.BlockSpec((1,) + dims, lambda s, *_: (s,) + (0,) * len(dims))

    def call(kernel, name, scalars, arrays, in_specs, outs, out_specs, scratch, mib, steps):
        return pl.pallas_call(
            kernel,
            grid_spec=pltpu.PrefetchScalarGridSpec(
                num_scalar_prefetch=len(scalars), grid=(steps,),
                in_specs=in_specs, out_specs=out_specs, scratch_shapes=scratch,
            ),
            out_shape=outs,
            compiler_params=pltpu.CompilerParams(
                vmem_limit_bytes=mib * 1024 * 1024, dimension_semantics=("arbitrary",)
            ),
            name=name,
        )(*scalars, *arrays)

    planes = cotangent.reshape(seqs, rows, 6, chans).transpose(0, 2, 1, 3)
    long = PLANES * RP
    padded = (rows + 7) // 8 * 8
    emb, conv, look, inner, id_rows = call(
        forward_kernel, "forward",
        [half, lengths, lang_ids], [byte_ids, planes, table, conv_w, score_w],
        [whole(seqs, slot), by_two(6, rows, chans), whole(vocab, full), whole(5, full), whole(groups, full)],
        [
            pltpu.HBM((seqs, long, chans), BF16), pltpu.HBM((seqs, PLANES, padded, chans), F32),
            shape((seqs, 8 * PLANES, 128), F32),
            shape((seqs, 32, 128), F32), shape((seqs, 8, long), F32),
        ],
        [
            pl.BlockSpec(memory_space=pltpu.HBM), pl.BlockSpec(memory_space=pltpu.HBM),
            whole(seqs, 8 * PLANES, 128), whole(seqs, 32, 128), whole(seqs, 8, long),
        ],
        [
            vmem((8, long), F32), vmem((long, 8), F32), vmem((long, 8), F32), vmem((long, 16), BF16),
            vmem((128, full), F32), vmem((384, full), BF16), vmem((3, 384, 32), BF16),
            vmem((128, chans), F32), vmem((384, chans + 128), BF16),
            vmem((long + 32, chans + 128), F32), vmem((long + 32, chans + 128), F32),
            vmem((long, chans), BF16), vmem((long, chans), BF16),
            vmem((5, chans), F32), vmem((6, RP, chans), F32), vmem((128, 128), F32), vmem((long, 384), BF16),
            vmem((PLANES, padded, chans), F32), vmem((PLANES, padded, chans), F32), pltpu.SemaphoreType.DMA((4,)),
        ],
        FORWARD_MIB, seqs // 2,
    )
    emb = pltpu.with_memory_space_constraint(emb, pltpu.HBM)
    other = lax.ppermute(inner, "blk", [(0, 1), (1, 0)])
    prob, coef = call(
        score_kernel, "scores",
        [lengths, lang_ids], [look, conv_w, score_w],
        [whole(seqs, 8 * PLANES, 128), whole(5, full), whole(groups, full)],
        [shape((seqs, 48, 128), F32), shape((seqs, 32, 128), F32)],
        [whole(seqs, 48, 128), whole(seqs, 32, 128)], [], 16, 1,
    )
    other, prob, coef = lax.optimization_barrier((other, prob, coef))
    total = -(-VP * (chans // 128) // 32) * 32
    keep, send = call(
        backward_kernel, "backward",
        [half, lengths, lang_ids, core.reshape(1)],
        [id_rows, planes, table, conv_w, score_w, emb, prob, coef, inner, other],
        [
            whole(seqs, 8, long), by_two(6, rows, chans), whole(vocab, full), whole(5, full), whole(groups, full),
            pl.BlockSpec(memory_space=pltpu.HBM), whole(seqs, 48, 128), whole(seqs, 32, 128),
            whole(seqs, 32, 128), whole(seqs, 32, 128),
        ],
        [shape((total // 2, 128), F32)] * 2,
        [whole(total // 2, 128)] * 2,
        [
            vmem((128, chans), F32), vmem((384, chans), BF16), vmem((128, 128), F32), vmem((128, 128), F32),
            vmem((chans // 128, long + 8, 128), F32), vmem((384, 128), F32), vmem((VP, chans), F32),
            vmem((5, 8, chans), F32), vmem((total, 128), F32), vmem((5, chans), F32), vmem((groups, chans), F32),
            vmem((6, RP, chans), F32),
            vmem((long, chans + 128), BF16), vmem((long, chans + 128), BF16),
            vmem((long, chans), BF16), vmem((long, chans), BF16),
            vmem((44, RP, 128), F32), vmem((44, RP, 128), F32),
            vmem((128, 128), F32), vmem((128, 128), F32), vmem((8, chans), F32), vmem((8, chans), F32),
            vmem((8, chans), F32), vmem((8, chans), F32), vmem((VP, long), BF16),
            vmem((44, 16, 128), BF16), pltpu.SemaphoreType.DMA((2,)),
        ],
        BACKWARD_MIB, seqs // 2,
    )

    def swap(x, step, odd_step):
        return lax.ppermute(x, "seq", [(i, i ^ (odd_step if i % 2 else step)) for i in range(seq_size)])

    def pooled_two(first, before):
        held = [] if first == 0 else [before]
        return pl.pallas_call(
            functools.partial(pooled_kernel, first),
            in_specs=[pl.BlockSpec(memory_space=pltpu.HBM)] * len(held)
            + [pl.BlockSpec(memory_space=pltpu.VMEM), pl.BlockSpec(memory_space=pltpu.HBM)],
            out_specs=pl.BlockSpec(memory_space=pltpu.HBM),
            scratch_shapes=[
                vmem((26, RP, 128), F32), vmem((2, chans // 128, PLANES, padded, 128), F32),
                vmem((6, padded, 128), F32), vmem((2, 6, rows, chans), BF16),
                vmem((32, 16, 128), BF16), vmem((128, 128), F32),
                pltpu.SemaphoreType.DMA((2 * (chans // 128) + 2,)),
            ],
            out_shape=pltpu.HBM((seqs, 6, rows, chans), BF16),
            input_output_aliases={0: 0} if held else {},
            compiler_params=pltpu.CompilerParams(vmem_limit_bytes=POOLED_MIB * 1024 * 1024),
            name="pooled",
        )(*held, coef, pltpu.with_memory_space_constraint(conv, pltpu.HBM))

    keep, conv = lax.optimization_barrier((keep, conv))
    mine = keep + swap(send, 1, 1)
    quarter = total // 4
    held = lax.dynamic_slice_in_dim(mine, near * quarter, quarter, 0)
    sent = lax.dynamic_slice_in_dim(mine, (1 - near) * quarter, quarter, 0)
    pooled = pooled_two(0, None)
    got, pooled = lax.optimization_barrier((swap(sent, 4, 2), pooled))
    held = held + got
    even, odd = [2, 8], [8, 4]
    step = 16
    while step < seq_size:
        even, odd, step = even + [step], odd + [step], step * 2
    for k, (step, odd_step) in enumerate(zip(even, odd)):
        got = swap(held, step, odd_step)
        if k == 0:
            for first in range(2, seqs, 2):
                pooled = pooled_two(first, pooled)
        elif k == 1:
            pooled = pooled.transpose(0, 2, 1, 3).reshape(seqs, half_rows, chans)
        if k < 2:
            got, pooled = lax.optimization_barrier((got, pooled))
        held = held + got
    mine = jnp.concatenate([held, swap(held, 4, 2)], axis=0)
    other = swap(mine, 1, 1)

    place = jnp.stack([core, near, near_other, seq])
    arrays = [mine, other, table, table_m, table_v, conv_w, conv_m, conv_v, score_w, score_m, score_v]
    outs = []
    for count in (vocab, 5):
        outs += [shape((count, 1, chans), F32)] * 3
    outs += [shape((1, groups, chans), F32)] * 3
    updated = call(
        update_kernel, "update",
        [half, place, owners], arrays, [whole(*x.shape) for x in arrays],
        outs, [whole(*x.shape) for x in outs], [vmem((total, 128), F32)], UPDATE_MIB, 1,
    )
    updated = [jnp.transpose(x, (1, 0, 2)) if k < 6 else x for k, x in enumerate(updated)]
    return (pooled, *updated)


def solution(mesh):
    row, split, copied = P("seq"), P(None, "blk"), P()
    return jax.shard_map(
        functools.partial(local, mesh.shape["seq"]),
        mesh=mesh,
        in_specs=(P("seq", None), row, row, copied, copied, copied, copied, P("seq", None, "blk"))
        + (split,) * 6,
        out_specs=(P("seq", None, "blk"),) * 10,
        check_vma=False,
    )
```

```python
import functools

import jax
import jax.numpy as jnp
from jax import lax
from jax.experimental import pallas as pl
from jax.experimental.pallas import tpu as pltpu
from jax.sharding import PartitionSpec as P

STEP_NUMBER = 5
F32, BF16 = jnp.float32, jnp.bfloat16
PLANES = 12
RP = 96
NO_ID = 511.0
VP = 272
FORWARD_MIB, POOLED_MIB, BACKWARD_MIB, UPDATE_MIB = 32, 16, 32, 16
NN = (((1,), (0,)), ((), ()))
NT = (((1,), (1,)), ((), ()))


def dot(a, b, dims=NN):
    return lax.dot_general(a, b, dims, preferred_element_type=F32)


def iota(shape, dim):
    return lax.broadcasted_iota(jnp.int32, shape, dim)


def split3(x):
    high = x.astype(BF16)
    rest = x - high.astype(F32)
    mid = rest.astype(BF16)
    return high, mid, (rest - mid.astype(F32)).astype(BF16)


def pick_row(x, index):
    return jnp.sum(jnp.where(iota(x.shape, 0) == index, x, 0.0), axis=0, keepdims=True)


def half_lanes(half_ref, chans):
    return pl.ds(pl.multiple_of(half_ref[0] * chans, 128), chans)


def load_table(table_ref, lanes, tail_ref, tab_ref, count):
    vocab = table_ref.shape[0]
    whole = vocab // 128 * 128
    tab_ref[:whole, :count] = table_ref[:whole, lanes].astype(BF16)
    tail_ref[...] = jnp.zeros(tail_ref.shape, F32)
    tail_ref[: vocab - whole, :] = table_ref[whole:, lanes]
    tab_ref[whole:, :count] = tail_ref[...].astype(BF16)


def blocks(x):
    two = [x[2 * p] + x[2 * p + 1] for p in range(6)]
    three = [two[0] + x[2], x[3] + two[2], two[3] + x[8], x[9] + two[5]]
    four = [two[0] + two[1], two[2] + two[3], two[4] + two[5]]
    return [x, two, three, four]


def live_planes(length):
    place = PLANES * iota((1, 128), 1)
    return [jnp.where(place + m < length, 1.0, 0.0).astype(F32) for m in range(PLANES)]


def inverse_counts(live):
    return [[1.0 / jnp.maximum(c, 1.0) for c in side] for side in blocks(live)]


def after_lane(x):
    return jnp.where(iota(x.shape, 1) == 127, 0.0, pltpu.roll(x, 127, 1))


def before_lane(x):
    return jnp.where(iota(x.shape, 1) == 0, 0.0, pltpu.roll(x, 1, 1))


def coefficients(weights):
    one, two, three, four = weights
    rows = [one[m] + two[m // 2 * 2] + two[m // 2 * 2 + 1] for m in range(PLANES)]
    rows += [four[2 * p] + four[2 * p + 1] for p in range(6)]
    for h in (0, 6):
        rows += [three[h] + three[h + 1], three[h + 2], three[h + 3], three[h + 4] + three[h + 5]]
    return rows


def convolved(w, e, behind, live):
    out = []
    for m in range(PLANES):
        value = w[4] + w[0] * e[m]
        for k in range(1, 4):
            value = value + w[k] * (e[m - k] if m >= k else behind[m - k + PLANES])
        out.append(jnp.where(live[m], value, 0.0))
    return out


def pair_terms(sums):
    terms = [(m, m // 2, sums[0][m]) for m in range(PLANES)]
    terms += [(12 + p, p, sums[3][p // 2]) for p in range(6)]
    for h in range(2):
        for k, (p, j) in enumerate(((0, 0), (1, 0), (1, 1), (2, 1))):
            terms.append((18 + 4 * h + k, 3 * h + p, sums[2][2 * h + j]))
    return terms


THIRD = [18, 18, 19, 20, 21, 21, 22, 22, 23, 24, 25, 25]


def forward_kernel(
    half_ref, len_ref, lang_ref, ids_ref, cot_ref, table_ref, convw_ref, score_ref,
    emb_out, conv_out, look_out, inner_out, rows_out,
    xs, cs, idcol, tail, tab_all, looks, tail_half, tab, emb_a, emb_b, low_a, low_b, extras,
    conv_half, cotf, turned, hots, conv_a, conv_b, sems,
):
    n = pl.program_id(0)
    seqs, slot = ids_ref.shape
    rows, chans = cot_ref.shape[2:]
    long = PLANES * RP
    mine = half_lanes(half_ref, chans)
    embs, lows = (emb_a, emb_b), (low_a, low_b)
    convs = (conv_a, conv_b)

    def send(q, k):
        return pltpu.make_async_copy(lows[k], emb_out.at[q], sems.at[k])

    def send_conv(q, k):
        return pltpu.make_async_copy(convs[k], conv_out.at[q], sems.at[2 + k])

    def look_up(q, u):
        emb = embs[u]
        tab[:, chans:] = extras[q]
        lane = iota((128, 128), 1).astype(F32)
        for at in range(0, long, 128):
            ids = jnp.broadcast_to(rows_out[q, 0:1, at : at + 128], (128, 128)).T
            for k in range(3):
                hots[at : at + 128, 128 * k : 128 * (k + 1)] = jnp.where(ids == lane + 128.0 * k, 1.0, 0.0).astype(BF16)
        found = dot(hots[...], tab[...])
        for c in range(chans // 128 + 1):
            emb[c, :long, :] = found[:, 128 * c : 128 * (c + 1)]
        lows[u][...] = found[:, :chans].astype(BF16)
        for m in range(PLANES):
            x = emb[chans // 128, RP * m : RP * m + 128, :24].T
            look_out[q, 8 * m : 8 * m + 8, :] = x[0:8] + x[8:16] + x[16:24]

    def convolve(q, u):
        emb = embs[u]
        length = len_ref[q]
        for p in range(6):
            cotf[p, :rows, :] = cot_ref[u, p].astype(F32)
        place = PLANES * iota((8, 128), 0)
        lane = iota((8, 128), 1)
        bits = [(lane >> k) % 2 == 1 for k in range(5)]
        for r in range(0, rows, 8):
            live = [place < length - (m + PLANES * r) for m in range(PLANES)]
            inner = [0.0] * 26
            for c in range(chans // 128):
                lanes = slice(128 * c, 128 * (c + 1))
                w = [conv_half[k : k + 1, lanes] for k in range(5)]
                e = [emb[c, RP * m + r : RP * m + r + 8, :] for m in range(PLANES)]
                behind = {m: emb[c, RP * m - 1 + r : RP * m + 7 + r, :] for m in (9, 10, 11)}
                conv = convolved(w, e, behind, live)
                for m in range(PLANES):
                    convs[u][m, r : r + 8, lanes] = conv[m]
                for k, p, x in pair_terms(blocks(conv)):
                    inner[k] = inner[k] + cotf[p, r : r + 8, lanes] * x
            level = [jnp.broadcast_to(jnp.sum(x, axis=1, keepdims=True), (8, 128)) for x in inner]
            for bit in bits:
                level.append(level[-1])
                level = [jnp.where(bit, b, a) for a, b in zip(level[0:-1:2], level[1::2])]
            turned[r : r + 8, :] = level[0]
        inner_out[q] = turned[...].T[:32]

    @pl.when(n == 0)
    def _():
        xs[...] = jnp.full(xs.shape, NO_ID, F32)
        xs[:seqs, :slot] = ids_ref[...].astype(F32)
        for i in range(xs.shape[1] // 128):
            cs[128 * i : 128 * (i + 1), :] = xs[:, 128 * i : 128 * (i + 1)].T
        idcol[...] = jnp.full(idcol.shape, NO_ID, F32)
        for m in range(PLANES):
            idcol[RP * m : RP * m + rows, :] = cs[pl.ds(m, rows, stride=PLANES), :]
        rows_out[...] = jnp.zeros(rows_out.shape, F32)
        for i in range(long // 128):
            flipped = idcol[128 * i : 128 * (i + 1), :].T
            for k in range(seqs):
                rows_out[k, 0:1, 128 * i : 128 * (i + 1)] = flipped[k : k + 1, :]
        load_table(table_ref, mine, tail_half, tab, chans)
        load_table(table_ref, slice(None), tail, tab_all, table_ref.shape[1])
        scores = score_ref[...]
        mixed = jnp.concatenate([convw_ref[k : k + 1, :] * scores for k in range(4)], axis=0)
        mixed = jnp.concatenate(list(split3(mixed)) + [jnp.zeros(mixed.shape, BF16)], axis=0)
        got = dot(tab_all[...], mixed, NT)
        got = got + pltpu.roll(got, 96, 1) + pltpu.roll(got, 64, 1)
        looks[...] = jnp.zeros(looks.shape, BF16)
        for k, part in enumerate(split3(got[:, :32])):
            looks[:, 32 * k : 32 * (k + 1)] = part
        sub, lane = iota((128, 128), 0), iota((128, 128), 1)
        for q in range(seqs):
            here = (sub % 8 == lang_ref[q]) & (lane == sub // 32 * 8 + sub % 32 // 8) & (sub < 96)
            extras[q] = dot(looks[...], jnp.where(here, 1.0, 0.0).astype(BF16)).astype(BF16)
        conv_half[...] = convw_ref[:, mine]
        turned[...] = jnp.zeros(turned.shape, F32)
        cotf[...] = jnp.zeros(cotf.shape, F32)
        for emb in embs:
            emb[:, long:, :] = jnp.zeros((emb.shape[0], emb.shape[1] - long, 128), F32)

    for u in range(2):
        q = 2 * n + u

        @pl.when(n > 0)
        def _():
            send(0, u).wait()
            send_conv(0, u).wait()

        look_up(q, u)
        send(q, u).start()
        convolve(q, u)
        send_conv(q, u).start()

    @pl.when(n == pl.num_programs(0) - 1)
    def _():
        for k in range(2):
            send(0, k).wait()
            send_conv(0, k).wait()


def score_kernel(len_ref, lang_ref, look_ref, convw_ref, score_ref, prob_out, coef_out):
    bias = jnp.sum(convw_ref[4:5, :] * score_ref[...], axis=1, keepdims=True)
    bias = jnp.broadcast_to(bias, (score_ref.shape[0], 128))
    for q in range(look_ref.shape[0]):
        look = [look_ref[q, 8 * m : 8 * m + 8, :] for m in range(PLANES)]
        ahead = {m: before_lane(look[m]) for m in (9, 10, 11)}
        live = live_planes(len_ref[q])
        inverse = inverse_counts(live)
        base = pick_row(bias, lang_ref[q])
        score = []
        for m in range(PLANES):
            value = base
            for k in range(4):
                x = look[m - k] if m >= k else ahead[m - k + PLANES]
                value = value + x[k : k + 1, :]
            score.append(jnp.where(live[m] > 0, value, 0.0))
        means = [[t * c for t, c in zip(side, inv)] for side, inv in zip(blocks(score), inverse)]
        weights = [[], [], [], []]
        for m in range(PLANES):
            own = [means[b][m // (b + 1)] for b in range(4)]
            top = functools.reduce(jnp.maximum, own)
            grown = [jnp.exp(x - top) for x in own]
            scale = 1.0 / functools.reduce(jnp.add, grown)
            for b in range(4):
                prob = grown[b] * scale
                prob_out[q, PLANES * b + m : PLANES * b + m + 1, :] = prob
                weights[b].append(0.5 * live[m] * prob * inverse[b][m // (b + 1)])
        coef_out[q, 24:32, :] = jnp.zeros((8, 128), F32)
        for k, row in enumerate(coefficients(weights)):
            coef_out[q, k : k + 1, :] = row


def spread_masks(keep_ref):
    lane = iota((16, 128), 1)
    for j in range(keep_ref.shape[0]):
        keep_ref[j] = jnp.where(lane % 64 == j, 1.0, 0.0).astype(BF16)


def spread_columns(both, keep_ref, cols_ref, columns):
    count = both.shape[0] // 16
    both = both.reshape(count, 16, 128)
    wide = [(both * keep_ref[j][None]).reshape(16 * count, 128) for j in columns]
    got = dot(jnp.concatenate(wide, axis=0), jnp.ones((128, 128), BF16))
    for k, j in enumerate(columns):
        cols_ref[j] = got[16 * count * k : 16 * count * (k + 1)]


def pooled_kernel(first, *refs):
    if first:
        refs = refs[1:]
    coef_ref, conv_ref, pooled_out, cols, conv, poolf, low, keep, both, sems = refs
    padded, chans = conv_ref.shape[2:]
    rows = pooled_out.shape[2]
    chunks = chans // 128
    fetches = []
    for u in range(2):
        for c in range(chunks):
            source = conv_ref.at[first + u, :, :, pl.ds(128 * c, 128)]
            fetches.append(pltpu.make_async_copy(source, conv.at[u, c], sems.at[chunks * u + c]))
            fetches[-1].start()
    sends = []
    spread_masks(keep)
    both[...] = jnp.zeros(both.shape, F32)
    for u in range(2):
        high = coef_ref[first + u].astype(BF16).astype(F32)
        both[0:32, :] = high
        both[64:96, :] = coef_ref[first + u] - high
        across = both[...].T[:RP].astype(BF16)
        for k in range(0, 26, 13):
            spread_columns(across, keep, cols, range(k, k + 13))
        for c in range(chunks):
            fetches[chunks * u + c].wait()
            for r in range(0, padded, 8):
                pooled = [0.0] * 6
                for k, p, x in pair_terms(blocks([conv[u, c, m, r : r + 8, :] for m in range(PLANES)])):
                    pooled[p] = pooled[p] + cols[k, r : r + 8, :] * x
                for p in range(6):
                    poolf[p, r : r + 8, :] = pooled[p]
            for p in range(6):
                low[u, p, :, 128 * c : 128 * (c + 1)] = poolf[p, :rows, :].astype(BF16)
        sends.append(pltpu.make_async_copy(low.at[u], pooled_out.at[first + u], sems.at[2 * chunks + u]))
        sends[-1].start()
    for copy in sends:
        copy.wait()


def backward_kernel(
    half_ref, len_ref, lang_ref, core_ref, rows_ref, cot_ref, table_ref, convw_ref, score_ref,
    emb_ref, prob_ref, coef_ref, inner_ref, other_ref,
    keep_out, send_out,
    tail, tab, pulls, mixed, grad, hist, acc, taps_acc, flat, conv_half, score_half, cotf,
    gemb, low_a, low_b, cols, across, totals, keep, sems,
):
    n = pl.program_id(0)
    seqs = len_ref.shape[0]
    rows, chans = cot_ref.shape[2:]
    groups = score_ref.shape[0]
    mine = half_lanes(half_ref, chans)
    padded = (rows + 7) // 8 * 8
    lows = (low_a, low_b)
    long = PLANES * RP

    def fetch(q, k):
        return pltpu.make_async_copy(emb_ref.at[q], lows[k], sems.at[k])

    def to_table():
        sub = iota((VP, long), 0).astype(F32)
        hot = [jnp.where(rows_ref[q, 0:1, :] == sub, 1.0, 0.0).astype(BF16) for q in range(seqs)]
        got = dot(jnp.concatenate(hot, axis=1), gemb[...])
        acc[...] = got[:, :chans]
        hist[:VP, :] = got[:, chans:]
        counts = hist[...].T
        counts = counts[: 4 * seqs] + counts[64 : 64 + 4 * seqs]
        from_table = dot(jnp.concatenate(split3(counts), axis=0), tab[...])
        from_table = from_table[: 4 * seqs] + from_table[4 * seqs : 8 * seqs] + from_table[8 * seqs :]
        group = iota((groups, chans), 0)
        total = 0.0
        for q in range(seqs):
            part = conv_half[4:5, :] * totals[q, 0:1, :]
            for j in range(4):
                part = part + conv_half[j : j + 1, :] * from_table[4 * q + j : 4 * q + j + 1, :]
            total = total + jnp.where(group == lang_ref[q], part, 0.0)
        acc[VP - groups : VP, :] += total

    def prepare(q):
        both = inner_ref[q] + other_ref[q]
        live = live_planes(len_ref[q])
        inverse = inverse_counts(live)
        row = lambda j: both[j : j + 1, :]
        pull = [[], [], [], []]
        for m in range(PLANES):
            p = m // 2
            dots = [row(m), row(2 * p) + row(2 * p + 1), row(THIRD[m]), row(12 + p)]
            prob = [prob_ref[q, PLANES * b + m : PLANES * b + m + 1, :] for b in range(4)]
            inv = [inverse[b][m // (b + 1)] for b in range(4)]
            inner = [0.5 * jnp.where(live[m] > 0, d, 0.0) * c for d, c in zip(dots, inv)]
            mean = functools.reduce(jnp.add, [x * y for x, y in zip(prob, inner)])
            for b in range(4):
                pull[b].append(prob[b] * (inner[b] - mean) * inv[b])
        sums = [blocks(pull[b])[b] for b in range(4)]
        pull = [live[m] * (sums[0][m] + sums[1][m // 2] + sums[2][m // 3] + sums[3][m // 4]) for m in range(PLANES)]
        whole = jnp.sum(functools.reduce(jnp.add, pull), axis=1, keepdims=True)
        totals[q] = jnp.broadcast_to(whole, totals.shape[1:])
        high = coef_ref[q].astype(BF16).astype(F32)
        mixed[q, 0:32, :] = high
        mixed[q, 64:96, :] = coef_ref[q] - high
        for m, x in enumerate(pull + [after_lane(x) for x in pull[:3]]):
            high = x.astype(BF16).astype(F32)
            pulls[q, m : m + 1, :] = high
            pulls[q, 64 + m : 65 + m, :] = x - high
            if m < PLANES:
                mixed[q, 32 + m : 33 + m, :] = high
                mixed[q, 96 + m : 97 + m, :] = x - high
        turned = pulls[q].T
        lane = iota((RP, 128), 1)
        for m in range(PLANES):
            x = turned if (4 * q - m) % 128 == 0 else pltpu.roll(turned, (4 * q - m) % 128, 1)
            x = jnp.where(lane % 64 // 4 == q, x[:RP], 0.0)
            gemb[long * q + RP * m : long * q + RP * (m + 1), chans:] = x.astype(BF16)
        across[q] = mixed[q].T[:RP].astype(BF16)

    def gradients(q, u):
        length = len_ref[q]
        score = pick_row(score_half[...], lang_ref[q])
        for p in range(6):
            cotf[p, :rows, :] = cot_ref[u, p].astype(F32)
        columns = [*range(26), *range(32, 44)]
        for r in range(0, rows, 8):
            if r % 16 == 0:
                spread_columns(across[q, r : r + 16, :], keep, cols.at[:, r : r + 16, :], columns)
            for c in range(chans // 128):
                lanes = slice(128 * c, 128 * (c + 1))
                cot = [cotf[p, r : r + 8, lanes] for p in range(6)]
                times = lambda j, p: cols[j, r : r + 8, :] * cot[p]
                four = [times(12 + 2 * j, 2 * j) + times(13 + 2 * j, 2 * j + 1) for j in range(3)]
                three = []
                for h in range(2):
                    three.append(times(18 + 4 * h, 3 * h) + times(19 + 4 * h, 3 * h + 1))
                    three.append(times(20 + 4 * h, 3 * h + 1) + times(21 + 4 * h, 3 * h + 2))
                for m in range(PLANES):
                    value = times(m, m // 2) + four[m // 4] + three[m // 3]
                    value = value + cols[32 + m, r : r + 8, :] * score[:, lanes]
                    grad[c, RP * m + r : RP * m + r + 8, :] = value
        end = length // PLANES
        for m in range(PLANES):
            for c in range(chans // 128):
                at = pl.ds(RP * m + end, 1)
                grad[c, at, :] = jnp.where(PLANES * end + m < length, grad[c, at, :], 0.0)

    def weight_gradients(q, u):
        low = lows[u]
        base = pl.multiple_of(q * long, 128)
        for c in range(chans // 128):
            lanes = slice(128 * c, 128 * (c + 1))
            w = [conv_half[k : k + 1, lanes] for k in range(4)]
            tap = [0.0] * 5
            for r in range(0, padded, 16):
                count = min(16, padded - r)
                g = [grad[c, RP * m + r : RP * m + r + count, :] for m in range(PLANES)]
                g += [grad[c, RP * m + r + 1 : RP * m + r + 1 + count, :] for m in range(3)]
                fold = lambda x: x[:8] + x[8:] if count == 16 else x
                for m in range(PLANES):
                    back = w[0] * g[m] + w[1] * g[m + 1] + w[2] * g[m + 2] + w[3] * g[m + 3]
                    if count < 16:
                        back = jnp.concatenate([back, jnp.zeros((16 - count, 128), F32)], axis=0)
                    gemb[pl.ds(base + RP * m + r, 16), lanes] = back.astype(BF16)
                    e = low[RP * m + r : RP * m + r + 16, lanes].astype(F32)[:count]
                    for k in range(4):
                        tap[k] = tap[k] + fold(e * g[m + k])
                    tap[4] = tap[4] + fold(g[m])
            for k in range(5):
                taps_acc[k, :, lanes] += tap[k]

    @pl.when(n == 0)
    def _():
        fetch(0, 0).start()
        load_table(table_ref, mine, tail, tab, chans)
        cotf[...] = jnp.zeros(cotf.shape, F32)
        pulls[...] = jnp.zeros(pulls.shape, F32)
        mixed[...] = jnp.zeros(mixed.shape, F32)
        for m in range(PLANES):
            grad[:, RP * m + rows : RP * (m + 1), :] = jnp.zeros((chans // 128, RP - rows, 128), F32)
        grad[:, PLANES * RP :, :] = jnp.zeros((chans // 128, 8, 128), F32)
        taps_acc[...] = jnp.zeros(taps_acc.shape, F32)
        hist[...] = jnp.zeros(hist.shape, F32)
        conv_half[...] = convw_ref[:, mine]
        score_half[...] = score_ref[:, mine]
        spread_masks(keep)
        for q in range(seqs):
            prepare(q)

    for u in range(2):
        q = 2 * n + u
        later = jnp.minimum(q + 1, seqs - 1)
        fetch(q, u).wait()

        @pl.when(q + 1 < seqs)
        def _():
            fetch(later, 1 - u).start()

        gradients(q, u)

        @pl.when(len_ref[q] > 0)
        def _():
            weight_gradients(q, u)

    @pl.when(n == pl.num_programs(0) - 1)
    def _():
        to_table()
        for k in range(5):
            at = VP - groups - 5 + k
            acc[at : at + 1, :] = jnp.sum(taps_acc[k], axis=0, keepdims=True)
        flat[VP * (chans // 128) :, :] = jnp.zeros((flat.shape[0] - VP * (chans // 128), 128), F32)
        for k in range(chans // 128):
            flat[VP * k : VP * (k + 1), :] = acc[:, 128 * k : 128 * (k + 1)]
        part = keep_out.shape[0]
        own = pl.multiple_of(core_ref[0] * part, 8)
        theirs = pl.multiple_of((1 - core_ref[0]) * part, 8)
        keep_out[...] = flat[pl.ds(own, part), :]
        send_out[...] = flat[pl.ds(theirs, part), :]


def adamw(weight, grad, moment, second, rate):
    new_m = 0.9 * moment + 0.1 * grad
    new_v = 0.999 * second + 0.001 * grad * grad
    m_hat = new_m / (1.0 - 0.9**STEP_NUMBER)
    v_hat = new_v / (1.0 - 0.999**STEP_NUMBER)
    new_w = weight - rate * (m_hat / (jnp.sqrt(v_hat) + 1e-08) + 0.01 * weight)
    return new_m, new_v, new_w


def update_kernel(half_ref, place_ref, owner_ref, mine_ref, other_ref, *refs):
    ins, outs, flat = refs[:9], refs[9:18], refs[18]
    core, seq = place_ref[0], place_ref[3]
    rows = mine_ref.shape[0] // 2
    for side, near, ref in ((core, place_ref[1], mine_ref), (1 - core, place_ref[2], other_ref)):
        for k in range(2):
            piece = near if k == 0 else 1 - near
            flat[pl.ds(pl.multiple_of((2 * side + piece) * rows, 8), rows), :] = ref[k * rows : (k + 1) * rows, :]
    vocab, chans = ins[1].shape
    groups = ins[6].shape[0]
    spans = ((0, vocab), (VP - groups - 5, 5), (VP - groups, groups))
    for t, rate in enumerate((0.5, 0.3, 0.05)):
        first, count = spans[t]
        owned = owner_ref[t] == seq
        for k in range(chans // 128):
            lanes = slice(128 * k, 128 * (k + 1))
            weight = ins[3 * t][:, pl.ds(pl.multiple_of(half_ref[0] * chans + 128 * k, 128), 128)]
            grad = flat[VP * k + first : VP * k + first + count, :]
            new = adamw(weight, grad, ins[3 * t + 1][:, lanes], ins[3 * t + 2][:, lanes], rate)
            for q in range(3):
                out = outs[3 * t + q]
                value = jnp.where(owned, new[q], 0.0)
                if count == groups:
                    out[0, :, lanes] = value
                else:
                    out[:, 0, lanes] = value


def local(
    seq_size, byte_ids, lengths, lang_ids, owners, table, conv_w, score_w, cotangent,
    table_m, table_v, conv_m, conv_v, score_m, score_v,
):
    seqs, slot = byte_ids.shape
    vocab, full = table.shape
    half_rows, chans = cotangent.shape[1:]
    groups = score_w.shape[0]
    rows = slot // PLANES
    assert rows * PLANES == slot and rows <= RP - 2 and seqs % 2 == 0 and seqs <= 16
    half = lax.axis_index("blk").astype(jnp.int32).reshape(1)
    seq = lax.axis_index("seq").astype(jnp.int32)
    core, far_bit, near_bit = seq % 2, (seq // 4) % 2, (seq // 2) % 2
    near = jnp.where(core == 0, far_bit, near_bit)
    near_other = jnp.where(core == 0, near_bit, far_bit)
    vmem = pltpu.VMEM
    shape = jax.ShapeDtypeStruct
    whole = lambda *dims: pl.BlockSpec(dims, lambda s, *_: (0,) * len(dims))
    by_two = lambda *dims: pl.BlockSpec((2,) + dims, lambda s, *_: (s,) + (0,) * len(dims))
    by_seq = lambda *dims: pl.BlockSpec((1,) + dims, lambda s, *_: (s,) + (0,) * len(dims))

    def call(kernel, name, scalars, arrays, in_specs, outs, out_specs, scratch, mib, steps):
        return pl.pallas_call(
            kernel,
            grid_spec=pltpu.PrefetchScalarGridSpec(
                num_scalar_prefetch=len(scalars), grid=(steps,),
                in_specs=in_specs, out_specs=out_specs, scratch_shapes=scratch,
            ),
            out_shape=outs,
            compiler_params=pltpu.CompilerParams(
                vmem_limit_bytes=mib * 1024 * 1024, dimension_semantics=("arbitrary",)
            ),
            name=name,
        )(*scalars, *arrays)

    planes = cotangent.reshape(seqs, rows, 6, chans).transpose(0, 2, 1, 3)
    long = PLANES * RP
    padded = (rows + 7) // 8 * 8
    emb, conv, look, inner, id_rows = call(
        forward_kernel, "forward",
        [half, lengths, lang_ids], [byte_ids, planes, table, conv_w, score_w],
        [whole(seqs, slot), by_two(6, rows, chans), whole(vocab, full), whole(5, full), whole(groups, full)],
        [
            pltpu.HBM((seqs, long, chans), BF16), pltpu.HBM((seqs, PLANES, padded, chans), F32),
            shape((seqs, 8 * PLANES, 128), F32),
            shape((seqs, 32, 128), F32), shape((seqs, 8, long), F32),
        ],
        [
            pl.BlockSpec(memory_space=pltpu.HBM), pl.BlockSpec(memory_space=pltpu.HBM),
            whole(seqs, 8 * PLANES, 128), whole(seqs, 32, 128), whole(seqs, 8, long),
        ],
        [
            vmem((8, long), F32), vmem((long, 8), F32), vmem((long, 8), F32),
            vmem((128, full), F32), vmem((384, full), BF16), vmem((384, 128), BF16),
            vmem((128, chans), F32), vmem((384, chans + 128), BF16),
            vmem((chans // 128 + 1, long + 32, 128), F32), vmem((chans // 128 + 1, long + 32, 128), F32),
            vmem((long, chans), BF16), vmem((long, chans), BF16), vmem((seqs, 384, 128), BF16),
            vmem((5, chans), F32), vmem((6, RP, chans), F32), vmem((128, 128), F32), vmem((long, 384), BF16),
            vmem((PLANES, padded, chans), F32), vmem((PLANES, padded, chans), F32),
            pltpu.SemaphoreType.DMA((4,)),
        ],
        FORWARD_MIB, seqs // 2,
    )
    emb = pltpu.with_memory_space_constraint(emb, pltpu.HBM)
    other = lax.ppermute(inner, "blk", [(0, 1), (1, 0)])
    prob, coef = call(
        score_kernel, "scores",
        [lengths, lang_ids], [look, conv_w, score_w],
        [whole(seqs, 8 * PLANES, 128), whole(5, full), whole(groups, full)],
        [shape((seqs, 48, 128), F32), shape((seqs, 32, 128), F32)],
        [whole(seqs, 48, 128), whole(seqs, 32, 128)], [], 16, 1,
    )
    other, prob, coef = lax.optimization_barrier((other, prob, coef))
    total = -(-VP * (chans // 128) // 32) * 32
    keep, send = call(
        backward_kernel, "backward",
        [half, lengths, lang_ids, core.reshape(1)],
        [id_rows, planes, table, conv_w, score_w, emb, prob, coef, inner, other],
        [
            whole(seqs, 8, long), by_two(6, rows, chans), whole(vocab, full), whole(5, full), whole(groups, full),
            pl.BlockSpec(memory_space=pltpu.HBM), whole(seqs, 48, 128), whole(seqs, 32, 128),
            whole(seqs, 32, 128), whole(seqs, 32, 128),
        ],
        [shape((total // 2, 128), F32)] * 2,
        [whole(total // 2, 128)] * 2,
        [
            vmem((128, chans), F32), vmem((384, chans), BF16),
            vmem((seqs, 128, 128), F32), vmem((seqs, 128, 128), F32),
            vmem((chans // 128, long + 8, 128), F32), vmem((384, 128), F32), vmem((VP, chans), F32),
            vmem((5, 8, chans), F32), vmem((total, 128), F32), vmem((5, chans), F32), vmem((groups, chans), F32),
            vmem((6, RP, chans), F32),
            vmem((seqs * long, chans + 128), BF16), vmem((long, chans), BF16), vmem((long, chans), BF16),
            vmem((44, RP, 128), F32), vmem((seqs, RP, 128), BF16), vmem((seqs, 8, chans), F32),
            vmem((44, 16, 128), BF16), pltpu.SemaphoreType.DMA((2,)),
        ],
        BACKWARD_MIB, seqs // 2,
    )

    def swap(x, step, odd_step):
        return lax.ppermute(x, "seq", [(i, i ^ (odd_step if i % 2 else step)) for i in range(seq_size)])

    def pooled_two(first, before):
        held = [] if first == 0 else [before]
        return pl.pallas_call(
            functools.partial(pooled_kernel, first),
            in_specs=[pl.BlockSpec(memory_space=pltpu.HBM)] * len(held)
            + [pl.BlockSpec(memory_space=pltpu.VMEM), pl.BlockSpec(memory_space=pltpu.HBM)],
            out_specs=pl.BlockSpec(memory_space=pltpu.HBM),
            scratch_shapes=[
                vmem((26, RP, 128), F32), vmem((2, chans // 128, PLANES, padded, 128), F32),
                vmem((6, padded, 128), F32), vmem((2, 6, rows, chans), BF16),
                vmem((32, 16, 128), BF16), vmem((128, 128), F32),
                pltpu.SemaphoreType.DMA((2 * (chans // 128) + 2,)),
            ],
            out_shape=pltpu.HBM((seqs, 6, rows, chans), BF16),
            input_output_aliases={0: 0} if held else {},
            compiler_params=pltpu.CompilerParams(vmem_limit_bytes=POOLED_MIB * 1024 * 1024),
            name="pooled",
        )(*held, coef, pltpu.with_memory_space_constraint(conv, pltpu.HBM))

    keep, conv = lax.optimization_barrier((keep, conv))
    mine = keep + swap(send, 1, 1)
    quarter = total // 4
    held = lax.dynamic_slice_in_dim(mine, near * quarter, quarter, 0)
    sent = lax.dynamic_slice_in_dim(mine, (1 - near) * quarter, quarter, 0)
    pooled = pooled_two(0, None)
    got, pooled = lax.optimization_barrier((swap(sent, 4, 2), pooled))
    held = held + got
    even, odd = [2, 8], [8, 4]
    step = 16
    while step < seq_size:
        even, odd, step = even + [step], odd + [step], step * 2
    for k, (step, odd_step) in enumerate(zip(even, odd)):
        got = swap(held, step, odd_step)
        if k == 0:
            for first in range(2, seqs, 2):
                pooled = pooled_two(first, pooled)
        elif k == 1:
            pooled = pooled.transpose(0, 2, 1, 3).reshape(seqs, half_rows, chans)
        if k < 2:
            got, pooled = lax.optimization_barrier((got, pooled))
        held = held + got
    mine = jnp.concatenate([held, swap(held, 4, 2)], axis=0)
    other = swap(mine, 1, 1)

    place = jnp.stack([core, near, near_other, seq])
    arrays = [mine, other, table, table_m, table_v, conv_w, conv_m, conv_v, score_w, score_m, score_v]
    outs = []
    for count in (vocab, 5):
        outs += [shape((count, 1, chans), F32)] * 3
    outs += [shape((1, groups, chans), F32)] * 3
    updated = call(
        update_kernel, "update",
        [half, place, owners], arrays, [whole(*x.shape) for x in arrays],
        outs, [whole(*x.shape) for x in outs], [vmem((total, 128), F32)], UPDATE_MIB, 1,
    )
    updated = [jnp.transpose(x, (1, 0, 2)) if k < 6 else x for k, x in enumerate(updated)]
    return (pooled, *updated)


def solution(mesh):
    row, split, copied = P("seq"), P(None, "blk"), P()
    return jax.shard_map(
        functools.partial(local, mesh.shape["seq"]),
        mesh=mesh,
        in_specs=(P("seq", None), row, row, copied, copied, copied, copied, P("seq", None, "blk"))
        + (split,) * 6,
        out_specs=(P("seq", None, "blk"),) * 10,
        check_vma=False,
    )
```

```python
import functools

import jax
import jax.numpy as jnp
from jax import lax
from jax.experimental import pallas as pl
from jax.experimental.pallas import tpu as pltpu
from jax.sharding import PartitionSpec as P

STEP_NUMBER = 5
F32, BF16 = jnp.float32, jnp.bfloat16
PLANES = 12
RP = 96
NO_ID = 511.0
VP = 272
FORWARD_MIB, POOLED_MIB, BACKWARD_MIB, UPDATE_MIB = 32, 16, 32, 16
NN = (((1,), (0,)), ((), ()))
NT = (((1,), (1,)), ((), ()))


def dot(a, b, dims=NN):
    return lax.dot_general(a, b, dims, preferred_element_type=F32)


def iota(shape, dim):
    return lax.broadcasted_iota(jnp.int32, shape, dim)


def split3(x):
    high = x.astype(BF16)
    rest = x - high.astype(F32)
    mid = rest.astype(BF16)
    return high, mid, (rest - mid.astype(F32)).astype(BF16)


def pick_row(x, index):
    return jnp.sum(jnp.where(iota(x.shape, 0) == index, x, 0.0), axis=0, keepdims=True)


def half_lanes(half_ref, chans):
    return pl.ds(pl.multiple_of(half_ref[0] * chans, 128), chans)


def load_table(table_ref, lanes, tail_ref, tab_ref, count):
    vocab = table_ref.shape[0]
    whole = vocab // 128 * 128
    tab_ref[:whole, :count] = table_ref[:whole, lanes].astype(BF16)
    tail_ref[...] = jnp.zeros(tail_ref.shape, F32)
    tail_ref[: vocab - whole, :] = table_ref[whole:, lanes]
    tab_ref[whole:, :count] = tail_ref[...].astype(BF16)


def blocks(x):
    two = [x[2 * p] + x[2 * p + 1] for p in range(6)]
    three = [two[0] + x[2], x[3] + two[2], two[3] + x[8], x[9] + two[5]]
    four = [two[0] + two[1], two[2] + two[3], two[4] + two[5]]
    return [x, two, three, four]


def live_planes(length):
    place = PLANES * iota((1, 128), 1)
    return [jnp.where(place + m < length, 1.0, 0.0).astype(F32) for m in range(PLANES)]


def inverse_counts(live):
    return [[1.0 / jnp.maximum(c, 1.0) for c in side] for side in blocks(live)]


def after_lane(x):
    return jnp.where(iota(x.shape, 1) == 127, 0.0, pltpu.roll(x, 127, 1))


def before_lane(x):
    return jnp.where(iota(x.shape, 1) == 0, 0.0, pltpu.roll(x, 1, 1))


def coefficients(weights):
    one, two, three, four = weights
    rows = [one[m] + two[m // 2 * 2] + two[m // 2 * 2 + 1] for m in range(PLANES)]
    rows += [four[2 * p] + four[2 * p + 1] for p in range(6)]
    for h in (0, 6):
        rows += [three[h] + three[h + 1], three[h + 2], three[h + 3], three[h + 4] + three[h + 5]]
    return rows


def convolved(w, e, behind, live):
    out = []
    for m in range(PLANES):
        value = w[4] + w[0] * e[m]
        for k in range(1, 4):
            value = value + w[k] * (e[m - k] if m >= k else behind[m - k + PLANES])
        out.append(jnp.where(live[m], value, 0.0))
    return out


def pair_terms(sums):
    terms = [(m, m // 2, sums[0][m]) for m in range(PLANES)]
    terms += [(12 + p, p, sums[3][p // 2]) for p in range(6)]
    for h in range(2):
        for k, (p, j) in enumerate(((0, 0), (1, 0), (1, 1), (2, 1))):
            terms.append((18 + 4 * h + k, 3 * h + p, sums[2][2 * h + j]))
    return terms


THIRD = [18, 18, 19, 20, 21, 21, 22, 22, 23, 24, 25, 25]


def forward_kernel(
    half_ref, len_ref, lang_ref, ids_ref, cot_ref, table_ref, convw_ref, score_ref,
    emb_out, conv_out, look_out, inner_out, rows_out,
    xs, cs, idcol, tail, tab_all, looks, tail_half, tab, emb_a, emb_b, low_a, low_b, extras,
    conv_half, cotf, turned, hots, conv_a, conv_b, sems,
):
    n = pl.program_id(0)
    seqs, slot = ids_ref.shape
    rows, chans = cot_ref.shape[2:]
    long = PLANES * RP
    mine = half_lanes(half_ref, chans)
    embs, lows = (emb_a, emb_b), (low_a, low_b)
    convs = (conv_a, conv_b)

    def send(q, k):
        return pltpu.make_async_copy(lows[k], emb_out.at[q], sems.at[k])

    def send_conv(q, k):
        return pltpu.make_async_copy(convs[k], conv_out.at[q], sems.at[2 + k])

    def look_up(q, u):
        emb = embs[u]
        tab[:, chans:] = extras[q]
        lane = iota((128, 128), 1).astype(F32)
        for at in range(0, long, 128):
            ids = jnp.broadcast_to(rows_out[q, 0:1, at : at + 128], (128, 128)).T
            for k in range(3):
                hots[at : at + 128, 128 * k : 128 * (k + 1)] = jnp.where(ids == lane + 128.0 * k, 1.0, 0.0).astype(BF16)
        found = dot(hots[...], tab[...])
        for c in range(chans // 128 + 1):
            emb[c, :long, :] = found[:, 128 * c : 128 * (c + 1)]
        lows[u][...] = found[:, :chans].astype(BF16)
        for m in range(PLANES):
            x = emb[chans // 128, RP * m : RP * m + 128, :24].T
            look_out[q, 8 * m : 8 * m + 8, :] = x[0:8] + x[8:16] + x[16:24]

    def convolve(q, u):
        emb = embs[u]
        length = len_ref[q]
        for p in range(6):
            cotf[p, :rows, :] = cot_ref[u, p].astype(F32)
        place = PLANES * iota((8, 128), 0)
        lane = iota((8, 128), 1)
        bits = [(lane >> k) % 2 == 1 for k in range(5)]
        for r in range(0, rows, 8):
            live = [place < length - (m + PLANES * r) for m in range(PLANES)]
            inner = [0.0] * 26
            for c in range(chans // 128):
                lanes = slice(128 * c, 128 * (c + 1))
                w = [conv_half[k : k + 1, lanes] for k in range(5)]
                e = [emb[c, RP * m + r : RP * m + r + 8, :] for m in range(PLANES)]
                behind = {m: emb[c, RP * m - 1 + r : RP * m + 7 + r, :] for m in (9, 10, 11)}
                conv = convolved(w, e, behind, live)
                for m in range(PLANES):
                    convs[u][m, r : r + 8, lanes] = conv[m]
                for k, p, x in pair_terms(blocks(conv)):
                    inner[k] = inner[k] + cotf[p, r : r + 8, lanes] * x
            level = [jnp.broadcast_to(jnp.sum(x, axis=1, keepdims=True), (8, 128)) for x in inner]
            for bit in bits:
                level.append(level[-1])
                level = [jnp.where(bit, b, a) for a, b in zip(level[0:-1:2], level[1::2])]
            turned[r : r + 8, :] = level[0]
        inner_out[q] = turned[...].T[:32]

    @pl.when(n == 0)
    def _():
        xs[...] = jnp.full(xs.shape, NO_ID, F32)
        xs[:seqs, :slot] = ids_ref[...].astype(F32)
        for i in range(xs.shape[1] // 128):
            cs[128 * i : 128 * (i + 1), :] = xs[:, 128 * i : 128 * (i + 1)].T
        idcol[...] = jnp.full(idcol.shape, NO_ID, F32)
        for m in range(PLANES):
            idcol[RP * m : RP * m + rows, :] = cs[pl.ds(m, rows, stride=PLANES), :]
        rows_out[...] = jnp.zeros(rows_out.shape, F32)
        for i in range(long // 128):
            flipped = idcol[128 * i : 128 * (i + 1), :].T
            for k in range(seqs):
                rows_out[k, 0:1, 128 * i : 128 * (i + 1)] = flipped[k : k + 1, :]
        load_table(table_ref, mine, tail_half, tab, chans)
        load_table(table_ref, slice(None), tail, tab_all, table_ref.shape[1])
        scores = score_ref[...]
        mixed = jnp.concatenate([convw_ref[k : k + 1, :] * scores for k in range(4)], axis=0)
        mixed = jnp.concatenate(list(split3(mixed)) + [jnp.zeros(mixed.shape, BF16)], axis=0)
        got = dot(tab_all[...], mixed, NT)
        got = got + pltpu.roll(got, 96, 1) + pltpu.roll(got, 64, 1)
        looks[...] = jnp.zeros(looks.shape, BF16)
        for k, part in enumerate(split3(got[:, :32])):
            looks[:, 32 * k : 32 * (k + 1)] = part
        sub, lane = iota((128, 128), 0), iota((128, 128), 1)
        for q in range(seqs):
            here = (sub % 8 == lang_ref[q]) & (lane == sub // 32 * 8 + sub % 32 // 8) & (sub < 96)
            extras[q] = dot(looks[...], jnp.where(here, 1.0, 0.0).astype(BF16)).astype(BF16)
        conv_half[...] = convw_ref[:, mine]
        turned[...] = jnp.zeros(turned.shape, F32)
        cotf[...] = jnp.zeros(cotf.shape, F32)
        for emb in embs:
            emb[:, long:, :] = jnp.zeros((emb.shape[0], emb.shape[1] - long, 128), F32)

    for u in range(2):
        q = 2 * n + u

        @pl.when(n > 0)
        def _():
            send(0, u).wait()
            send_conv(0, u).wait()

        look_up(q, u)
        send(q, u).start()
        convolve(q, u)
        send_conv(q, u).start()

    @pl.when(n == pl.num_programs(0) - 1)
    def _():
        for k in range(2):
            send(0, k).wait()
            send_conv(0, k).wait()


def score_kernel(len_ref, lang_ref, look_ref, convw_ref, score_ref, prob_out, coef_out):
    bias = jnp.sum(convw_ref[4:5, :] * score_ref[...], axis=1, keepdims=True)
    bias = jnp.broadcast_to(bias, (score_ref.shape[0], 128))
    for q in range(look_ref.shape[0]):
        look = [look_ref[q, 8 * m : 8 * m + 8, :] for m in range(PLANES)]
        ahead = {m: before_lane(look[m]) for m in (9, 10, 11)}
        live = live_planes(len_ref[q])
        inverse = inverse_counts(live)
        base = pick_row(bias, lang_ref[q])
        score = []
        for m in range(PLANES):
            value = base
            for k in range(4):
                x = look[m - k] if m >= k else ahead[m - k + PLANES]
                value = value + x[k : k + 1, :]
            score.append(jnp.where(live[m] > 0, value, 0.0))
        means = [[t * c for t, c in zip(side, inv)] for side, inv in zip(blocks(score), inverse)]
        weights = [[], [], [], []]
        for m in range(PLANES):
            own = [means[b][m // (b + 1)] for b in range(4)]
            top = functools.reduce(jnp.maximum, own)
            grown = [jnp.exp(x - top) for x in own]
            scale = 1.0 / functools.reduce(jnp.add, grown)
            for b in range(4):
                prob = grown[b] * scale
                prob_out[q, PLANES * b + m : PLANES * b + m + 1, :] = prob
                weights[b].append(0.5 * live[m] * prob * inverse[b][m // (b + 1)])
        coef_out[q, 24:32, :] = jnp.zeros((8, 128), F32)
        for k, row in enumerate(coefficients(weights)):
            coef_out[q, k : k + 1, :] = row


def spread_masks(keep_ref):
    lane = iota((16, 128), 1)
    for j in range(keep_ref.shape[0]):
        keep_ref[j] = jnp.where(lane % 64 == j, 1.0, 0.0).astype(BF16)


def spread_columns(both, keep_ref, cols_ref, columns):
    count = both.shape[0] // 16
    both = both.reshape(count, 16, 128)
    wide = [(both * keep_ref[j][None]).reshape(16 * count, 128) for j in columns]
    got = dot(jnp.concatenate(wide, axis=0), jnp.ones((128, 128), BF16))
    for k, j in enumerate(columns):
        cols_ref[j] = got[16 * count * k : 16 * count * (k + 1)]


def pooled_kernel(first, *refs):
    if first:
        refs = refs[1:]
    coef_ref, conv_ref, pooled_out, cols, conv, poolf, low, keep, both, sems = refs
    padded, chans = conv_ref.shape[2:]
    rows = pooled_out.shape[2]
    chunks = chans // 128
    fetches = []
    for u in range(2):
        for c in range(chunks):
            source = conv_ref.at[first + u, :, :, pl.ds(128 * c, 128)]
            fetches.append(pltpu.make_async_copy(source, conv.at[u, c], sems.at[chunks * u + c]))
            fetches[-1].start()
    sends = []
    spread_masks(keep)
    both[...] = jnp.zeros(both.shape, F32)
    for u in range(2):
        high = coef_ref[first + u].astype(BF16).astype(F32)
        both[0:32, :] = high
        both[64:96, :] = coef_ref[first + u] - high
        across = both[...].T[:RP].astype(BF16)
        for k in range(0, 26, 13):
            spread_columns(across, keep, cols, range(k, k + 13))
        for c in range(chunks):
            fetches[chunks * u + c].wait()
            for r in range(0, padded, 8):
                pooled = [0.0] * 6
                for k, p, x in pair_terms(blocks([conv[u, c, m, r : r + 8, :] for m in range(PLANES)])):
                    pooled[p] = pooled[p] + cols[k, r : r + 8, :] * x
                for p in range(6):
                    poolf[p, r : r + 8, :] = pooled[p]
            for p in range(6):
                low[u, p, :, 128 * c : 128 * (c + 1)] = poolf[p, :rows, :].astype(BF16)
        sends.append(pltpu.make_async_copy(low.at[u], pooled_out.at[first + u], sems.at[2 * chunks + u]))
        sends[-1].start()
    for copy in sends:
        copy.wait()


def backward_kernel(
    half_ref, len_ref, lang_ref, core_ref, rows_ref, cot_ref, table_ref, convw_ref, score_ref,
    emb_ref, prob_ref, coef_ref, inner_ref, other_ref,
    keep_out, send_out,
    tail, tab, pulls, mixed, grad, hist, acc, taps_acc, flat, conv_half, score_half, cotf,
    gemb, low, cols, across, totals, keep, sems,
):
    n = pl.program_id(0)
    seqs = len_ref.shape[0]
    rows, chans = cot_ref.shape[2:]
    groups = score_ref.shape[0]
    mine = half_lanes(half_ref, chans)
    padded = (rows + 7) // 8 * 8
    long = PLANES * RP

    def fetch(q):
        return pltpu.make_async_copy(emb_ref.at[q], low.at[q], sems.at[q])

    def to_table():
        sub = iota((VP, long), 0).astype(F32)
        hot = [jnp.where(rows_ref[q, 0:1, :] == sub, 1.0, 0.0).astype(BF16) for q in range(seqs)]
        got = dot(jnp.concatenate(hot, axis=1), gemb[...])
        acc[...] = got[:, :chans]
        hist[:VP, :] = got[:, chans:]
        counts = hist[...].T
        counts = counts[: 4 * seqs] + counts[64 : 64 + 4 * seqs]
        from_table = dot(jnp.concatenate(split3(counts), axis=0), tab[...])
        from_table = from_table[: 4 * seqs] + from_table[4 * seqs : 8 * seqs] + from_table[8 * seqs :]
        group = iota((groups, chans), 0)
        total = 0.0
        for q in range(seqs):
            part = conv_half[4:5, :] * totals[q, 0:1, :]
            for j in range(4):
                part = part + conv_half[j : j + 1, :] * from_table[4 * q + j : 4 * q + j + 1, :]
            total = total + jnp.where(group == lang_ref[q], part, 0.0)
        acc[VP - groups : VP, :] += total

    def prepare(q):
        both = inner_ref[q] + other_ref[q]
        live = live_planes(len_ref[q])
        inverse = inverse_counts(live)
        row = lambda j: both[j : j + 1, :]
        pull = [[], [], [], []]
        for m in range(PLANES):
            p = m // 2
            dots = [row(m), row(2 * p) + row(2 * p + 1), row(THIRD[m]), row(12 + p)]
            prob = [prob_ref[q, PLANES * b + m : PLANES * b + m + 1, :] for b in range(4)]
            inv = [inverse[b][m // (b + 1)] for b in range(4)]
            inner = [0.5 * jnp.where(live[m] > 0, d, 0.0) * c for d, c in zip(dots, inv)]
            mean = functools.reduce(jnp.add, [x * y for x, y in zip(prob, inner)])
            for b in range(4):
                pull[b].append(prob[b] * (inner[b] - mean) * inv[b])
        sums = [blocks(pull[b])[b] for b in range(4)]
        pull = [live[m] * (sums[0][m] + sums[1][m // 2] + sums[2][m // 3] + sums[3][m // 4]) for m in range(PLANES)]
        whole = jnp.sum(functools.reduce(jnp.add, pull), axis=1, keepdims=True)
        totals[q] = jnp.broadcast_to(whole, totals.shape[1:])
        high = coef_ref[q].astype(BF16).astype(F32)
        mixed[q, 0:32, :] = high
        mixed[q, 64:96, :] = coef_ref[q] - high
        for m, x in enumerate(pull + [after_lane(x) for x in pull[:3]]):
            high = x.astype(BF16).astype(F32)
            pulls[q, m : m + 1, :] = high
            pulls[q, 64 + m : 65 + m, :] = x - high
            if m < PLANES:
                mixed[q, 32 + m : 33 + m, :] = high
                mixed[q, 96 + m : 97 + m, :] = x - high
        turned = pulls[q].T
        lane = iota((RP, 128), 1)
        for m in range(PLANES):
            x = turned if (4 * q - m) % 128 == 0 else pltpu.roll(turned, (4 * q - m) % 128, 1)
            x = jnp.where(lane % 64 // 4 == q, x[:RP], 0.0)
            gemb[long * q + RP * m : long * q + RP * (m + 1), chans:] = x.astype(BF16)
        across[q] = mixed[q].T[:RP].astype(BF16)

    def gradients(q, u):
        length = len_ref[q]
        score = pick_row(score_half[...], lang_ref[q])
        for p in range(6):
            cotf[p, :rows, :] = cot_ref[u, p].astype(F32)
        columns = [*range(26), *range(32, 44)]
        for r in range(0, rows, 8):
            if r % 16 == 0:
                spread_columns(across[q, r : r + 16, :], keep, cols.at[:, r : r + 16, :], columns)
            for c in range(chans // 128):
                lanes = slice(128 * c, 128 * (c + 1))
                cot = [cotf[p, r : r + 8, lanes] for p in range(6)]
                times = lambda j, p: cols[j, r : r + 8, :] * cot[p]
                four = [times(12 + 2 * j, 2 * j) + times(13 + 2 * j, 2 * j + 1) for j in range(3)]
                three = []
                for h in range(2):
                    three.append(times(18 + 4 * h, 3 * h) + times(19 + 4 * h, 3 * h + 1))
                    three.append(times(20 + 4 * h, 3 * h + 1) + times(21 + 4 * h, 3 * h + 2))
                for m in range(PLANES):
                    value = times(m, m // 2) + four[m // 4] + three[m // 3]
                    value = value + cols[32 + m, r : r + 8, :] * score[:, lanes]
                    grad[c, RP * m + r : RP * m + r + 8, :] = value
        end = length // PLANES
        for m in range(PLANES):
            for c in range(chans // 128):
                at = pl.ds(RP * m + end, 1)
                grad[c, at, :] = jnp.where(PLANES * end + m < length, grad[c, at, :], 0.0)

    def weight_gradients(q, u):
        base = pl.multiple_of(q * long, 128)
        for c in range(chans // 128):
            lanes = slice(128 * c, 128 * (c + 1))
            w = [conv_half[k : k + 1, lanes] for k in range(4)]
            tap = [0.0] * 5
            for r in range(0, padded, 16):
                count = min(16, padded - r)
                g = [grad[c, RP * m + r : RP * m + r + count, :] for m in range(PLANES)]
                g += [grad[c, RP * m + r + 1 : RP * m + r + 1 + count, :] for m in range(3)]
                fold = lambda x: x[:8] + x[8:] if count == 16 else x
                for m in range(PLANES):
                    back = w[0] * g[m] + w[1] * g[m + 1] + w[2] * g[m + 2] + w[3] * g[m + 3]
                    if count < 16:
                        back = jnp.concatenate([back, jnp.zeros((16 - count, 128), F32)], axis=0)
                    gemb[pl.ds(base + RP * m + r, 16), lanes] = back.astype(BF16)
                    e = low[q, RP * m + r : RP * m + r + 16, lanes].astype(F32)[:count]
                    for k in range(4):
                        tap[k] = tap[k] + fold(e * g[m + k])
                    tap[4] = tap[4] + fold(g[m])
            for k in range(5):
                taps_acc[k, :, lanes] += tap[k]

    @pl.when(n == 0)
    def _():
        for q in range(seqs):
            fetch(q).start()
        load_table(table_ref, mine, tail, tab, chans)
        cotf[...] = jnp.zeros(cotf.shape, F32)
        pulls[...] = jnp.zeros(pulls.shape, F32)
        mixed[...] = jnp.zeros(mixed.shape, F32)
        for m in range(PLANES):
            grad[:, RP * m + rows : RP * (m + 1), :] = jnp.zeros((chans // 128, RP - rows, 128), F32)
        grad[:, PLANES * RP :, :] = jnp.zeros((chans // 128, 8, 128), F32)
        taps_acc[...] = jnp.zeros(taps_acc.shape, F32)
        hist[...] = jnp.zeros(hist.shape, F32)
        conv_half[...] = convw_ref[:, mine]
        score_half[...] = score_ref[:, mine]
        spread_masks(keep)
        for q in range(seqs):
            prepare(q)

    for u in range(2):
        q = 2 * n + u
        gradients(q, u)
        fetch(q).wait()

        @pl.when(len_ref[q] > 0)
        def _():
            weight_gradients(q, u)

    @pl.when(n == pl.num_programs(0) - 1)
    def _():
        to_table()
        for k in range(5):
            at = VP - groups - 5 + k
            acc[at : at + 1, :] = jnp.sum(taps_acc[k], axis=0, keepdims=True)
        flat[VP * (chans // 128) :, :] = jnp.zeros((flat.shape[0] - VP * (chans // 128), 128), F32)
        for k in range(chans // 128):
            flat[VP * k : VP * (k + 1), :] = acc[:, 128 * k : 128 * (k + 1)]
        part = keep_out.shape[0]
        own = pl.multiple_of(core_ref[0] * part, 8)
        theirs = pl.multiple_of((1 - core_ref[0]) * part, 8)
        keep_out[...] = flat[pl.ds(own, part), :]
        send_out[...] = flat[pl.ds(theirs, part), :]


def adamw(weight, grad, moment, second, rate):
    new_m = 0.9 * moment + 0.1 * grad
    new_v = 0.999 * second + 0.001 * grad * grad
    m_hat = new_m / (1.0 - 0.9**STEP_NUMBER)
    v_hat = new_v / (1.0 - 0.999**STEP_NUMBER)
    new_w = weight - rate * (m_hat / (jnp.sqrt(v_hat) + 1e-08) + 0.01 * weight)
    return new_m, new_v, new_w


def update_kernel(half_ref, place_ref, owner_ref, mine_ref, other_ref, *refs):
    ins, outs, flat = refs[:9], refs[9:18], refs[18]
    core, seq = place_ref[0], place_ref[3]
    rows = mine_ref.shape[0] // 2
    for side, near, ref in ((core, place_ref[1], mine_ref), (1 - core, place_ref[2], other_ref)):
        for k in range(2):
            piece = near if k == 0 else 1 - near
            flat[pl.ds(pl.multiple_of((2 * side + piece) * rows, 8), rows), :] = ref[k * rows : (k + 1) * rows, :]
    vocab, chans = ins[1].shape
    groups = ins[6].shape[0]
    spans = ((0, vocab), (VP - groups - 5, 5), (VP - groups, groups))
    for t, rate in enumerate((0.5, 0.3, 0.05)):
        first, count = spans[t]
        owned = owner_ref[t] == seq
        for k in range(chans // 128):
            lanes = slice(128 * k, 128 * (k + 1))
            weight = ins[3 * t][:, pl.ds(pl.multiple_of(half_ref[0] * chans + 128 * k, 128), 128)]
            grad = flat[VP * k + first : VP * k + first + count, :]
            new = adamw(weight, grad, ins[3 * t + 1][:, lanes], ins[3 * t + 2][:, lanes], rate)
            for q in range(3):
                out = outs[3 * t + q]
                value = jnp.where(owned, new[q], 0.0)
                if count == groups:
                    out[0, :, lanes] = value
                else:
                    out[:, 0, lanes] = value


def local(
    seq_size, byte_ids, lengths, lang_ids, owners, table, conv_w, score_w, cotangent,
    table_m, table_v, conv_m, conv_v, score_m, score_v,
):
    seqs, slot = byte_ids.shape
    vocab, full = table.shape
    half_rows, chans = cotangent.shape[1:]
    groups = score_w.shape[0]
    rows = slot // PLANES
    assert rows * PLANES == slot and rows <= RP - 2 and seqs % 2 == 0 and seqs <= 16
    half = lax.axis_index("blk").astype(jnp.int32).reshape(1)
    seq = lax.axis_index("seq").astype(jnp.int32)
    core, far_bit, near_bit = seq % 2, (seq // 4) % 2, (seq // 2) % 2
    near = jnp.where(core == 0, far_bit, near_bit)
    near_other = jnp.where(core == 0, near_bit, far_bit)
    vmem = pltpu.VMEM
    shape = jax.ShapeDtypeStruct
    whole = lambda *dims: pl.BlockSpec(dims, lambda s, *_: (0,) * len(dims))
    by_two = lambda *dims: pl.BlockSpec((2,) + dims, lambda s, *_: (s,) + (0,) * len(dims))
    by_seq = lambda *dims: pl.BlockSpec((1,) + dims, lambda s, *_: (s,) + (0,) * len(dims))

    def call(kernel, name, scalars, arrays, in_specs, outs, out_specs, scratch, mib, steps):
        return pl.pallas_call(
            kernel,
            grid_spec=pltpu.PrefetchScalarGridSpec(
                num_scalar_prefetch=len(scalars), grid=(steps,),
                in_specs=in_specs, out_specs=out_specs, scratch_shapes=scratch,
            ),
            out_shape=outs,
            compiler_params=pltpu.CompilerParams(
                vmem_limit_bytes=mib * 1024 * 1024, dimension_semantics=("arbitrary",)
            ),
            name=name,
        )(*scalars, *arrays)

    planes = cotangent.reshape(seqs, rows, 6, chans).transpose(0, 2, 1, 3)
    long = PLANES * RP
    padded = (rows + 7) // 8 * 8
    emb, conv, look, inner, id_rows = call(
        forward_kernel, "forward",
        [half, lengths, lang_ids], [byte_ids, planes, table, conv_w, score_w],
        [whole(seqs, slot), by_two(6, rows, chans), whole(vocab, full), whole(5, full), whole(groups, full)],
        [
            pltpu.HBM((seqs, long, chans), BF16), pltpu.HBM((seqs, PLANES, padded, chans), F32),
            shape((seqs, 8 * PLANES, 128), F32),
            shape((seqs, 32, 128), F32), shape((seqs, 8, long), F32),
        ],
        [
            pl.BlockSpec(memory_space=pltpu.HBM), pl.BlockSpec(memory_space=pltpu.HBM),
            whole(seqs, 8 * PLANES, 128), whole(seqs, 32, 128), whole(seqs, 8, long),
        ],
        [
            vmem((8, long), F32), vmem((long, 8), F32), vmem((long, 8), F32),
            vmem((128, full), F32), vmem((384, full), BF16), vmem((384, 128), BF16),
            vmem((128, chans), F32), vmem((384, chans + 128), BF16),
            vmem((chans // 128 + 1, long + 32, 128), F32), vmem((chans // 128 + 1, long + 32, 128), F32),
            vmem((long, chans), BF16), vmem((long, chans), BF16), vmem((seqs, 384, 128), BF16),
            vmem((5, chans), F32), vmem((6, RP, chans), F32), vmem((128, 128), F32), vmem((long, 384), BF16),
            vmem((PLANES, padded, chans), F32), vmem((PLANES, padded, chans), F32),
            pltpu.SemaphoreType.DMA((4,)),
        ],
        FORWARD_MIB, seqs // 2,
    )
    emb = pltpu.with_memory_space_constraint(emb, pltpu.HBM)
    other = lax.ppermute(inner, "blk", [(0, 1), (1, 0)])
    prob, coef = call(
        score_kernel, "scores",
        [lengths, lang_ids], [look, conv_w, score_w],
        [whole(seqs, 8 * PLANES, 128), whole(5, full), whole(groups, full)],
        [shape((seqs, 48, 128), F32), shape((seqs, 32, 128), F32)],
        [whole(seqs, 48, 128), whole(seqs, 32, 128)], [], 16, 1,
    )
    other, prob, coef = lax.optimization_barrier((other, prob, coef))
    total = -(-VP * (chans // 128) // 32) * 32
    keep, send = call(
        backward_kernel, "backward",
        [half, lengths, lang_ids, core.reshape(1)],
        [id_rows, planes, table, conv_w, score_w, emb, prob, coef, inner, other],
        [
            whole(seqs, 8, long), by_two(6, rows, chans), whole(vocab, full), whole(5, full), whole(groups, full),
            pl.BlockSpec(memory_space=pltpu.HBM), whole(seqs, 48, 128), whole(seqs, 32, 128),
            whole(seqs, 32, 128), whole(seqs, 32, 128),
        ],
        [shape((total // 2, 128), F32)] * 2,
        [whole(total // 2, 128)] * 2,
        [
            vmem((128, chans), F32), vmem((384, chans), BF16),
            vmem((seqs, 128, 128), F32), vmem((seqs, 128, 128), F32),
            vmem((chans // 128, long + 8, 128), F32), vmem((384, 128), F32), vmem((VP, chans), F32),
            vmem((5, 8, chans), F32), vmem((total, 128), F32), vmem((5, chans), F32), vmem((groups, chans), F32),
            vmem((6, RP, chans), F32),
            vmem((seqs * long, chans + 128), BF16), vmem((seqs, long, chans), BF16),
            vmem((44, RP, 128), F32), vmem((seqs, RP, 128), BF16), vmem((seqs, 8, chans), F32),
            vmem((44, 16, 128), BF16), pltpu.SemaphoreType.DMA((seqs,)),
        ],
        BACKWARD_MIB, seqs // 2,
    )

    def swap(x, step, odd_step):
        return lax.ppermute(x, "seq", [(i, i ^ (odd_step if i % 2 else step)) for i in range(seq_size)])

    def pooled_two(first, before):
        held = [] if first == 0 else [before]
        return pl.pallas_call(
            functools.partial(pooled_kernel, first),
            in_specs=[pl.BlockSpec(memory_space=pltpu.HBM)] * len(held)
            + [pl.BlockSpec(memory_space=pltpu.VMEM), pl.BlockSpec(memory_space=pltpu.HBM)],
            out_specs=pl.BlockSpec(memory_space=pltpu.HBM),
            scratch_shapes=[
                vmem((26, RP, 128), F32), vmem((2, chans // 128, PLANES, padded, 128), F32),
                vmem((6, padded, 128), F32), vmem((2, 6, rows, chans), BF16),
                vmem((32, 16, 128), BF16), vmem((128, 128), F32),
                pltpu.SemaphoreType.DMA((2 * (chans // 128) + 2,)),
            ],
            out_shape=pltpu.HBM((seqs, 6, rows, chans), BF16),
            input_output_aliases={0: 0} if held else {},
            compiler_params=pltpu.CompilerParams(vmem_limit_bytes=POOLED_MIB * 1024 * 1024),
            name="pooled",
        )(*held, coef, pltpu.with_memory_space_constraint(conv, pltpu.HBM))

    keep, conv = lax.optimization_barrier((keep, conv))
    mine = keep + swap(send, 1, 1)
    quarter = total // 4
    held = lax.dynamic_slice_in_dim(mine, near * quarter, quarter, 0)
    sent = lax.dynamic_slice_in_dim(mine, (1 - near) * quarter, quarter, 0)
    pooled = pooled_two(0, None)
    got, pooled = lax.optimization_barrier((swap(sent, 4, 2), pooled))
    held = held + got
    even, odd = [2, 8], [8, 4]
    step = 16
    while step < seq_size:
        even, odd, step = even + [step], odd + [step], step * 2
    for k, (step, odd_step) in enumerate(zip(even, odd)):
        got = swap(held, step, odd_step)
        if k == 0:
            for first in range(2, seqs, 2):
                pooled = pooled_two(first, pooled)
        elif k == 1:
            pooled = pooled.transpose(0, 2, 1, 3).reshape(seqs, half_rows, chans)
        if k < 2:
            got, pooled = lax.optimization_barrier((got, pooled))
        held = held + got
    mine = jnp.concatenate([held, swap(held, 4, 2)], axis=0)
    other = swap(mine, 1, 1)

    place = jnp.stack([core, near, near_other, seq])
    arrays = [mine, other, table, table_m, table_v, conv_w, conv_m, conv_v, score_w, score_m, score_v]
    outs = []
    for count in (vocab, 5):
        outs += [shape((count, 1, chans), F32)] * 3
    outs += [shape((1, groups, chans), F32)] * 3
    updated = call(
        update_kernel, "update",
        [half, place, owners], arrays, [whole(*x.shape) for x in arrays],
        outs, [whole(*x.shape) for x in outs], [vmem((total, 128), F32)], UPDATE_MIB, 1,
    )
    updated = [jnp.transpose(x, (1, 0, 2)) if k < 6 else x for k, x in enumerate(updated)]
    return (pooled, *updated)


def solution(mesh):
    row, split, copied = P("seq"), P(None, "blk"), P()
    return jax.shard_map(
        functools.partial(local, mesh.shape["seq"]),
        mesh=mesh,
        in_specs=(P("seq", None), row, row, copied, copied, copied, copied, P("seq", None, "blk"))
        + (split,) * 6,
        out_specs=(P("seq", None, "blk"),) * 10,
        check_vma=False,
    )
```

```python
import functools

import jax
import jax.numpy as jnp
from jax import lax
from jax.experimental import pallas as pl
from jax.experimental.pallas import tpu as pltpu
from jax.sharding import PartitionSpec as P

STEP_NUMBER = 5
F32, BF16 = jnp.float32, jnp.bfloat16
PLANES = 12
RP = 96
NO_ID = 511.0
VP = 272
FORWARD_MIB, POOLED_MIB, BACKWARD_MIB, UPDATE_MIB = 32, 16, 32, 16
NN = (((1,), (0,)), ((), ()))
NT = (((1,), (1,)), ((), ()))


def dot(a, b, dims=NN):
    return lax.dot_general(a, b, dims, preferred_element_type=F32)


def iota(shape, dim):
    return lax.broadcasted_iota(jnp.int32, shape, dim)


def split3(x):
    high = x.astype(BF16)
    rest = x - high.astype(F32)
    mid = rest.astype(BF16)
    return high, mid, (rest - mid.astype(F32)).astype(BF16)


def pick_row(x, index):
    return jnp.sum(jnp.where(iota(x.shape, 0) == index, x, 0.0), axis=0, keepdims=True)


def half_lanes(half_ref, chans):
    return pl.ds(pl.multiple_of(half_ref[0] * chans, 128), chans)


def load_table(table_ref, lanes, tail_ref, tab_ref, count):
    vocab = table_ref.shape[0]
    whole = vocab // 128 * 128
    tab_ref[:whole, :count] = table_ref[:whole, lanes].astype(BF16)
    tail_ref[...] = jnp.zeros(tail_ref.shape, F32)
    tail_ref[: vocab - whole, :] = table_ref[whole:, lanes]
    tab_ref[whole:, :count] = tail_ref[...].astype(BF16)


def blocks(x):
    two = [x[2 * p] + x[2 * p + 1] for p in range(6)]
    three = [two[0] + x[2], x[3] + two[2], two[3] + x[8], x[9] + two[5]]
    four = [two[0] + two[1], two[2] + two[3], two[4] + two[5]]
    return [x, two, three, four]


def live_planes(length):
    place = PLANES * iota((1, 128), 1)
    return [jnp.where(place + m < length, 1.0, 0.0).astype(F32) for m in range(PLANES)]


def inverse_counts(live):
    return [[1.0 / jnp.maximum(c, 1.0) for c in side] for side in blocks(live)]


def after_lane(x):
    return jnp.where(iota(x.shape, 1) == 127, 0.0, pltpu.roll(x, 127, 1))


def before_lane(x):
    return jnp.where(iota(x.shape, 1) == 0, 0.0, pltpu.roll(x, 1, 1))


def coefficients(weights):
    one, two, three, four = weights
    rows = [one[m] + two[m // 2 * 2] + two[m // 2 * 2 + 1] for m in range(PLANES)]
    rows += [four[2 * p] + four[2 * p + 1] for p in range(6)]
    for h in (0, 6):
        rows += [three[h] + three[h + 1], three[h + 2], three[h + 3], three[h + 4] + three[h + 5]]
    return rows


def convolved(w, e, behind, live):
    out = []
    for m in range(PLANES):
        value = w[4] + w[0] * e[m]
        for k in range(1, 4):
            value = value + w[k] * (e[m - k] if m >= k else behind[m - k + PLANES])
        out.append(jnp.where(live[m], value, 0.0))
    return out


def pair_terms(sums):
    terms = [(m, m // 2, sums[0][m]) for m in range(PLANES)]
    terms += [(12 + p, p, sums[3][p // 2]) for p in range(6)]
    for h in range(2):
        for k, (p, j) in enumerate(((0, 0), (1, 0), (1, 1), (2, 1))):
            terms.append((18 + 4 * h + k, 3 * h + p, sums[2][2 * h + j]))
    return terms


THIRD = [18, 18, 19, 20, 21, 21, 22, 22, 23, 24, 25, 25]


def forward_kernel(
    half_ref, len_ref, lang_ref, ids_ref, cot_ref, table_ref, convw_ref, score_ref,
    emb_out, conv_out, look_out, inner_out, rows_out,
    xs, cs, idcol, tail, tab_all, looks, tail_half, tab, emb_a, emb_b, low_a, low_b, extras,
    conv_half, cotf, turned, hots, conv_a, conv_b, sems,
):
    n = pl.program_id(0)
    seqs, slot = ids_ref.shape
    rows, chans = cot_ref.shape[2:]
    long = PLANES * RP
    mine = half_lanes(half_ref, chans)
    embs, lows = (emb_a, emb_b), (low_a, low_b)
    convs = (conv_a, conv_b)

    def send(q, k):
        return pltpu.make_async_copy(lows[k], emb_out.at[q], sems.at[k])

    def send_conv(q, k):
        return pltpu.make_async_copy(convs[k], conv_out.at[q], sems.at[2 + k])

    def look_up(q, u):
        emb = embs[u]
        tab[:, chans:] = extras[q]
        lane = iota((128, 128), 1).astype(F32)
        for at in range(0, long, 128):
            ids = jnp.broadcast_to(rows_out[q, 0:1, at : at + 128], (128, 128)).T
            for k in range(3):
                hots[at : at + 128, 128 * k : 128 * (k + 1)] = jnp.where(ids == lane + 128.0 * k, 1.0, 0.0).astype(BF16)
        found = dot(hots[...], tab[...])
        for c in range(chans // 128 + 1):
            emb[c, :long, :] = found[:, 128 * c : 128 * (c + 1)]
        lows[u][...] = found[:, :chans].astype(BF16)
        for m in range(PLANES):
            x = emb[chans // 128, RP * m : RP * m + 128, :24].T
            look_out[q, 8 * m : 8 * m + 8, :] = x[0:8] + x[8:16] + x[16:24]

    def convolve(q, u):
        emb = embs[u]
        length = len_ref[q]
        for p in range(6):
            cotf[p, :rows, :] = cot_ref[u, p].astype(F32)
        place = PLANES * iota((8, 128), 0)
        lane = iota((8, 128), 1)
        bits = [(lane >> k) % 2 == 1 for k in range(5)]
        for r in range(0, rows, 8):
            live = [place < length - (m + PLANES * r) for m in range(PLANES)]
            inner = [0.0] * 26
            for c in range(chans // 128):
                lanes = slice(128 * c, 128 * (c + 1))
                w = [conv_half[k : k + 1, lanes] for k in range(5)]
                e = [emb[c, RP * m + r : RP * m + r + 8, :] for m in range(PLANES)]
                behind = {m: emb[c, RP * m - 1 + r : RP * m + 7 + r, :] for m in (9, 10, 11)}
                conv = convolved(w, e, behind, live)
                for m in range(PLANES):
                    convs[u][m, r : r + 8, lanes] = conv[m]
                for k, p, x in pair_terms(blocks(conv)):
                    inner[k] = inner[k] + cotf[p, r : r + 8, lanes] * x
            level = [jnp.broadcast_to(jnp.sum(x, axis=1, keepdims=True), (8, 128)) for x in inner]
            for bit in bits:
                level.append(level[-1])
                level = [jnp.where(bit, b, a) for a, b in zip(level[0:-1:2], level[1::2])]
            turned[r : r + 8, :] = level[0]
        inner_out[q] = turned[...].T[:32]

    @pl.when(n == 0)
    def _():
        xs[...] = jnp.full(xs.shape, NO_ID, F32)
        xs[:seqs, :slot] = ids_ref[...].astype(F32)
        for i in range(xs.shape[1] // 128):
            cs[128 * i : 128 * (i + 1), :] = xs[:, 128 * i : 128 * (i + 1)].T
        idcol[...] = jnp.full(idcol.shape, NO_ID, F32)
        for m in range(PLANES):
            idcol[RP * m : RP * m + rows, :] = cs[pl.ds(m, rows, stride=PLANES), :]
        rows_out[...] = jnp.zeros(rows_out.shape, F32)
        for i in range(long // 128):
            flipped = idcol[128 * i : 128 * (i + 1), :].T
            for k in range(seqs):
                rows_out[k, 0:1, 128 * i : 128 * (i + 1)] = flipped[k : k + 1, :]
        load_table(table_ref, mine, tail_half, tab, chans)
        load_table(table_ref, slice(None), tail, tab_all, table_ref.shape[1])
        scores = score_ref[...]
        mixed = jnp.concatenate([convw_ref[k : k + 1, :] * scores for k in range(4)], axis=0)
        mixed = jnp.concatenate(list(split3(mixed)) + [jnp.zeros(mixed.shape, BF16)], axis=0)
        got = dot(tab_all[...], mixed, NT)
        got = got + pltpu.roll(got, 96, 1) + pltpu.roll(got, 64, 1)
        looks[...] = jnp.zeros(looks.shape, BF16)
        for k, part in enumerate(split3(got[:, :32])):
            looks[:, 32 * k : 32 * (k + 1)] = part
        sub, lane = iota((128, 128), 0), iota((128, 128), 1)
        for q in range(seqs):
            here = (sub % 8 == lang_ref[q]) & (lane == sub // 32 * 8 + sub % 32 // 8) & (sub < 96)
            extras[q] = dot(looks[...], jnp.where(here, 1.0, 0.0).astype(BF16)).astype(BF16)
        conv_half[...] = convw_ref[:, mine]
        turned[...] = jnp.zeros(turned.shape, F32)
        cotf[...] = jnp.zeros(cotf.shape, F32)
        for emb in embs:
            emb[:, long:, :] = jnp.zeros((emb.shape[0], emb.shape[1] - long, 128), F32)

    for u in range(2):
        q = 2 * n + u

        @pl.when(n > 0)
        def _():
            send(0, u).wait()
            send_conv(0, u).wait()

        look_up(q, u)
        send(q, u).start()
        convolve(q, u)
        send_conv(q, u).start()

    @pl.when(n == pl.num_programs(0) - 1)
    def _():
        for k in range(2):
            send(0, k).wait()
            send_conv(0, k).wait()


def score_kernel(len_ref, lang_ref, look_ref, convw_ref, score_ref, prob_out, coef_out):
    prob_out[...] = jnp.zeros(prob_out.shape, F32)
    bias = jnp.sum(convw_ref[4:5, :] * score_ref[...], axis=1, keepdims=True)
    bias = jnp.broadcast_to(bias, (score_ref.shape[0], 128))
    for q in range(look_ref.shape[0]):
        look = [look_ref[q, 8 * m : 8 * m + 8, :] for m in range(PLANES)]
        ahead = {m: before_lane(look[m]) for m in (9, 10, 11)}
        live = live_planes(len_ref[q])
        inverse = inverse_counts(live)
        base = pick_row(bias, lang_ref[q])
        score = []
        for m in range(PLANES):
            value = base
            for k in range(4):
                x = look[m - k] if m >= k else ahead[m - k + PLANES]
                value = value + x[k : k + 1, :]
            score.append(jnp.where(live[m] > 0, value, 0.0))
        means = [[t * c for t, c in zip(side, inv)] for side, inv in zip(blocks(score), inverse)]
        weights = [[], [], [], []]
        for m in range(PLANES):
            own = [means[b][m // (b + 1)] for b in range(4)]
            top = functools.reduce(jnp.maximum, own)
            grown = [jnp.exp(x - top) for x in own]
            scale = 1.0 / functools.reduce(jnp.add, grown)
            for b in range(4):
                prob = grown[b] * scale
                prob_out[PLANES * b + m, q : q + 1, :] = prob
                weights[b].append(0.5 * live[m] * prob * inverse[b][m // (b + 1)])
        coef_out[q, 24:32, :] = jnp.zeros((8, 128), F32)
        for k, row in enumerate(coefficients(weights)):
            coef_out[q, k : k + 1, :] = row


def spread_masks(keep_ref):
    lane = iota((16, 128), 1)
    for j in range(keep_ref.shape[0]):
        keep_ref[j] = jnp.where(lane % 64 == j, 1.0, 0.0).astype(BF16)


def spread_columns(both, keep_ref, cols_ref, columns):
    count = both.shape[0] // 16
    both = both.reshape(count, 16, 128)
    wide = [(both * keep_ref[j][None]).reshape(16 * count, 128) for j in columns]
    got = dot(jnp.concatenate(wide, axis=0), jnp.ones((128, 128), BF16))
    for k, j in enumerate(columns):
        cols_ref[j] = got[16 * count * k : 16 * count * (k + 1)]


def pooled_kernel(first, *refs):
    if first:
        refs = refs[1:]
    coef_ref, conv_ref, pooled_out, cols, conv, poolf, low, keep, both, sems = refs
    padded, chans = conv_ref.shape[2:]
    rows = pooled_out.shape[2]
    chunks = chans // 128
    fetches = []
    for u in range(2):
        for c in range(chunks):
            source = conv_ref.at[first + u, :, :, pl.ds(128 * c, 128)]
            fetches.append(pltpu.make_async_copy(source, conv.at[u, c], sems.at[chunks * u + c]))
            fetches[-1].start()
    sends = []
    spread_masks(keep)
    both[...] = jnp.zeros(both.shape, F32)
    for u in range(2):
        high = coef_ref[first + u].astype(BF16).astype(F32)
        both[0:32, :] = high
        both[64:96, :] = coef_ref[first + u] - high
        across = both[...].T[:RP].astype(BF16)
        for k in range(0, 26, 13):
            spread_columns(across, keep, cols.at[u], range(k, k + 13))
    for u in range(2):
        for c in range(chunks):
            fetches[chunks * u + c].wait()
            for r in range(0, padded, 8):
                pooled = [0.0] * 6
                for k, p, x in pair_terms(blocks([conv[u, c, m, r : r + 8, :] for m in range(PLANES)])):
                    pooled[p] = pooled[p] + cols[u, k, r : r + 8, :] * x
                for p in range(6):
                    poolf[p, r : r + 8, :] = pooled[p]
            for p in range(6):
                low[u, p, :, 128 * c : 128 * (c + 1)] = poolf[p, :rows, :].astype(BF16)
        sends.append(pltpu.make_async_copy(low.at[u], pooled_out.at[first + u], sems.at[2 * chunks + u]))
        sends[-1].start()
    for copy in sends:
        copy.wait()


def backward_kernel(
    half_ref, len_ref, lang_ref, core_ref, rows_ref, cot_ref, table_ref, convw_ref, score_ref,
    emb_ref, prob_ref, coef_ref, inner_ref, other_ref,
    keep_out, send_out,
    tail, tab, pulls, mixed, grad, hist, acc, taps_acc, flat, conv_half, score_half, cotf,
    gemb, low, cols, across, totals, keep, products, sems,
):
    n = pl.program_id(0)
    seqs = len_ref.shape[0]
    rows, chans = cot_ref.shape[2:]
    groups = score_ref.shape[0]
    mine = half_lanes(half_ref, chans)
    padded = (rows + 7) // 8 * 8
    long = PLANES * RP

    def fetch(q):
        return pltpu.make_async_copy(emb_ref.at[q], low.at[q], sems.at[q])

    def to_table():
        sub = iota((VP, long), 0).astype(F32)
        hot = [jnp.where(rows_ref[q, 0:1, :] == sub, 1.0, 0.0).astype(BF16) for q in range(seqs)]
        got = dot(jnp.concatenate(hot, axis=1), gemb[...])
        acc[...] = got[:, :chans]
        hist[:VP, :] = got[:, chans:]
        counts = hist[...].T
        counts = counts[: 4 * seqs] + counts[64 : 64 + 4 * seqs]
        from_table = dot(jnp.concatenate(split3(counts), axis=0), tab[...])
        from_table = from_table[: 4 * seqs] + from_table[4 * seqs : 8 * seqs] + from_table[8 * seqs :]
        group = iota((groups, chans), 0)
        total = 0.0
        for q in range(seqs):
            part = conv_half[4:5, :] * totals[q, 0:1, :]
            for j in range(4):
                part = part + conv_half[j : j + 1, :] * from_table[4 * q + j : 4 * q + j + 1, :]
            total = total + jnp.where(group == lang_ref[q], part, 0.0)
        acc[VP - groups : VP, :] += total

    def prepare():
        sub, lane = iota((8, 128), 0), iota((8, 128), 1)
        length = jnp.zeros((8, 128), jnp.int32)
        for q in range(seqs):
            both = inner_ref[q] + other_ref[q]
            for j in range(26):
                products[j, q : q + 1, :] = both[j : j + 1, :]
            length = jnp.where(sub == q, len_ref[q], length)
        live = [jnp.where(PLANES * lane + m < length, 1.0, 0.0).astype(F32) for m in range(PLANES)]
        inverse = inverse_counts(live)
        pull = [[], [], [], []]
        for m in range(PLANES):
            p = m // 2
            dots = [products[m], products[2 * p] + products[2 * p + 1], products[THIRD[m]], products[12 + p]]
            prob = [prob_ref[PLANES * b + m] for b in range(4)]
            inv = [inverse[b][m // (b + 1)] for b in range(4)]
            inner = [0.5 * jnp.where(live[m] > 0, d, 0.0) * c for d, c in zip(dots, inv)]
            mean = functools.reduce(jnp.add, [x * y for x, y in zip(prob, inner)])
            for b in range(4):
                pull[b].append(prob[b] * (inner[b] - mean) * inv[b])
        sums = [blocks(pull[b])[b] for b in range(4)]
        pull = [live[m] * (sums[0][m] + sums[1][m // 2] + sums[2][m // 3] + sums[3][m // 4]) for m in range(PLANES)]
        whole = jnp.sum(functools.reduce(jnp.add, pull), axis=1, keepdims=True)
        for m, x in enumerate(pull + [after_lane(x) for x in pull[:3]]):
            high = x.astype(BF16).astype(F32)
            low_part = x - high
            for q in range(seqs):
                pulls[q, m : m + 1, :] = high[q : q + 1, :]
                pulls[q, 64 + m : 65 + m, :] = low_part[q : q + 1, :]
                if m < PLANES:
                    mixed[q, 32 + m : 33 + m, :] = high[q : q + 1, :]
                    mixed[q, 96 + m : 97 + m, :] = low_part[q : q + 1, :]
        lane = iota((RP, 128), 1)
        for q in range(seqs):
            totals[q] = jnp.broadcast_to(whole[q : q + 1, :], totals.shape[1:])
            high = coef_ref[q].astype(BF16).astype(F32)
            mixed[q, 0:32, :] = high
            mixed[q, 64:96, :] = coef_ref[q] - high
            turned = pulls[q].T
            for m in range(PLANES):
                x = turned if (4 * q - m) % 128 == 0 else pltpu.roll(turned, (4 * q - m) % 128, 1)
                x = jnp.where(lane % 64 // 4 == q, x[:RP], 0.0)
                gemb[long * q + RP * m : long * q + RP * (m + 1), chans:] = x.astype(BF16)
            across[q] = mixed[q].T[:RP].astype(BF16)

    def gradients(q, u):
        length = len_ref[q]
        score = pick_row(score_half[...], lang_ref[q])
        for p in range(6):
            cotf[p, :rows, :] = cot_ref[u, p].astype(F32)
        columns = [*range(26), *range(32, 44)]
        for r in range(0, rows, 8):
            if r % 16 == 0:
                spread_columns(across[q, r : r + 16, :], keep, cols.at[:, r : r + 16, :], columns)
            for c in range(chans // 128):
                lanes = slice(128 * c, 128 * (c + 1))
                cot = [cotf[p, r : r + 8, lanes] for p in range(6)]
                times = lambda j, p: cols[j, r : r + 8, :] * cot[p]
                four = [times(12 + 2 * j, 2 * j) + times(13 + 2 * j, 2 * j + 1) for j in range(3)]
                three = []
                for h in range(2):
                    three.append(times(18 + 4 * h, 3 * h) + times(19 + 4 * h, 3 * h + 1))
                    three.append(times(20 + 4 * h, 3 * h + 1) + times(21 + 4 * h, 3 * h + 2))
                for m in range(PLANES):
                    value = times(m, m // 2) + four[m // 4] + three[m // 3]
                    value = value + cols[32 + m, r : r + 8, :] * score[:, lanes]
                    grad[c, RP * m + r : RP * m + r + 8, :] = value
        end = length // PLANES
        for m in range(PLANES):
            for c in range(chans // 128):
                at = pl.ds(RP * m + end, 1)
                grad[c, at, :] = jnp.where(PLANES * end + m < length, grad[c, at, :], 0.0)

    def weight_gradients(q, u):
        base = pl.multiple_of(q * long, 128)
        for c in range(chans // 128):
            lanes = slice(128 * c, 128 * (c + 1))
            w = [conv_half[k : k + 1, lanes] for k in range(4)]
            tap = [0.0] * 5
            for r in range(0, padded, 16):
                count = min(16, padded - r)
                g = [grad[c, RP * m + r : RP * m + r + count, :] for m in range(PLANES)]
                g += [grad[c, RP * m + r + 1 : RP * m + r + 1 + count, :] for m in range(3)]
                fold = lambda x: x[:8] + x[8:] if count == 16 else x
                for m in range(PLANES):
                    back = w[0] * g[m] + w[1] * g[m + 1] + w[2] * g[m + 2] + w[3] * g[m + 3]
                    if count < 16:
                        back = jnp.concatenate([back, jnp.zeros((16 - count, 128), F32)], axis=0)
                    gemb[pl.ds(base + RP * m + r, 16), lanes] = back.astype(BF16)
                    e = low[q, RP * m + r : RP * m + r + 16, lanes].astype(F32)[:count]
                    for k in range(4):
                        tap[k] = tap[k] + fold(e * g[m + k])
                    tap[4] = tap[4] + fold(g[m])
            for k in range(5):
                taps_acc[k, :, lanes] += tap[k]

    @pl.when(n == 0)
    def _():
        for q in range(seqs):
            fetch(q).start()
        load_table(table_ref, mine, tail, tab, chans)
        cotf[...] = jnp.zeros(cotf.shape, F32)
        pulls[...] = jnp.zeros(pulls.shape, F32)
        mixed[...] = jnp.zeros(mixed.shape, F32)
        for m in range(PLANES):
            grad[:, RP * m + rows : RP * (m + 1), :] = jnp.zeros((chans // 128, RP - rows, 128), F32)
        grad[:, PLANES * RP :, :] = jnp.zeros((chans // 128, 8, 128), F32)
        taps_acc[...] = jnp.zeros(taps_acc.shape, F32)
        hist[...] = jnp.zeros(hist.shape, F32)
        conv_half[...] = convw_ref[:, mine]
        score_half[...] = score_ref[:, mine]
        spread_masks(keep)
        products[...] = jnp.zeros(products.shape, F32)
        prepare()

    for u in range(2):
        q = 2 * n + u
        gradients(q, u)
        fetch(q).wait()

        @pl.when(len_ref[q] > 0)
        def _():
            weight_gradients(q, u)

    @pl.when(n == pl.num_programs(0) - 1)
    def _():
        to_table()
        for k in range(5):
            at = VP - groups - 5 + k
            acc[at : at + 1, :] = jnp.sum(taps_acc[k], axis=0, keepdims=True)
        flat[VP * (chans // 128) :, :] = jnp.zeros((flat.shape[0] - VP * (chans // 128), 128), F32)
        for k in range(chans // 128):
            flat[VP * k : VP * (k + 1), :] = acc[:, 128 * k : 128 * (k + 1)]
        part = keep_out.shape[0]
        own = pl.multiple_of(core_ref[0] * part, 8)
        theirs = pl.multiple_of((1 - core_ref[0]) * part, 8)
        keep_out[...] = flat[pl.ds(own, part), :]
        send_out[...] = flat[pl.ds(theirs, part), :]


def adamw(weight, grad, moment, second, rate):
    new_m = 0.9 * moment + 0.1 * grad
    new_v = 0.999 * second + 0.001 * grad * grad
    m_hat = new_m / (1.0 - 0.9**STEP_NUMBER)
    v_hat = new_v / (1.0 - 0.999**STEP_NUMBER)
    new_w = weight - rate * (m_hat / (jnp.sqrt(v_hat) + 1e-08) + 0.01 * weight)
    return new_m, new_v, new_w


def update_kernel(half_ref, place_ref, owner_ref, mine_ref, other_ref, *refs):
    ins, outs, flat = refs[:9], refs[9:18], refs[18]
    core, seq = place_ref[0], place_ref[3]
    rows = mine_ref.shape[0] // 2
    for side, near, ref in ((core, place_ref[1], mine_ref), (1 - core, place_ref[2], other_ref)):
        for k in range(2):
            piece = near if k == 0 else 1 - near
            flat[pl.ds(pl.multiple_of((2 * side + piece) * rows, 8), rows), :] = ref[k * rows : (k + 1) * rows, :]
    vocab, chans = ins[1].shape
    groups = ins[6].shape[0]
    spans = ((0, vocab), (VP - groups - 5, 5), (VP - groups, groups))
    for t, rate in enumerate((0.5, 0.3, 0.05)):
        first, count = spans[t]
        owned = owner_ref[t] == seq
        for k in range(chans // 128):
            lanes = slice(128 * k, 128 * (k + 1))
            weight = ins[3 * t][:, pl.ds(pl.multiple_of(half_ref[0] * chans + 128 * k, 128), 128)]
            grad = flat[VP * k + first : VP * k + first + count, :]
            new = adamw(weight, grad, ins[3 * t + 1][:, lanes], ins[3 * t + 2][:, lanes], rate)
            for q in range(3):
                out = outs[3 * t + q]
                value = jnp.where(owned, new[q], 0.0)
                if count == groups:
                    out[0, :, lanes] = value
                else:
                    out[:, 0, lanes] = value


def local(
    seq_size, byte_ids, lengths, lang_ids, owners, table, conv_w, score_w, cotangent,
    table_m, table_v, conv_m, conv_v, score_m, score_v,
):
    seqs, slot = byte_ids.shape
    vocab, full = table.shape
    half_rows, chans = cotangent.shape[1:]
    groups = score_w.shape[0]
    rows = slot // PLANES
    assert rows * PLANES == slot and rows <= RP - 2 and seqs % 2 == 0 and seqs <= 8
    half = lax.axis_index("blk").astype(jnp.int32).reshape(1)
    seq = lax.axis_index("seq").astype(jnp.int32)
    core, far_bit, near_bit = seq % 2, (seq // 4) % 2, (seq // 2) % 2
    near = jnp.where(core == 0, far_bit, near_bit)
    near_other = jnp.where(core == 0, near_bit, far_bit)
    vmem = pltpu.VMEM
    shape = jax.ShapeDtypeStruct
    whole = lambda *dims: pl.BlockSpec(dims, lambda s, *_: (0,) * len(dims))
    by_two = lambda *dims: pl.BlockSpec((2,) + dims, lambda s, *_: (s,) + (0,) * len(dims))
    by_seq = lambda *dims: pl.BlockSpec((1,) + dims, lambda s, *_: (s,) + (0,) * len(dims))

    def call(kernel, name, scalars, arrays, in_specs, outs, out_specs, scratch, mib, steps):
        return pl.pallas_call(
            kernel,
            grid_spec=pltpu.PrefetchScalarGridSpec(
                num_scalar_prefetch=len(scalars), grid=(steps,),
                in_specs=in_specs, out_specs=out_specs, scratch_shapes=scratch,
            ),
            out_shape=outs,
            compiler_params=pltpu.CompilerParams(
                vmem_limit_bytes=mib * 1024 * 1024, dimension_semantics=("arbitrary",)
            ),
            name=name,
        )(*scalars, *arrays)

    planes = cotangent.reshape(seqs, rows, 6, chans).transpose(0, 2, 1, 3)
    long = PLANES * RP
    padded = (rows + 7) // 8 * 8
    emb, conv, look, inner, id_rows = call(
        forward_kernel, "forward",
        [half, lengths, lang_ids], [byte_ids, planes, table, conv_w, score_w],
        [whole(seqs, slot), by_two(6, rows, chans), whole(vocab, full), whole(5, full), whole(groups, full)],
        [
            pltpu.HBM((seqs, long, chans), BF16), pltpu.HBM((seqs, PLANES, padded, chans), F32),
            shape((seqs, 8 * PLANES, 128), F32),
            shape((seqs, 32, 128), F32), shape((seqs, 8, long), F32),
        ],
        [
            pl.BlockSpec(memory_space=pltpu.HBM), pl.BlockSpec(memory_space=pltpu.HBM),
            whole(seqs, 8 * PLANES, 128), whole(seqs, 32, 128), whole(seqs, 8, long),
        ],
        [
            vmem((8, long), F32), vmem((long, 8), F32), vmem((long, 8), F32),
            vmem((128, full), F32), vmem((384, full), BF16), vmem((384, 128), BF16),
            vmem((128, chans), F32), vmem((384, chans + 128), BF16),
            vmem((chans // 128 + 1, long + 32, 128), F32), vmem((chans // 128 + 1, long + 32, 128), F32),
            vmem((long, chans), BF16), vmem((long, chans), BF16), vmem((seqs, 384, 128), BF16),
            vmem((5, chans), F32), vmem((6, RP, chans), F32), vmem((128, 128), F32), vmem((long, 384), BF16),
            vmem((PLANES, padded, chans), F32), vmem((PLANES, padded, chans), F32),
            pltpu.SemaphoreType.DMA((4,)),
        ],
        FORWARD_MIB, seqs // 2,
    )
    emb = pltpu.with_memory_space_constraint(emb, pltpu.HBM)
    other = lax.ppermute(inner, "blk", [(0, 1), (1, 0)])
    prob, coef = call(
        score_kernel, "scores",
        [lengths, lang_ids], [look, conv_w, score_w],
        [whole(seqs, 8 * PLANES, 128), whole(5, full), whole(groups, full)],
        [shape((48, 8, 128), F32), shape((seqs, 32, 128), F32)],
        [whole(48, 8, 128), whole(seqs, 32, 128)], [], 16, 1,
    )
    other, prob, coef = lax.optimization_barrier((other, prob, coef))
    total = -(-VP * (chans // 128) // 32) * 32
    keep, send = call(
        backward_kernel, "backward",
        [half, lengths, lang_ids, core.reshape(1)],
        [id_rows, planes, table, conv_w, score_w, emb, prob, coef, inner, other],
        [
            whole(seqs, 8, long), by_two(6, rows, chans), whole(vocab, full), whole(5, full), whole(groups, full),
            pl.BlockSpec(memory_space=pltpu.HBM), whole(48, 8, 128), whole(seqs, 32, 128),
            whole(seqs, 32, 128), whole(seqs, 32, 128),
        ],
        [shape((total // 2, 128), F32)] * 2,
        [whole(total // 2, 128)] * 2,
        [
            vmem((128, chans), F32), vmem((384, chans), BF16),
            vmem((seqs, 128, 128), F32), vmem((seqs, 128, 128), F32),
            vmem((chans // 128, long + 8, 128), F32), vmem((384, 128), F32), vmem((VP, chans), F32),
            vmem((5, 8, chans), F32), vmem((total, 128), F32), vmem((5, chans), F32), vmem((groups, chans), F32),
            vmem((6, RP, chans), F32),
            vmem((seqs * long, chans + 128), BF16), vmem((seqs, long, chans), BF16),
            vmem((44, RP, 128), F32), vmem((seqs, RP, 128), BF16), vmem((seqs, 8, chans), F32),
            vmem((44, 16, 128), BF16), vmem((26, 8, 128), F32), pltpu.SemaphoreType.DMA((seqs,)),
        ],
        BACKWARD_MIB, seqs // 2,
    )

    def swap(x, step, odd_step):
        return lax.ppermute(x, "seq", [(i, i ^ (odd_step if i % 2 else step)) for i in range(seq_size)])

    def pooled_two(first, before):
        held = [] if first == 0 else [before]
        return pl.pallas_call(
            functools.partial(pooled_kernel, first),
            in_specs=[pl.BlockSpec(memory_space=pltpu.HBM)] * len(held)
            + [pl.BlockSpec(memory_space=pltpu.VMEM), pl.BlockSpec(memory_space=pltpu.HBM)],
            out_specs=pl.BlockSpec(memory_space=pltpu.HBM),
            scratch_shapes=[
                vmem((2, 26, RP, 128), F32), vmem((2, chans // 128, PLANES, padded, 128), F32),
                vmem((6, padded, 128), F32), vmem((2, 6, rows, chans), BF16),
                vmem((32, 16, 128), BF16), vmem((128, 128), F32),
                pltpu.SemaphoreType.DMA((2 * (chans // 128) + 2,)),
            ],
            out_shape=pltpu.HBM((seqs, 6, rows, chans), BF16),
            input_output_aliases={0: 0} if held else {},
            compiler_params=pltpu.CompilerParams(vmem_limit_bytes=POOLED_MIB * 1024 * 1024),
            name="pooled",
        )(*held, coef, pltpu.with_memory_space_constraint(conv, pltpu.HBM))

    keep, conv = lax.optimization_barrier((keep, conv))
    mine = keep + swap(send, 1, 1)
    quarter = total // 4
    held = lax.dynamic_slice_in_dim(mine, near * quarter, quarter, 0)
    sent = lax.dynamic_slice_in_dim(mine, (1 - near) * quarter, quarter, 0)
    pooled = pooled_two(0, None)
    got, pooled = lax.optimization_barrier((swap(sent, 4, 2), pooled))
    held = held + got
    even, odd = [2, 8], [8, 4]
    step = 16
    while step < seq_size:
        even, odd, step = even + [step], odd + [step], step * 2
    for k, (step, odd_step) in enumerate(zip(even, odd)):
        got = swap(held, step, odd_step)
        if k == 0:
            for first in range(2, seqs, 2):
                pooled = pooled_two(first, pooled)
        elif k == 1:
            pooled = pooled.transpose(0, 2, 1, 3).reshape(seqs, half_rows, chans)
        if k < 2:
            got, pooled = lax.optimization_barrier((got, pooled))
        held = held + got
    mine = jnp.concatenate([held, swap(held, 4, 2)], axis=0)
    other = swap(mine, 1, 1)

    place = jnp.stack([core, near, near_other, seq])
    arrays = [mine, other, table, table_m, table_v, conv_w, conv_m, conv_v, score_w, score_m, score_v]
    outs = []
    for count in (vocab, 5):
        outs += [shape((count, 1, chans), F32)] * 3
    outs += [shape((1, groups, chans), F32)] * 3
    updated = call(
        update_kernel, "update",
        [half, place, owners], arrays, [whole(*x.shape) for x in arrays],
        outs, [whole(*x.shape) for x in outs], [vmem((total, 128), F32)], UPDATE_MIB, 1,
    )
    updated = [jnp.transpose(x, (1, 0, 2)) if k < 6 else x for k, x in enumerate(updated)]
    return (pooled, *updated)


def solution(mesh):
    row, split, copied = P("seq"), P(None, "blk"), P()
    return jax.shard_map(
        functools.partial(local, mesh.shape["seq"]),
        mesh=mesh,
        in_specs=(P("seq", None), row, row, copied, copied, copied, copied, P("seq", None, "blk"))
        + (split,) * 6,
        out_specs=(P("seq", None, "blk"),) * 10,
        check_vma=False,
    )
```

```python
import functools

import jax
import jax.numpy as jnp
from jax import lax
from jax.experimental import pallas as pl
from jax.experimental.pallas import tpu as pltpu
from jax.sharding import PartitionSpec as P

STEP_NUMBER = 5
F32, BF16 = jnp.float32, jnp.bfloat16
PLANES = 12
RP = 96
NO_ID = 511.0
VP = 272
FORWARD_MIB, POOLED_MIB, BACKWARD_MIB, UPDATE_MIB = 32, 16, 32, 16
NN = (((1,), (0,)), ((), ()))
NT = (((1,), (1,)), ((), ()))


def dot(a, b, dims=NN):
    return lax.dot_general(a, b, dims, preferred_element_type=F32)


def iota(shape, dim):
    return lax.broadcasted_iota(jnp.int32, shape, dim)


def split3(x):
    high = x.astype(BF16)
    rest = x - high.astype(F32)
    mid = rest.astype(BF16)
    return high, mid, (rest - mid.astype(F32)).astype(BF16)


def pick_row(x, index):
    return jnp.sum(jnp.where(iota(x.shape, 0) == index, x, 0.0), axis=0, keepdims=True)


def half_lanes(half_ref, chans):
    return pl.ds(pl.multiple_of(half_ref[0] * chans, 128), chans)


def load_table(table_ref, lanes, tail_ref, tab_ref, count):
    vocab = table_ref.shape[0]
    whole = vocab // 128 * 128
    tab_ref[:whole, :count] = table_ref[:whole, lanes].astype(BF16)
    tail_ref[...] = jnp.zeros(tail_ref.shape, F32)
    tail_ref[: vocab - whole, :] = table_ref[whole:, lanes]
    tab_ref[whole:, :count] = tail_ref[...].astype(BF16)


def blocks(x):
    two = [x[2 * p] + x[2 * p + 1] for p in range(6)]
    three = [two[0] + x[2], x[3] + two[2], two[3] + x[8], x[9] + two[5]]
    four = [two[0] + two[1], two[2] + two[3], two[4] + two[5]]
    return [x, two, three, four]


def live_planes(length):
    place = PLANES * iota((1, 128), 1)
    return [jnp.where(place + m < length, 1.0, 0.0).astype(F32) for m in range(PLANES)]


def inverse_counts(live):
    return [[1.0 / jnp.maximum(c, 1.0) for c in side] for side in blocks(live)]


def after_lane(x):
    return jnp.where(iota(x.shape, 1) == 127, 0.0, pltpu.roll(x, 127, 1))


def before_lane(x):
    return jnp.where(iota(x.shape, 1) == 0, 0.0, pltpu.roll(x, 1, 1))


def coefficients(weights):
    one, two, three, four = weights
    rows = [one[m] + two[m // 2 * 2] + two[m // 2 * 2 + 1] for m in range(PLANES)]
    rows += [four[2 * p] + four[2 * p + 1] for p in range(6)]
    for h in (0, 6):
        rows += [three[h] + three[h + 1], three[h + 2], three[h + 3], three[h + 4] + three[h + 5]]
    return rows


def convolved(w, e, behind, live):
    out = []
    for m in range(PLANES):
        value = w[4] + w[0] * e[m]
        for k in range(1, 4):
            value = value + w[k] * (e[m - k] if m >= k else behind[m - k + PLANES])
        out.append(jnp.where(live[m], value, 0.0))
    return out


def pair_terms(sums):
    terms = [(m, m // 2, sums[0][m]) for m in range(PLANES)]
    terms += [(12 + p, p, sums[3][p // 2]) for p in range(6)]
    for h in range(2):
        for k, (p, j) in enumerate(((0, 0), (1, 0), (1, 1), (2, 1))):
            terms.append((18 + 4 * h + k, 3 * h + p, sums[2][2 * h + j]))
    return terms


THIRD = [18, 18, 19, 20, 21, 21, 22, 22, 23, 24, 25, 25]


def forward_kernel(
    half_ref, len_ref, lang_ref, ids_ref, cot_ref, table_ref, convw_ref, score_ref,
    emb_out, conv_out, look_out, inner_out, rows_out,
    xs, cs, idcol, tail, tab_all, looks, tail_half, tab, emb_a, emb_b, low_a, low_b, extras,
    conv_half, cotf, turned, hots, conv_a, conv_b, sems,
):
    n = pl.program_id(0)
    seqs, slot = ids_ref.shape
    rows, chans = cot_ref.shape[2:]
    long = PLANES * RP
    mine = half_lanes(half_ref, chans)
    embs, lows = (emb_a, emb_b), (low_a, low_b)
    convs = (conv_a, conv_b)

    def send(q, k):
        return pltpu.make_async_copy(lows[k], emb_out.at[q], sems.at[k])

    def send_conv(q, k):
        return pltpu.make_async_copy(convs[k], conv_out.at[q], sems.at[2 + k])

    def look_up(q, u):
        emb = embs[u]
        tab[:, chans:] = extras[q]
        lane = iota((128, 128), 1).astype(F32)
        for at in range(0, long, 128):
            ids = jnp.broadcast_to(rows_out[q, 0:1, at : at + 128], (128, 128)).T
            for k in range(3):
                hots[at : at + 128, 128 * k : 128 * (k + 1)] = jnp.where(ids == lane + 128.0 * k, 1.0, 0.0).astype(BF16)
        found = dot(hots[...], tab[...])
        for c in range(chans // 128 + 1):
            emb[c, :long, :] = found[:, 128 * c : 128 * (c + 1)]
        lows[u][...] = found[:, :chans].astype(BF16)
        for m in range(PLANES):
            x = emb[chans // 128, RP * m : RP * m + 128, :24].T
            look_out[q, 8 * m : 8 * m + 8, :] = x[0:8] + x[8:16] + x[16:24]

    def convolve(q, u):
        emb = embs[u]
        length = len_ref[q]
        for p in range(6):
            cotf[p, :rows, :] = cot_ref[u, p].astype(F32)
        place = PLANES * iota((8, 128), 0)
        lane = iota((8, 128), 1)
        bits = [(lane >> k) % 2 == 1 for k in range(5)]
        for r in range(0, rows, 8):
            live = [place < length - (m + PLANES * r) for m in range(PLANES)]
            inner = [0.0] * 26
            for c in range(chans // 128):
                lanes = slice(128 * c, 128 * (c + 1))
                w = [conv_half[k : k + 1, lanes] for k in range(5)]
                e = [emb[c, RP * m + r : RP * m + r + 8, :] for m in range(PLANES)]
                behind = {m: emb[c, RP * m - 1 + r : RP * m + 7 + r, :] for m in (9, 10, 11)}
                conv = convolved(w, e, behind, live)
                for m in range(PLANES):
                    convs[u][m, r : r + 8, lanes] = conv[m]
                for k, p, x in pair_terms(blocks(conv)):
                    inner[k] = inner[k] + cotf[p, r : r + 8, lanes] * x
            level = [jnp.broadcast_to(jnp.sum(x, axis=1, keepdims=True), (8, 128)) for x in inner]
            for bit in bits:
                level.append(level[-1])
                level = [jnp.where(bit, b, a) for a, b in zip(level[0:-1:2], level[1::2])]
            turned[r : r + 8, :] = level[0]
        inner_out[q] = turned[...].T[:32]

    @pl.when(n == 0)
    def _():
        xs[...] = jnp.full(xs.shape, NO_ID, F32)
        xs[:seqs, :slot] = ids_ref[...].astype(F32)
        for i in range(xs.shape[1] // 128):
            cs[128 * i : 128 * (i + 1), :] = xs[:, 128 * i : 128 * (i + 1)].T
        idcol[...] = jnp.full(idcol.shape, NO_ID, F32)
        for m in range(PLANES):
            idcol[RP * m : RP * m + rows, :] = cs[pl.ds(m, rows, stride=PLANES), :]
        rows_out[...] = jnp.zeros(rows_out.shape, F32)
        for i in range(long // 128):
            flipped = idcol[128 * i : 128 * (i + 1), :].T
            for k in range(seqs):
                rows_out[k, 0:1, 128 * i : 128 * (i + 1)] = flipped[k : k + 1, :]
        load_table(table_ref, mine, tail_half, tab, chans)
        load_table(table_ref, slice(None), tail, tab_all, table_ref.shape[1])
        scores = score_ref[...]
        mixed = jnp.concatenate([convw_ref[k : k + 1, :] * scores for k in range(4)], axis=0)
        mixed = jnp.concatenate(list(split3(mixed)) + [jnp.zeros(mixed.shape, BF16)], axis=0)
        got = dot(tab_all[...], mixed, NT)
        got = got + pltpu.roll(got, 96, 1) + pltpu.roll(got, 64, 1)
        looks[...] = jnp.zeros(looks.shape, BF16)
        for k, part in enumerate(split3(got[:, :32])):
            looks[:, 32 * k : 32 * (k + 1)] = part
        sub, lane = iota((128, 128), 0), iota((128, 128), 1)
        for q in range(seqs):
            here = (sub % 8 == lang_ref[q]) & (lane == sub // 32 * 8 + sub % 32 // 8) & (sub < 96)
            extras[q] = dot(looks[...], jnp.where(here, 1.0, 0.0).astype(BF16)).astype(BF16)
        conv_half[...] = convw_ref[:, mine]
        turned[...] = jnp.zeros(turned.shape, F32)
        cotf[...] = jnp.zeros(cotf.shape, F32)
        for emb in embs:
            emb[:, long:, :] = jnp.zeros((emb.shape[0], emb.shape[1] - long, 128), F32)

    for u in range(2):
        q = 2 * n + u

        @pl.when(n > 0)
        def _():
            send(0, u).wait()
            send_conv(0, u).wait()

        look_up(q, u)
        convolve(q, u)
        send(q, u).start()
        send_conv(q, u).start()

    @pl.when(n == pl.num_programs(0) - 1)
    def _():
        for k in range(2):
            send(0, k).wait()
            send_conv(0, k).wait()


def score_kernel(len_ref, lang_ref, look_ref, convw_ref, score_ref, prob_out, coef_out):
    prob_out[...] = jnp.zeros(prob_out.shape, F32)
    bias = jnp.sum(convw_ref[4:5, :] * score_ref[...], axis=1, keepdims=True)
    bias = jnp.broadcast_to(bias, (score_ref.shape[0], 128))
    for q in range(look_ref.shape[0]):
        look = [look_ref[q, 8 * m : 8 * m + 8, :] for m in range(PLANES)]
        ahead = {m: before_lane(look[m]) for m in (9, 10, 11)}
        live = live_planes(len_ref[q])
        inverse = inverse_counts(live)
        base = pick_row(bias, lang_ref[q])
        score = []
        for m in range(PLANES):
            value = base
            for k in range(4):
                x = look[m - k] if m >= k else ahead[m - k + PLANES]
                value = value + x[k : k + 1, :]
            score.append(jnp.where(live[m] > 0, value, 0.0))
        means = [[t * c for t, c in zip(side, inv)] for side, inv in zip(blocks(score), inverse)]
        weights = [[], [], [], []]
        for m in range(PLANES):
            own = [means[b][m // (b + 1)] for b in range(4)]
            top = functools.reduce(jnp.maximum, own)
            grown = [jnp.exp(x - top) for x in own]
            scale = 1.0 / functools.reduce(jnp.add, grown)
            for b in range(4):
                prob = grown[b] * scale
                prob_out[PLANES * b + m, q : q + 1, :] = prob
                weights[b].append(0.5 * live[m] * prob * inverse[b][m // (b + 1)])
        coef_out[q, 24:32, :] = jnp.zeros((8, 128), F32)
        for k, row in enumerate(coefficients(weights)):
            coef_out[q, k : k + 1, :] = row


def spread_masks(keep_ref):
    lane = iota((16, 128), 1)
    for j in range(keep_ref.shape[0]):
        keep_ref[j] = jnp.where(lane % 64 == j, 1.0, 0.0).astype(BF16)


def spread_columns(both, keep_ref, cols_ref, columns):
    count = both.shape[0] // 16
    both = both.reshape(count, 16, 128)
    wide = [(both * keep_ref[j][None]).reshape(16 * count, 128) for j in columns]
    got = dot(jnp.concatenate(wide, axis=0), jnp.ones((128, 128), BF16))
    for k, j in enumerate(columns):
        cols_ref[j] = got[16 * count * k : 16 * count * (k + 1)]


def pooled_kernel(first, *refs):
    if first:
        refs = refs[1:]
    coef_ref, conv_ref, pooled_out, cols, conv, poolf, low, keep, both, sems = refs
    padded, chans = conv_ref.shape[2:]
    rows = pooled_out.shape[2]
    chunks = chans // 128
    fetches = []
    for u in range(2):
        for c in range(chunks):
            source = conv_ref.at[first + u, :, :, pl.ds(128 * c, 128)]
            fetches.append(pltpu.make_async_copy(source, conv.at[u, c], sems.at[chunks * u + c]))
            fetches[-1].start()
    sends = []
    spread_masks(keep)
    both[...] = jnp.zeros(both.shape, F32)
    for u in range(2):
        high = coef_ref[first + u].astype(BF16).astype(F32)
        both[0:32, :] = high
        both[64:96, :] = coef_ref[first + u] - high
        across = both[...].T[:RP].astype(BF16)
        for k in range(0, 26, 13):
            spread_columns(across, keep, cols.at[u], range(k, k + 13))
    for u in range(2):
        for c in range(chunks):
            fetches[chunks * u + c].wait()
            for r in range(0, padded, 8):
                pooled = [0.0] * 6
                for k, p, x in pair_terms(blocks([conv[u, c, m, r : r + 8, :] for m in range(PLANES)])):
                    pooled[p] = pooled[p] + cols[u, k, r : r + 8, :] * x
                for p in range(6):
                    poolf[p, r : r + 8, :] = pooled[p]
            for p in range(6):
                low[u, p, :, 128 * c : 128 * (c + 1)] = poolf[p, :rows, :].astype(BF16)
        sends.append(pltpu.make_async_copy(low.at[u], pooled_out.at[first + u], sems.at[2 * chunks + u]))
        sends[-1].start()
    for copy in sends:
        copy.wait()


def backward_kernel(
    half_ref, len_ref, lang_ref, core_ref, rows_ref, cot_ref, table_ref, convw_ref, score_ref,
    emb_ref, prob_ref, coef_ref, inner_ref, other_ref,
    keep_out, send_out,
    tail, tab, pulls, mixed, grad, hist, acc, taps_acc, flat, conv_half, score_half, cotf,
    gemb, low, cols, across, totals, keep, products, sems,
):
    n = pl.program_id(0)
    seqs = len_ref.shape[0]
    rows, chans = cot_ref.shape[2:]
    groups = score_ref.shape[0]
    mine = half_lanes(half_ref, chans)
    padded = (rows + 7) // 8 * 8
    long = PLANES * RP

    def fetch(q):
        return pltpu.make_async_copy(emb_ref.at[q], low.at[q], sems.at[q])

    def to_table():
        sub = iota((VP, long), 0).astype(F32)
        hot = [jnp.where(rows_ref[q, 0:1, :] == sub, 1.0, 0.0).astype(BF16) for q in range(seqs)]
        got = dot(jnp.concatenate(hot, axis=1), gemb[...])
        acc[...] = got[:, :chans]
        hist[:VP, :] = got[:, chans:]
        counts = hist[...].T
        counts = counts[: 4 * seqs] + counts[64 : 64 + 4 * seqs]
        from_table = dot(jnp.concatenate(split3(counts), axis=0), tab[...])
        from_table = from_table[: 4 * seqs] + from_table[4 * seqs : 8 * seqs] + from_table[8 * seqs :]
        group = iota((groups, chans), 0)
        total = 0.0
        for q in range(seqs):
            part = conv_half[4:5, :] * totals[q, 0:1, :]
            for j in range(4):
                part = part + conv_half[j : j + 1, :] * from_table[4 * q + j : 4 * q + j + 1, :]
            total = total + jnp.where(group == lang_ref[q], part, 0.0)
        acc[VP - groups : VP, :] += total

    def prepare():
        sub, lane = iota((8, 128), 0), iota((8, 128), 1)
        length = jnp.zeros((8, 128), jnp.int32)
        for q in range(seqs):
            both = inner_ref[q] + other_ref[q]
            for j in range(26):
                products[j, q : q + 1, :] = both[j : j + 1, :]
            length = jnp.where(sub == q, len_ref[q], length)
        live = [jnp.where(PLANES * lane + m < length, 1.0, 0.0).astype(F32) for m in range(PLANES)]
        inverse = inverse_counts(live)
        pull = [[], [], [], []]
        for m in range(PLANES):
            p = m // 2
            dots = [products[m], products[2 * p] + products[2 * p + 1], products[THIRD[m]], products[12 + p]]
            prob = [prob_ref[PLANES * b + m] for b in range(4)]
            inv = [inverse[b][m // (b + 1)] for b in range(4)]
            inner = [0.5 * jnp.where(live[m] > 0, d, 0.0) * c for d, c in zip(dots, inv)]
            mean = functools.reduce(jnp.add, [x * y for x, y in zip(prob, inner)])
            for b in range(4):
                pull[b].append(prob[b] * (inner[b] - mean) * inv[b])
        sums = [blocks(pull[b])[b] for b in range(4)]
        pull = [live[m] * (sums[0][m] + sums[1][m // 2] + sums[2][m // 3] + sums[3][m // 4]) for m in range(PLANES)]
        whole = jnp.sum(functools.reduce(jnp.add, pull), axis=1, keepdims=True)
        for m, x in enumerate(pull + [after_lane(x) for x in pull[:3]]):
            high = x.astype(BF16).astype(F32)
            low_part = x - high
            for q in range(seqs):
                pulls[q, m : m + 1, :] = high[q : q + 1, :]
                pulls[q, 64 + m : 65 + m, :] = low_part[q : q + 1, :]
                if m < PLANES:
                    mixed[q, 32 + m : 33 + m, :] = high[q : q + 1, :]
                    mixed[q, 96 + m : 97 + m, :] = low_part[q : q + 1, :]
        lane = iota((RP, 128), 1)
        for q in range(seqs):
            totals[q] = jnp.broadcast_to(whole[q : q + 1, :], totals.shape[1:])
            high = coef_ref[q].astype(BF16).astype(F32)
            mixed[q, 0:32, :] = high
            mixed[q, 64:96, :] = coef_ref[q] - high
            turned = pulls[q].T
            for m in range(PLANES):
                x = turned if (4 * q - m) % 128 == 0 else pltpu.roll(turned, (4 * q - m) % 128, 1)
                x = jnp.where(lane % 64 // 4 == q, x[:RP], 0.0)
                gemb[long * q + RP * m : long * q + RP * (m + 1), chans:] = x.astype(BF16)
            across[q] = mixed[q].T[:RP].astype(BF16)

    def gradients(q, u):
        length = len_ref[q]
        score = pick_row(score_half[...], lang_ref[q])
        for p in range(6):
            cotf[p, :rows, :] = cot_ref[u, p].astype(F32)
        columns = [*range(26), *range(32, 44)]
        for r in range(0, rows, 8):
            if r % 16 == 0:
                spread_columns(across[q, r : r + 16, :], keep, cols.at[:, r : r + 16, :], columns)
            for c in range(chans // 128):
                lanes = slice(128 * c, 128 * (c + 1))
                cot = [cotf[p, r : r + 8, lanes] for p in range(6)]
                times = lambda j, p: cols[j, r : r + 8, :] * cot[p]
                four = [times(12 + 2 * j, 2 * j) + times(13 + 2 * j, 2 * j + 1) for j in range(3)]
                three = []
                for h in range(2):
                    three.append(times(18 + 4 * h, 3 * h) + times(19 + 4 * h, 3 * h + 1))
                    three.append(times(20 + 4 * h, 3 * h + 1) + times(21 + 4 * h, 3 * h + 2))
                for m in range(PLANES):
                    value = times(m, m // 2) + four[m // 4] + three[m // 3]
                    value = value + cols[32 + m, r : r + 8, :] * score[:, lanes]
                    grad[c, RP * m + r : RP * m + r + 8, :] = value
        end = length // PLANES
        for m in range(PLANES):
            for c in range(chans // 128):
                at = pl.ds(RP * m + end, 1)
                grad[c, at, :] = jnp.where(PLANES * end + m < length, grad[c, at, :], 0.0)

    def weight_gradients(q, u):
        base = pl.multiple_of(q * long, 128)
        for c in range(chans // 128):
            lanes = slice(128 * c, 128 * (c + 1))
            w = [conv_half[k : k + 1, lanes] for k in range(4)]
            tap = [0.0] * 5
            for r in range(0, padded, 16):
                count = min(16, padded - r)
                g = [grad[c, RP * m + r : RP * m + r + count, :] for m in range(PLANES)]
                g += [grad[c, RP * m + r + 1 : RP * m + r + 1 + count, :] for m in range(3)]
                fold = lambda x: x[:8] + x[8:] if count == 16 else x
                for m in range(PLANES):
                    back = w[0] * g[m] + w[1] * g[m + 1] + w[2] * g[m + 2] + w[3] * g[m + 3]
                    if count < 16:
                        back = jnp.concatenate([back, jnp.zeros((16 - count, 128), F32)], axis=0)
                    gemb[pl.ds(base + RP * m + r, 16), lanes] = back.astype(BF16)
                    e = low[q, RP * m + r : RP * m + r + 16, lanes].astype(F32)[:count]
                    for k in range(4):
                        tap[k] = tap[k] + fold(e * g[m + k])
                    tap[4] = tap[4] + fold(g[m])
            for k in range(5):
                taps_acc[k, :, lanes] += tap[k]

    @pl.when(n == 0)
    def _():
        for q in range(seqs):
            fetch(q).start()
        load_table(table_ref, mine, tail, tab, chans)
        cotf[...] = jnp.zeros(cotf.shape, F32)
        pulls[...] = jnp.zeros(pulls.shape, F32)
        mixed[...] = jnp.zeros(mixed.shape, F32)
        for m in range(PLANES):
            grad[:, RP * m + rows : RP * (m + 1), :] = jnp.zeros((chans // 128, RP - rows, 128), F32)
        grad[:, PLANES * RP :, :] = jnp.zeros((chans // 128, 8, 128), F32)
        taps_acc[...] = jnp.zeros(taps_acc.shape, F32)
        hist[...] = jnp.zeros(hist.shape, F32)
        conv_half[...] = convw_ref[:, mine]
        score_half[...] = score_ref[:, mine]
        spread_masks(keep)
        products[...] = jnp.zeros(products.shape, F32)
        prepare()

    for u in range(2):
        q = 2 * n + u
        gradients(q, u)
        fetch(q).wait()

        @pl.when(len_ref[q] > 0)
        def _():
            weight_gradients(q, u)

    @pl.when(n == pl.num_programs(0) - 1)
    def _():
        to_table()
        for k in range(5):
            at = VP - groups - 5 + k
            acc[at : at + 1, :] = jnp.sum(taps_acc[k], axis=0, keepdims=True)
        flat[VP * (chans // 128) :, :] = jnp.zeros((flat.shape[0] - VP * (chans // 128), 128), F32)
        for k in range(chans // 128):
            flat[VP * k : VP * (k + 1), :] = acc[:, 128 * k : 128 * (k + 1)]
        part = keep_out.shape[0]
        own = pl.multiple_of(core_ref[0] * part, 8)
        theirs = pl.multiple_of((1 - core_ref[0]) * part, 8)
        keep_out[...] = flat[pl.ds(own, part), :]
        send_out[...] = flat[pl.ds(theirs, part), :]


def adamw(weight, grad, moment, second, rate):
    new_m = 0.9 * moment + 0.1 * grad
    new_v = 0.999 * second + 0.001 * grad * grad
    m_hat = new_m / (1.0 - 0.9**STEP_NUMBER)
    v_hat = new_v / (1.0 - 0.999**STEP_NUMBER)
    new_w = weight - rate * (m_hat / (jnp.sqrt(v_hat) + 1e-08) + 0.01 * weight)
    return new_m, new_v, new_w


def update_kernel(half_ref, place_ref, owner_ref, mine_ref, other_ref, *refs):
    ins, outs, flat = refs[:9], refs[9:18], refs[18]
    core, seq = place_ref[0], place_ref[3]
    rows = mine_ref.shape[0] // 2
    for side, near, ref in ((core, place_ref[1], mine_ref), (1 - core, place_ref[2], other_ref)):
        for k in range(2):
            piece = near if k == 0 else 1 - near
            flat[pl.ds(pl.multiple_of((2 * side + piece) * rows, 8), rows), :] = ref[k * rows : (k + 1) * rows, :]
    vocab, chans = ins[1].shape
    groups = ins[6].shape[0]
    spans = ((0, vocab), (VP - groups - 5, 5), (VP - groups, groups))
    for t, rate in enumerate((0.5, 0.3, 0.05)):
        first, count = spans[t]
        owned = owner_ref[t] == seq
        for k in range(chans // 128):
            lanes = slice(128 * k, 128 * (k + 1))
            weight = ins[3 * t][:, pl.ds(pl.multiple_of(half_ref[0] * chans + 128 * k, 128), 128)]
            grad = flat[VP * k + first : VP * k + first + count, :]
            new = adamw(weight, grad, ins[3 * t + 1][:, lanes], ins[3 * t + 2][:, lanes], rate)
            for q in range(3):
                out = outs[3 * t + q]
                value = jnp.where(owned, new[q], 0.0)
                if count == groups:
                    out[0, :, lanes] = value
                else:
                    out[:, 0, lanes] = value


def local(
    seq_size, byte_ids, lengths, lang_ids, owners, table, conv_w, score_w, cotangent,
    table_m, table_v, conv_m, conv_v, score_m, score_v,
):
    seqs, slot = byte_ids.shape
    vocab, full = table.shape
    half_rows, chans = cotangent.shape[1:]
    groups = score_w.shape[0]
    rows = slot // PLANES
    assert rows * PLANES == slot and rows <= RP - 2 and seqs % 2 == 0 and seqs <= 8
    half = lax.axis_index("blk").astype(jnp.int32).reshape(1)
    seq = lax.axis_index("seq").astype(jnp.int32)
    core, far_bit, near_bit = seq % 2, (seq // 4) % 2, (seq // 2) % 2
    near = jnp.where(core == 0, far_bit, near_bit)
    near_other = jnp.where(core == 0, near_bit, far_bit)
    vmem = pltpu.VMEM
    shape = jax.ShapeDtypeStruct
    whole = lambda *dims: pl.BlockSpec(dims, lambda s, *_: (0,) * len(dims))
    by_two = lambda *dims: pl.BlockSpec((2,) + dims, lambda s, *_: (s,) + (0,) * len(dims))
    by_seq = lambda *dims: pl.BlockSpec((1,) + dims, lambda s, *_: (s,) + (0,) * len(dims))

    def call(kernel, name, scalars, arrays, in_specs, outs, out_specs, scratch, mib, steps):
        return pl.pallas_call(
            kernel,
            grid_spec=pltpu.PrefetchScalarGridSpec(
                num_scalar_prefetch=len(scalars), grid=(steps,),
                in_specs=in_specs, out_specs=out_specs, scratch_shapes=scratch,
            ),
            out_shape=outs,
            compiler_params=pltpu.CompilerParams(
                vmem_limit_bytes=mib * 1024 * 1024, dimension_semantics=("arbitrary",)
            ),
            name=name,
        )(*scalars, *arrays)

    planes = cotangent.reshape(seqs, rows, 6, chans).transpose(0, 2, 1, 3)
    long = PLANES * RP
    padded = (rows + 7) // 8 * 8
    emb, conv, look, inner, id_rows = call(
        forward_kernel, "forward",
        [half, lengths, lang_ids], [byte_ids, planes, table, conv_w, score_w],
        [whole(seqs, slot), by_two(6, rows, chans), whole(vocab, full), whole(5, full), whole(groups, full)],
        [
            pltpu.HBM((seqs, long, chans), BF16), pltpu.HBM((seqs, PLANES, padded, chans), F32),
            shape((seqs, 8 * PLANES, 128), F32),
            shape((seqs, 32, 128), F32), shape((seqs, 8, long), F32),
        ],
        [
            pl.BlockSpec(memory_space=pltpu.HBM), pl.BlockSpec(memory_space=pltpu.HBM),
            whole(seqs, 8 * PLANES, 128), whole(seqs, 32, 128), whole(seqs, 8, long),
        ],
        [
            vmem((8, long), F32), vmem((long, 8), F32), vmem((long, 8), F32),
            vmem((128, full), F32), vmem((384, full), BF16), vmem((384, 128), BF16),
            vmem((128, chans), F32), vmem((384, chans + 128), BF16),
            vmem((chans // 128 + 1, long + 32, 128), F32), vmem((chans // 128 + 1, long + 32, 128), F32),
            vmem((long, chans), BF16), vmem((long, chans), BF16), vmem((seqs, 384, 128), BF16),
            vmem((5, chans), F32), vmem((6, RP, chans), F32), vmem((128, 128), F32), vmem((long, 384), BF16),
            vmem((PLANES, padded, chans), F32), vmem((PLANES, padded, chans), F32),
            pltpu.SemaphoreType.DMA((4,)),
        ],
        FORWARD_MIB, seqs // 2,
    )
    emb = pltpu.with_memory_space_constraint(emb, pltpu.HBM)
    other = lax.ppermute(inner, "blk", [(0, 1), (1, 0)])
    prob, coef = call(
        score_kernel, "scores",
        [lengths, lang_ids], [look, conv_w, score_w],
        [whole(seqs, 8 * PLANES, 128), whole(5, full), whole(groups, full)],
        [shape((48, 8, 128), F32), shape((seqs, 32, 128), F32)],
        [whole(48, 8, 128), whole(seqs, 32, 128)], [], 16, 1,
    )
    other, prob, coef = lax.optimization_barrier((other, prob, coef))
    total = -(-VP * (chans // 128) // 32) * 32
    keep, send = call(
        backward_kernel, "backward",
        [half, lengths, lang_ids, core.reshape(1)],
        [id_rows, planes, table, conv_w, score_w, emb, prob, coef, inner, other],
        [
            whole(seqs, 8, long), by_two(6, rows, chans), whole(vocab, full), whole(5, full), whole(groups, full),
            pl.BlockSpec(memory_space=pltpu.HBM), whole(48, 8, 128), whole(seqs, 32, 128),
            whole(seqs, 32, 128), whole(seqs, 32, 128),
        ],
        [shape((total // 2, 128), F32)] * 2,
        [whole(total // 2, 128)] * 2,
        [
            vmem((128, chans), F32), vmem((384, chans), BF16),
            vmem((seqs, 128, 128), F32), vmem((seqs, 128, 128), F32),
            vmem((chans // 128, long + 8, 128), F32), vmem((384, 128), F32), vmem((VP, chans), F32),
            vmem((5, 8, chans), F32), vmem((total, 128), F32), vmem((5, chans), F32), vmem((groups, chans), F32),
            vmem((6, RP, chans), F32),
            vmem((seqs * long, chans + 128), BF16), vmem((seqs, long, chans), BF16),
            vmem((44, RP, 128), F32), vmem((seqs, RP, 128), BF16), vmem((seqs, 8, chans), F32),
            vmem((44, 16, 128), BF16), vmem((26, 8, 128), F32), pltpu.SemaphoreType.DMA((seqs,)),
        ],
        BACKWARD_MIB, seqs // 2,
    )

    def swap(x, step, odd_step):
        return lax.ppermute(x, "seq", [(i, i ^ (odd_step if i % 2 else step)) for i in range(seq_size)])

    def pooled_two(first, before):
        held = [] if first == 0 else [before]
        return pl.pallas_call(
            functools.partial(pooled_kernel, first),
            in_specs=[pl.BlockSpec(memory_space=pltpu.HBM)] * len(held)
            + [pl.BlockSpec(memory_space=pltpu.VMEM), pl.BlockSpec(memory_space=pltpu.HBM)],
            out_specs=pl.BlockSpec(memory_space=pltpu.HBM),
            scratch_shapes=[
                vmem((2, 26, RP, 128), F32), vmem((2, chans // 128, PLANES, padded, 128), F32),
                vmem((6, padded, 128), F32), vmem((2, 6, rows, chans), BF16),
                vmem((32, 16, 128), BF16), vmem((128, 128), F32),
                pltpu.SemaphoreType.DMA((2 * (chans // 128) + 2,)),
            ],
            out_shape=pltpu.HBM((seqs, 6, rows, chans), BF16),
            input_output_aliases={0: 0} if held else {},
            compiler_params=pltpu.CompilerParams(vmem_limit_bytes=POOLED_MIB * 1024 * 1024),
            name="pooled",
        )(*held, coef, pltpu.with_memory_space_constraint(conv, pltpu.HBM))

    keep, conv = lax.optimization_barrier((keep, conv))
    mine = keep + swap(send, 1, 1)
    quarter = total // 4
    held = lax.dynamic_slice_in_dim(mine, near * quarter, quarter, 0)
    sent = lax.dynamic_slice_in_dim(mine, (1 - near) * quarter, quarter, 0)
    pooled = pooled_two(0, None)
    got, pooled = lax.optimization_barrier((swap(sent, 4, 2), pooled))
    held = held + got
    even, odd = [2, 8], [8, 4]
    step = 16
    while step < seq_size:
        even, odd, step = even + [step], odd + [step], step * 2
    for k, (step, odd_step) in enumerate(zip(even, odd)):
        got = swap(held, step, odd_step)
        if k == 0:
            for first in range(2, seqs, 2):
                pooled = pooled_two(first, pooled)
        elif k == 1:
            pooled = pooled.transpose(0, 2, 1, 3).reshape(seqs, half_rows, chans)
        if k < 2:
            got, pooled = lax.optimization_barrier((got, pooled))
        held = held + got
    mine = jnp.concatenate([held, swap(held, 4, 2)], axis=0)
    other = swap(mine, 1, 1)

    place = jnp.stack([core, near, near_other, seq])
    arrays = [mine, other, table, table_m, table_v, conv_w, conv_m, conv_v, score_w, score_m, score_v]
    outs = []
    for count in (vocab, 5):
        outs += [shape((count, 1, chans), F32)] * 3
    outs += [shape((1, groups, chans), F32)] * 3
    updated = call(
        update_kernel, "update",
        [half, place, owners], arrays, [whole(*x.shape) for x in arrays],
        outs, [whole(*x.shape) for x in outs], [vmem((total, 128), F32)], UPDATE_MIB, 1,
    )
    updated = [jnp.transpose(x, (1, 0, 2)) if k < 6 else x for k, x in enumerate(updated)]
    return (pooled, *updated)


def solution(mesh):
    row, split, copied = P("seq"), P(None, "blk"), P()
    return jax.shard_map(
        functools.partial(local, mesh.shape["seq"]),
        mesh=mesh,
        in_specs=(P("seq", None), row, row, copied, copied, copied, copied, P("seq", None, "blk"))
        + (split,) * 6,
        out_specs=(P("seq", None, "blk"),) * 10,
        check_vma=False,
    )
```
